32 devices in a mesh: dp: 16 (over z, y, x), mp: 2 (over core).
Axes of the slice: x: 2, y: 2, z: 4, core: 2. Of those that a mesh axis runs over, the one named last changes fastest.
Arguments:
- tokens: bfloat16 [8192, 768], P('dp'), may hold values from -6 to 6
- out_grad: bfloat16 [8192, 128], P('dp', 'mp'), may hold values from -6 to 6
- doc_lengths: int32 [16], P('dp'), may hold values from 40 to 512, as said below
- owner_list: int32 [96], replicated, may hold values from 0 to 15, as said below
- bucket_table: int32 [1023], replicated, may hold values from 0 to 31
- unit_weight: float32 [208, 128, 768], P('dp', None, 'mp'), as said below
- unit_first: float32 [208, 128, 768], P('dp', None, 'mp'), as said below
- unit_second: float32 [208, 128, 768], P('dp', None, 'mp'), as said below
- gain_weight: float32 [3, 768], replicated, may hold values from 0.5 to 1.5
- gain_first: float32 [3, 768], replicated, may hold values from -192 to 192
- gain_second: float32 [3, 768], replicated, may hold values from 1170 to 4681
- bias_weight: float32 [32, 12], P(None, 'mp'), may hold values from -3 to 3
- bias_first: float32 [32, 12], P(None, 'mp'), may hold values from -192 to 192
- bias_second: float32 [32, 12], P(None, 'mp'), may hold values from 910 to 3640
- proj_weight: float32 [768, 128], P(None, 'mp'), may hold values from -0.21875 to 0.21875
- proj_first: float32 [768, 128], P(None, 'mp'), may hold values from -448 to 448
- proj_second: float32 [768, 128], P(None, 'mp'), may hold values from 5734 to 22937
Outputs:
- encoded: float32 [8192, 128], P('dp', 'mp')
- token_grad: float32 [8192, 768], P('dp')
- unit_weights: float32 [208, 128, 768], P('dp', None, 'mp')
- unit_firsts: float32 [208, 128, 768], P('dp', None, 'mp')
- unit_seconds: float32 [208, 128, 768], P('dp', None, 'mp')
- unit_copies: bfloat16 [208, 128, 768], P('dp', None, 'mp')
- gain_weights: float32 [3, 768], replicated
- gain_firsts: float32 [3, 768], replicated
- gain_seconds: float32 [3, 768], replicated
- bias_weights: float32 [32, 12], P(None, 'mp')
- bias_firsts: float32 [32, 12], P(None, 'mp')
- bias_seconds: float32 [32, 12], P(None, 'mp')
- proj_weights: float32 [768, 128], P(None, 'mp')
- proj_firsts: float32 [768, 128], P(None, 'mp')
- proj_seconds: float32 [768, 128], P(None, 'mp')
The draws below stay inside these ranges and needn't reach their ends.
Inputs may be any that keep to these rules, and one draw needn't show every extreme that they name: A document's tokens fill the first doc_lengths places of its slot of 512; some document has exactly 512 in every draw. `owner_list`: no dp index owns more than 13 units, and one owns exactly 13 in every draw. `unit_weight`: slot d * 13 + j holds the j-th unit, in unit order, of those that owner_list gives to dp index d; other slots hold values that take part in the update only. `unit_first`: laid out in slots as unit_weight. `unit_second`: laid out in slots as unit_weight; positive.
All inputs are finite; a program needn't handle non-finite values.
Results may differ from the reference program's by a relative error of at most 0.015.
The reference program's roundings to bfloat16 on the way count: a program that leaves them out, or rounds other values in their place, can miss the bound.
Values may be sent and summed in bfloat16 or wider, within the bound.
No kernel may reach another device: no remote copies, remote signals or barrier semaphores. Data moves between devices by JAX's collectives and lax.ppermute only.
A program may use at most 448 MiB of HBM per device.

```python
import math
import jax
import jax.numpy as jnp
from jax import lax

D = 768
HEADS = 12
HEAD_DIM = 64
FF = 3072
PROJ = 128
BUCKETS = 32
SLOT = 512
MIN_LEN = 40
UROWS = 128
STEP = 5
DOCS_DEV = 1
DOCS = 16
NU = 96
OWN_MOST = 13
N_DP = 16
N_MP = 2


def owner_draw(key):
    unit_key, device_key = jax.random.split(jax.random.fold_in(key, 11))
    shuffled = jax.random.permutation(unit_key, NU)
    devices = jax.random.permutation(device_key, N_DP)
    indices = jnp.arange(NU, dtype=jnp.int32)
    others = 1 + (indices - OWN_MOST) % (N_DP - 1)
    chosen = jnp.where(indices < OWN_MOST, 0, others)
    placed = jnp.take(devices, chosen).astype(jnp.int32)
    return jnp.zeros((NU,), jnp.int32).at[shuffled].set(placed)


def draw_owner_list(key, part):
    return owner_draw(key)


def draw_doc_lengths(key, part):
    reach = SLOT - MIN_LEN
    pick_key, full_key = jax.random.split(jax.random.fold_in(key, 31))
    picked = jax.random.randint(pick_key, (DOCS,), 0, reach + 1)
    lengths = SLOT - picked * picked // reach
    full_doc = jax.random.randint(full_key, (), 0, DOCS)
    return jnp.where(jnp.arange(DOCS) == full_doc, SLOT, lengths).astype(jnp.int32)


def slot_kinds(key):
    owners = owner_draw(key)
    indices = jnp.arange(NU, dtype=jnp.int32)
    earlier = (owners[:, None] == owners[None, :]) & (indices[None, :] < indices[:, None])
    slot_of = owners * OWN_MOST + jnp.sum(earlier.astype(jnp.int32), axis=1)
    slot_ids = jnp.arange(N_DP * OWN_MOST, dtype=jnp.int32)
    matches = slot_of[None, :] == slot_ids[:, None]
    unit_of = jnp.sum(jnp.where(matches, indices[None, :], 0), axis=1)
    row_count = D // UROWS
    stride = row_count * (FF // D)
    kind_ids = jnp.zeros_like(unit_of)
    for boundary in (row_count, 2 * row_count, 3 * row_count, 4 * row_count, 4 * row_count + stride, 4 * row_count + 2 * stride):
        kind_ids = kind_ids + (unit_of >= boundary).astype(jnp.int32)
    return kind_ids


def kind_scale(kind_ids, scale_table):
    return jnp.take(jnp.array(scale_table, jnp.float32), kind_ids)[:, None, None]


def grad_table():
    tokens_real = math.sqrt(0.7 * DOCS * SLOT)
    return [tokens_real * factor for factor in (1.0, 1.0, 0.28, 0.055, 0.085, 0.09, 0.18)]


def draw_unit_weight(key, part):
    inverse_root = 1.0 / math.sqrt(D)
    scale_table = [0.45 * inverse_root, 0.45 * inverse_root, inverse_root, 5.0 * inverse_root, inverse_root, inverse_root, 1.0 / math.sqrt(FF)]
    normal_noise = jax.random.truncated_normal(jax.random.fold_in(key, 21), -4.0, 4.0, (N_DP * OWN_MOST, UROWS, D), jnp.float32)
    return normal_noise * kind_scale(slot_kinds(key), scale_table)


def draw_unit_first(key, part):
    normal_noise = jax.random.truncated_normal(jax.random.fold_in(key, 22), -4.0, 4.0, (N_DP * OWN_MOST, UROWS, D), jnp.float32)
    return normal_noise * kind_scale(slot_kinds(key), grad_table())


def draw_unit_second(key, part):
    spread = jax.random.uniform(jax.random.fold_in(key, 23), (N_DP * OWN_MOST, UROWS, D), jnp.float32, math.log(0.5), math.log(2.0))
    squares = [amount * amount for amount in grad_table()]
    return 2.0 * jnp.exp(spread) * kind_scale(slot_kinds(key), squares)


def with_ends(values, key, smallest, high):
    index_at = [jax.random.randint(jax.random.fold_in(key, axis), (), 0, length) for axis, length in enumerate(values.shape)]
    widest = values.shape.index(max(values.shape))
    neighbour = index_at[:widest] + [(index_at[widest] + 1) % values.shape[widest]] + index_at[widest + 1:]
    return values.at[tuple(index_at)].set(smallest).at[tuple(neighbour)].set(high)


def block_scale(stream_key, extent, cuts, smallest, high):
    def one(position, shards_of):
        steps = jax.random.uniform(jax.random.fold_in(jax.random.fold_in(stream_key, 6), position), (shards_of,), jnp.float32, smallest / len(cuts), high / len(cuts))
        return jnp.repeat(jnp.exp(steps), extent[position] // shards_of).reshape((-1,) + (1,) * (len(extent) - position - 1))

    factor_of = one(*cuts[0])
    for cut in cuts[1:]:
        factor_of = factor_of * one(*cut)
    return factor_of


def scatter_about(stream_key, extent, width, most, cuts=(), kind=jnp.bfloat16):
    entries = width * jax.random.normal(stream_key, extent, jnp.float32)
    if cuts:
        entries = entries * block_scale(stream_key, extent, cuts, -0.22, 0.18)
    return jnp.clip(entries, -most, most).astype(kind)


def setup_inputs(seed: int = 0) -> dict:
    key_list = jax.random.split(jax.random.key(seed), 18)
    tokens = scatter_about(key_list[0], (DOCS * SLOT, D), 1.0, 6.0, ((0, 16),))
    out_grad = scatter_about(key_list[1], (DOCS * SLOT, PROJ), 1.0, 6.0, ((0, 16), (1, 2)))
    doc_lengths = draw_doc_lengths(jax.random.fold_in(key_list[17], 71), 0)
    owner_list = draw_owner_list(jax.random.fold_in(key_list[17], 71), 0)
    bucket_table = with_ends(jax.random.randint(key_list[4], (2 * SLOT - 1,), 0, BUCKETS), jax.random.fold_in(key_list[4], 1), 0, BUCKETS - 1).astype(jnp.int32)
    unit_weight = draw_unit_weight(jax.random.fold_in(key_list[17], 71), 0)
    unit_first = draw_unit_first(jax.random.fold_in(key_list[17], 71), 0)
    unit_second = draw_unit_second(jax.random.fold_in(key_list[17], 71), 0)
    gain_weight = jnp.clip(1.0 + 0.1 * jax.random.normal(key_list[8], (3, D), jnp.float32), 0.5, 1.5)
    gain_first = scatter_about(key_list[9], (3, D), ((DOCS * SLOT // 7) ** 0.5), 192.0, (), jnp.float32)
    gain_second = jnp.clip(jnp.exp(jax.random.uniform(key_list[10], (3, D), jnp.float32, math.log(1170.0), math.log(4681.0))), 1170.0, 4681.0)
    bias_weight = scatter_about(key_list[11], (BUCKETS, HEADS), 0.5, 3.0, ((1, 2),), jnp.float32)
    bias_first = scatter_about(key_list[12], (BUCKETS, HEADS), ((DOCS * SLOT // 9) ** 0.5), 192.0, ((1, 2),), jnp.float32)
    bias_second = jnp.clip(jnp.exp(math.log(3640.0) - 1.3862944 * jax.random.uniform(key_list[13], (BUCKETS, HEADS), jnp.float32) ** block_scale(key_list[13], (BUCKETS, HEADS), ((1, 2),), -0.2, 0.2)), 910.0, 3640.0)
    proj_weight = scatter_about(key_list[14], (D, PROJ), D ** -0.5, 0.21875, ((1, 2),), jnp.float32)
    proj_first = scatter_about(key_list[15], (D, PROJ), ((7 * DOCS * SLOT // 10) ** 0.5), 448.0, ((1, 2),), jnp.float32)
    proj_second = jnp.clip(jnp.exp(math.log(22937.0) - 1.386338 * jax.random.uniform(key_list[16], (D, PROJ), jnp.float32) ** block_scale(key_list[16], (D, PROJ), ((1, 2),), -0.2, 0.2)), 5734.0, 22937.0)
    return {"tokens": tokens, "out_grad": out_grad, "doc_lengths": doc_lengths, "owner_list": owner_list, "bucket_table": bucket_table, "unit_weight": unit_weight, "unit_first": unit_first, "unit_second": unit_second, "gain_weight": gain_weight, "gain_first": gain_first, "gain_second": gain_second, "bias_weight": bias_weight, "bias_first": bias_first, "bias_second": bias_second, "proj_weight": proj_weight, "proj_first": proj_first, "proj_second": proj_second}


@jax.custom_vjp
def low(v):
    return lax.optimization_barrier(v.astype(jnp.bfloat16)).astype(jnp.float32)

@jax.custom_vjp
def low_back(v):
    return v

def low_keep(v):
    return (low(v), None)

def low_pass(kept, grad):
    return (grad,)

def back_keep(v):
    return (v, None)

def back_low(kept, grad):
    return (low(grad),)
low.defvjp(low_keep, low_pass)
low_back.defvjp(back_keep, back_low)
NORM_EPS = 1e-06
ADAM_EPS = 1e-08
BETA_ONE = 0.5
BETA_TWO = 0.5
DECAY = 0.01
RATE_MATRIX = 0.02
RATE_SMALL = 0.1
RATE_GAIN = 0.6
GELU_C = 0.7978845608
GELU_K = 0.044715
HIGHEST = lax.Precision.HIGHEST

def matmul(left_side, right_side):
    return jnp.dot(left_side, right_side, precision=HIGHEST, preferred_element_type=jnp.float32)

def rms_norm(values, gain_row):
    return values * lax.rsqrt(lax.optimization_barrier(jnp.mean(values * values, axis=-1, keepdims=True)) + NORM_EPS) * gain_row

def gelu_tanh(values):
    return 0.5 * values * (1.0 + jnp.tanh(GELU_C * (values + GELU_K * values * values * values)))

def slot_table(owner_list):
    indices = jnp.arange(owner_list.shape[0], dtype=jnp.int32)
    earlier = (owner_list[:, None] == owner_list[None, :]) & (indices[None, :] < indices[:, None])
    return owner_list * OWN_MOST + lax.optimization_barrier(jnp.sum(earlier.astype(jnp.int32), axis=1))

def assemble(unit_stack):
    row_count = D // UROWS
    blocks = FF // D
    half_width = D // N_MP

    def square(first_unit):
        return unit_stack[first_unit:first_unit + row_count].reshape(D, D)

    def wide_matrix(first_unit):
        pieces = unit_stack[first_unit:first_unit + row_count * blocks].reshape(row_count, blocks, UROWS, N_MP, half_width)
        return pieces.transpose(0, 2, 3, 1, 4).reshape(D, FF)
    offset = 4 * row_count
    stride = row_count * blocks
    return (square(0), square(row_count), square(2 * row_count), square(3 * row_count), wide_matrix(offset), wide_matrix(offset + stride), wide_matrix(offset + 2 * stride))

def position_bias(bias_weight, bucket_table):
    places = jnp.arange(SLOT, dtype=jnp.int32)
    relative = places[None, :] - places[:, None] + SLOT - 1
    buckets = jnp.take(bucket_table, relative, axis=0)
    return jnp.transpose(jnp.take(bias_weight, buckets, axis=0), (2, 0, 1))

def attention(queries, key_proj, value_proj, score_bias, valid_keys):
    scores = jnp.einsum('gqhd,gkhd->ghqk', queries, key_proj, precision=HIGHEST)
    scores = low_back(scores + score_bias[None])
    scores = jnp.where(valid_keys[:, None, None, :], scores, -1000000000.0)
    probabilities = jax.nn.softmax(scores, axis=-1)
    weights = low(probabilities)
    return jnp.einsum('ghqk,gkhd->gqhd', weights, value_proj, precision=HIGHEST)

def forward(inputs, unit_stack, gain_rows, bias_weight, proj_weight, bucket_table, valid_keys):
    query_weight, key_weight, value_weight, out_weight, gate_weight, up_weight, down_weight = assemble(low(unit_stack))
    doc_count = valid_keys.shape[0]
    first_in = low(rms_norm(inputs, gain_rows[0]))

    def project(weight_matrix):
        return low(low_back(matmul(first_in, weight_matrix))).reshape(doc_count, SLOT, HEADS, HEAD_DIM)
    score_bias = position_bias(bias_weight, bucket_table)
    mixed_heads = attention(project(query_weight), project(key_weight), project(value_weight), score_bias, valid_keys)
    mixed_heads = low(low_back(mixed_heads.reshape(doc_count * SLOT, D)))
    attn_out = low_back(matmul(mixed_heads, out_weight.T))
    residual_one = inputs + attn_out
    second_in = low(rms_norm(residual_one, gain_rows[1]))
    gate_value = low_back(matmul(second_in, gate_weight))
    upward = low_back(matmul(second_in, up_weight))
    hidden = low(gelu_tanh(gate_value) * upward)
    feed_out = low_back(matmul(hidden, down_weight.T))
    residual_two = residual_one + feed_out
    third_in = low(rms_norm(residual_two, gain_rows[2]))
    return matmul(third_in, low(proj_weight))

def adamw_step(weight_now, first_now, second_now, grad_in, rate):
    first_new = BETA_ONE * first_now + (1.0 - BETA_ONE) * grad_in
    second_new = BETA_TWO * second_now + (1.0 - BETA_TWO) * grad_in * grad_in
    first_hat = first_new / (1.0 - BETA_ONE ** STEP)
    second_hat = second_new / (1.0 - BETA_TWO ** STEP)
    weight_new = weight_now - rate * (first_hat / (jnp.sqrt(second_hat) + ADAM_EPS) + DECAY * weight_now)
    return (weight_new, first_new, second_new)

def reference(tokens, out_grad, doc_lengths, owner_list, bucket_table, unit_weight, unit_first, unit_second, gain_weight, gain_first, gain_second, bias_weight, bias_first, bias_second, proj_weight, proj_first, proj_second):
    slot_of = slot_table(owner_list)
    unit_stack, pull_units = jax.vjp(lambda slots: jnp.take(slots, slot_of, axis=0), unit_weight)
    groups = DOCS // DOCS_DEV
    inputs = tokens.astype(jnp.float32).reshape(groups, DOCS_DEV * SLOT, D)
    cotangent = out_grad.astype(jnp.float32).reshape(groups, DOCS_DEV * SLOT, PROJ)
    lengths = doc_lengths.reshape(groups, DOCS_DEV)
    places = jnp.arange(SLOT, dtype=jnp.int32)

    def group_step(totals, doc_item):
        group_in, group_cot, group_len = doc_item
        valid_keys = places[None, :] < group_len[:, None]
        rowmask = valid_keys.reshape(-1).astype(jnp.float32)

        def local_pass(inputs_in, units_in, gains_in, bias_in, proj_in):
            return forward(inputs_in, units_in, gains_in, bias_in, proj_in, bucket_table, valid_keys)
        encoded, pull_back = jax.vjp(local_pass, group_in, unit_stack, gain_weight, bias_weight, proj_weight)
        grads = pull_back(group_cot * rowmask[:, None])
        totals = jax.tree.map(lambda running, adding: running + adding, totals, tuple(grads[1:]))
        return (totals, (encoded, grads[0]))
    zero_grads = (jnp.zeros_like(unit_stack), jnp.zeros_like(gain_weight), jnp.zeros_like(bias_weight), jnp.zeros_like(proj_weight))
    totals, (encoded, token_grad) = lax.scan(group_step, zero_grads, (inputs, cotangent, lengths))
    slot_grad = pull_units(totals[0])[0]
    unit_weights, unit_firsts, unit_seconds = adamw_step(unit_weight, unit_first, unit_second, slot_grad, RATE_MATRIX)
    gain_weights, gain_firsts, gain_seconds = adamw_step(gain_weight, gain_first, gain_second, totals[1], RATE_GAIN)
    bias_weights, bias_firsts, bias_seconds = adamw_step(bias_weight, bias_first, bias_second, totals[2], RATE_SMALL)
    proj_weights, proj_firsts, proj_seconds = adamw_step(proj_weight, proj_first, proj_second, totals[3], RATE_MATRIX)
    return (encoded.reshape(DOCS * SLOT, PROJ), token_grad.reshape(DOCS * SLOT, D), unit_weights, unit_firsts, unit_seconds, unit_weights.astype(jnp.bfloat16), gain_weights, gain_firsts, gain_seconds, bias_weights, bias_firsts, bias_seconds, proj_weights, proj_firsts, proj_seconds)
```

```python
import functools

import jax
import jax.numpy as jnp
from jax import lax
from jax.experimental import pallas as pl
from jax.experimental.pallas import tpu as pltpu
from jax.sharding import PartitionSpec as P

D = 768
HEAD_DIM = 64
FF = 3072
BUCKETS = 32
SLOT = 512
UROWS = 128
STEP = 5
HALF = UROWS // 2

NORM_EPS = 1e-06
ADAM_EPS = 1e-08
BETA_ONE = 0.5
BETA_TWO = 0.5
DECAY = 0.01
RATE_MATRIX = 0.02
RATE_SMALL = 0.1
RATE_GAIN = 0.6
GELU_C = 0.7978845608
GELU_K = 0.044715
MASKED = -1000000000.0

ROWS = D // UROWS
BLOCKS = FF // D
SQUARES = 4 * ROWS
SPREAD = 2 * SLOT
SMALL_TILE = 16
F32 = jnp.float32
BF16 = jnp.bfloat16
ANY = pl.BlockSpec(memory_space=pl.ANY)
SMEM = pl.BlockSpec(memory_space=pltpu.SMEM)
VMEM = pl.BlockSpec(memory_space=pltpu.VMEM)
PAIR = 2 * HEAD_DIM


def dot(left, right):
    return jnp.dot(left, right, preferred_element_type=F32)


def dot_nt(left, right):
    return lax.dot_general(left, right, (((1,), (1,)), ((), ())), preferred_element_type=F32)


def dot_tn(left, right):
    return lax.dot_general(left, right, (((0,), (0,)), ((), ())), preferred_element_type=F32)


def precise_dot(left, right):
    return jnp.dot(left, right, precision=lax.Precision.HIGHEST, preferred_element_type=F32)


def inverse_rms(values):
    return lax.rsqrt(jnp.mean(values * values, axis=-1, keepdims=True) + NORM_EPS)


def norm_back(values, inv_rms, gain_row, grad_in):
    weighted = grad_in * gain_row
    gain_grad = jnp.sum(grad_in * values * inv_rms, axis=0, keepdims=True)
    slope = jnp.mean(weighted * values, axis=-1, keepdims=True)
    values_grad = inv_rms * weighted - values * (inv_rms * inv_rms * inv_rms) * slope
    return values_grad, gain_grad


def adamw_step(weight_now, first_now, second_now, grad_in, rate):
    first_new = BETA_ONE * first_now + (1.0 - BETA_ONE) * grad_in
    second_new = BETA_TWO * second_now + (1.0 - BETA_TWO) * grad_in * grad_in
    first_hat = first_new / (1.0 - BETA_ONE**STEP)
    second_hat = second_new / (1.0 - BETA_TWO**STEP)
    weight_new = weight_now - rate * (
        first_hat / (jnp.sqrt(second_hat) + ADAM_EPS) + DECAY * weight_now
    )
    return weight_new, first_new, second_new


def params(limit_mib):
    return pltpu.CompilerParams(vmem_limit_bytes=limit_mib * 1024 * 1024)


def cost(flops, moved, exps=0):
    return pl.CostEstimate(flops=int(flops), bytes_accessed=int(moved), transcendentals=int(exps))


def ring_order(line):
    return list(range(0, line, 2)) + list(range(line - 1 - line % 2, 0, -2))


def ring_place(z, line):
    return jnp.where(z % 2 == 0, z // 2, line - (z + 1) // 2)


def ring_device(place, line):
    return jnp.where(2 * place < line, 2 * place, 2 * (line - place) - 1)


def hops(devices):
    line = devices // 4
    order = ring_order(line)
    after = {order[i]: order[(i + 1) % line] for i in range(line)}
    along_x = [(i, i ^ 1) for i in range(devices)]
    along_y = [(i, i ^ 2) for i in range(devices)]
    along_z = [(i, after[i // 4] * 4 + i % 4) for i in range(devices)]
    return along_x, along_y, along_z


def send(values, pairs):
    return lax.ppermute(values, "dp", pairs)


def swap(values):
    return lax.ppermute(values, "mp", [(0, 1), (1, 0)])


def unit_place(unit):
    inner = unit - SQUARES
    matrix = inner // (ROWS * BLOCKS)
    rest = inner % (ROWS * BLOCKS)
    wide = SQUARES + matrix * ROWS * BLOCKS + (rest % BLOCKS) * ROWS + rest // BLOCKS
    return jnp.where(unit < SQUARES, unit, wide)


def strays_kernel(own, most, devices, where_ref, weight_ref, keep_a, send_a, keep_b, send_b, stage, sem):
    line = devices // 4
    load = pltpu.make_async_copy(weight_ref.at[own:most], stage, sem)
    load.start()
    for out in (keep_a, send_a, keep_b, send_b):
        out[...] = jnp.zeros_like(out)
    load.wait()
    me = where_ref[0]
    first = where_ref[1]
    count = where_ref[2]
    for j in range(most - own):
        home = first + j

        @pl.when(jnp.logical_and(j < count, home < devices))
        def _():
            rel = jnp.bitwise_xor(home, me)
            rx = jnp.bitwise_and(rel, 1)
            ry = jnp.bitwise_and(rel // 2, 1)
            rz = (ring_place(home // 4, line) - ring_place(me // 4, line) + line) % line
            unit = stage[j].astype(BF16)
            for bit, (here, there) in enumerate(((keep_a, keep_b), (send_a, send_b))):

                @pl.when(rx == bit)
                def _():
                    here[ry, rz] = unit[:HALF]

                @pl.when(ry == bit)
                def _():
                    there[rx, rz] = unit[HALF:]


def assemble_kernel(own, devices, units, extra_count, where_ref, table_ref, *refs):
    line = devices // 4
    *pieces, out_ref, sem, extra_sem = refs
    strays, extra = pieces[8 * line], pieces[8 * line + 1]
    me = where_ref[0]
    slots = own + 1

    def unit_of(rx, ry, rz, slot):
        z = ring_device((ring_place(me // 4, line) - rz + line) % line, line)
        other = z * 4 + jnp.bitwise_xor(me % 4, 2 * ry + rx)
        return table_ref[other * slots + slot]

    for rz in range(line):
        for ry in range(2):
            for rx in range(2):
                block = 8 * rz + 4 * ry + 2 * rx
                for slot in range(own):
                    place = unit_of(rx, ry, rz, slot)
                    for half in range(2):
                        pltpu.make_async_copy(
                            pieces[block + half].at[slot],
                            out_ref.at[place, half * HALF : (half + 1) * HALF],
                            sem,
                        ).start()
                place = unit_of(rx, ry, rz, own)
                pltpu.make_async_copy(
                    strays.at[rz, 2 * ry + rx], out_ref.at[place], sem
                ).start()
    total = devices * slots
    done = 0
    while done < total:
        step = min(units, total - done)
        pltpu.make_async_copy(out_ref.at[0:step], out_ref.at[0:step], sem).wait()
        done += step
    if extra_count:

        @pl.loop(0, where_ref[3])
        def _(i):
            move = pltpu.make_async_copy(
                extra.at[i], out_ref.at[table_ref[devices * slots + i]], extra_sem
            )
            move.start()
            move.wait()


def spread_kernel(own, devices, units, where_ref, table_ref, squares_ref, wides_ref, small_ref, *refs):
    line = devices // 4
    *outs, sem, small_sem = refs
    me = where_ref[0]
    slots = own + 1
    stray_outs = outs[4 * line :]

    def ahead(rx, ry, rz):
        z = ring_device((ring_place(me // 4, line) + rz) % line, line)
        return z * 4 + jnp.bitwise_xor(me % 4, 2 * ry + rx)

    def fetch(place, rows, target):
        bounded = jnp.minimum(place, units - 1)

        @pl.when(bounded < SQUARES)
        def _():
            pltpu.make_async_copy(squares_ref.at[bounded, rows], target, sem).start()

        @pl.when(bounded >= SQUARES)
        def _():
            pltpu.make_async_copy(wides_ref.at[bounded - SQUARES, rows], target, sem).start()

    low, high = pl.ds(0, HALF), pl.ds(HALF, HALF)
    for rz in range(line - 1, -1, -1):
        for ry in range(2):
            for rx in range(2):
                other = ahead(rx, ry, rz)
                for slot in range(own):
                    place = table_ref[other * slots + slot]
                    fetch(place, low, outs[4 * rz + rx].at[ry, slot])
                    fetch(place, high, outs[4 * rz + 2 + ry].at[rx, slot])
                place = table_ref[other * slots + own]
                fetch(place, low, stray_outs[rx].at[ry, rz])
                fetch(place, high, stray_outs[2 + ry].at[rx, rz, low])
                pltpu.make_async_copy(
                    small_ref.at[other],
                    stray_outs[2 + ry].at[rx, rz, pl.ds(HALF, SMALL_TILE)],
                    small_sem,
                ).start()
    total = devices * slots
    done = 0
    while done < total:
        step = min(wides_ref.shape[0], total - done)
        pltpu.make_async_copy(wides_ref.at[0:step], wides_ref.at[0:step], sem).wait()
        done += step
    pltpu.make_async_copy(small_ref, small_ref, small_sem).wait()


def toeplitz(row):
    width = SPREAD
    tile = jnp.broadcast_to(pltpu.roll(row, width - (SLOT - 1), 1), (8, width))
    places = lax.broadcasted_iota(jnp.int32, (8, width), 0)
    for bit in (1, 2, 4):
        tile = jnp.where(jnp.bitwise_and(places, bit) != 0, pltpu.roll(tile, bit, 1), tile)
    reach = 8
    while reach < SLOT // 2:
        tile = jnp.concatenate([tile, pltpu.roll(tile, reach, 1)], axis=0)
        reach *= 2
    lower = jnp.concatenate([tile[:, width - reach :], tile[:, : SLOT - reach]], axis=1)
    return jnp.concatenate([tile[:, :SLOT], lower], axis=0)


def diagonals(tile):
    rows = SLOT
    while rows > 128:
        rows //= 2
        blank = jnp.zeros((rows, rows), F32)
        tile = jnp.concatenate([tile[rows:], blank], axis=1) + jnp.concatenate(
            [blank, tile[:rows]], axis=1
        )
    tile = jnp.concatenate([tile, jnp.zeros((rows, SPREAD - tile.shape[1]), F32)], axis=1)
    while rows > 8:
        rows //= 2
        tile = tile[rows:] + pltpu.roll(tile[:rows], rows, 1)
    places = lax.broadcasted_iota(jnp.int32, tile.shape, 0)
    for bit in (4, 2, 1):
        tile = jnp.where(jnp.bitwise_and(places, bit) == 0, pltpu.roll(tile, bit, 1), tile)
    return jnp.sum(tile, axis=0, keepdims=True)


def matrix(ref, first):
    return ref[first : first + ROWS].reshape(D, ref.shape[2])


def pair_columns(ref, step):
    return ref[:, pl.ds(pl.multiple_of(step * PAIR, PAIR), PAIR)]


def attend_kernel(
    lengths_ref, tokens_ref, gain_ref, weight_ref, bias_ref,
    norm_ref, query_ref, key_ref, value_ref, prob_ref, mixed_ref, part_ref,
):
    step = pl.program_id(0)

    @pl.when(step == 0)
    def _():
        inputs = tokens_ref[...].astype(F32)
        normed = (inputs * inverse_rms(inputs) * gain_ref[0:1, :]).astype(BF16)
        norm_ref[...] = normed
        query_ref[...] = dot(normed, matrix(weight_ref, 0)).astype(BF16)
        key_ref[...] = dot(normed, matrix(weight_ref, ROWS)).astype(BF16)
        value_ref[...] = dot(normed, matrix(weight_ref, 2 * ROWS)).astype(BF16)

    queries = pair_columns(query_ref, step)
    keys = pair_columns(key_ref, step)
    values = pair_columns(value_ref, step)
    lanes = lax.broadcasted_iota(jnp.int32, (SLOT, PAIR), 1) // HEAD_DIM
    seen = lax.broadcasted_iota(jnp.int32, (1, SLOT), 1) < lengths_ref[0]
    mixes = []
    for which in range(2):
        scores = dot_nt(jnp.where(lanes == which, queries, jnp.zeros_like(queries)), keys)
        scores = scores + toeplitz(bias_ref[pl.ds(2 * step + which, 1), :])
        scores = jnp.where(seen, scores, MASKED)
        powers = jnp.exp(scores - jnp.max(scores, axis=-1, keepdims=True))
        probabilities = powers * (1.0 / jnp.sum(powers, axis=-1, keepdims=True))
        prob_ref[which] = probabilities
        mixes.append(dot(probabilities.astype(BF16), values))
    mixed = jnp.where(lanes == 0, mixes[0], mixes[1]).astype(BF16)
    mixed_ref[:, pl.ds(pl.multiple_of(step * PAIR, PAIR), PAIR)] = mixed

    @pl.when(step == pl.num_programs(0) - 1)
    def _():
        part_ref[...] = dot_nt(mixed_ref[...], matrix(weight_ref, 3 * ROWS))


def gelu_tanh(values):
    return jnp.tanh(GELU_C * (values + GELU_K * values * values * values))


def feed_kernel(
    tokens_ref, mine_ref, other_ref, gain_ref, gate_w, up_w, down_w,
    residual_ref, norm_ref, gate_ref, up_ref, hidden_ref, part_ref,
):
    step = pl.program_id(0)

    @pl.when(step == 0)
    def _():
        residual = tokens_ref[...].astype(F32) + (mine_ref[...] + other_ref[...])
        residual_ref[...] = residual
        norm_ref[...] = (residual * inverse_rms(residual) * gain_ref[1:2, :]).astype(BF16)
        part_ref[...] = jnp.zeros_like(part_ref)

    normed = norm_ref[...]
    gate = dot(normed, matrix(gate_w, 0))
    up = dot(normed, matrix(up_w, 0))
    gate_ref[...] = gate
    up_ref[...] = up
    hidden = (0.5 * gate * (1.0 + gelu_tanh(gate)) * up).astype(BF16)
    hidden_ref[...] = hidden
    part_ref[...] += dot_nt(hidden, matrix(down_w, 0))


def turn_kernel(
    lengths_ref, residual_ref, mine_ref, other_ref, gain_ref, proj_ref, proj_other, cot_ref, cot_other,
    gate_ref, up_ref, gate_w, up_w, down_w,
    encoded_ref, proj_grad, gain_grad, grad_ref, feed_ref, dgate_ref, dup_ref, part_ref,
):
    step = pl.program_id(0)

    @pl.when(step == 0)
    def _():
        residual = residual_ref[...] + (mine_ref[...] + other_ref[...])
        inv_rms = inverse_rms(residual)
        normed = (residual * inv_rms * gain_ref[2:3, :]).astype(BF16)
        encoded_ref[...] = dot(normed, proj_ref[...])
        rows = lax.broadcasted_iota(jnp.int32, (SLOT, 1), 0) < lengths_ref[0]
        mine = jnp.where(rows, cot_ref[...], jnp.zeros_like(cot_ref))
        other = jnp.where(rows, cot_other[...], jnp.zeros_like(cot_other))
        backward = dot_tn(mine, normed)
        proj_grad[0] = backward[:, : D // 2]
        proj_grad[1] = backward[:, D // 2 :]
        third = dot_nt(mine, proj_ref[...]) + dot_nt(other, proj_other[...])
        grad, gain = norm_back(residual, inv_rms, gain_ref[2:3, :], third)
        gain_grad[...] = gain
        grad_ref[...] = grad
        feed_ref[...] = grad.astype(BF16)
        part_ref[...] = jnp.zeros_like(part_ref)

    dhidden = dot(feed_ref[...], matrix(down_w, 0))
    gate = gate_ref[...]
    bend = gelu_tanh(gate)
    slope = 0.5 * (1.0 + bend) + 0.5 * gate * (1.0 - bend * bend) * (
        GELU_C * (1.0 + 3.0 * GELU_K * gate * gate)
    )
    dgate = (dhidden * up_ref[...] * slope).astype(BF16)
    dup = (dhidden * (0.5 * gate * (1.0 + bend))).astype(BF16)
    dgate_ref[...] = dgate
    dup_ref[...] = dup
    part_ref[...] += dot_nt(dgate, matrix(gate_w, 0)) + dot_nt(dup, matrix(up_w, 0))


def wide_grads_kernel(norm_ref, feed_ref, hidden_ref, dgate_ref, dup_ref, out_ref):
    normed = norm_ref[...]
    shape = out_ref.shape[2:]
    out_ref[0, 0] = dot_tn(normed, dgate_ref[...]).astype(BF16).reshape(shape)
    out_ref[1, 0] = dot_tn(normed, dup_ref[...]).astype(BF16).reshape(shape)
    out_ref[2, 0] = dot_tn(feed_ref[...], hidden_ref[...]).astype(BF16).reshape(shape)


def attend_back_kernel(
    grad_ref, residual_ref, mine_ref, other_ref, gain_ref, weight_ref,
    query_ref, key_ref, value_ref, prob_ref,
    grad_one, gain_grad, attn_ref, dquery_ref, dkey_ref, dvalue_ref, part_ref, offset_ref,
    dmixed_ref,
):
    step = pl.program_id(0)

    @pl.when(step == 0)
    def _():
        residual = residual_ref[...]
        second = mine_ref[...] + other_ref[...]
        back, gain = norm_back(residual, inverse_rms(residual), gain_ref[1:2, :], second)
        gain_grad[...] = gain
        total = grad_ref[...] + back
        grad_one[...] = total
        lowered = total.astype(BF16)
        attn_ref[...] = lowered
        dmixed_ref[...] = dot(lowered, matrix(weight_ref, 3 * ROWS)).astype(BF16)
        offset_ref[...] = jnp.zeros_like(offset_ref)

    queries = pair_columns(query_ref, step)
    keys = pair_columns(key_ref, step)
    values = pair_columns(value_ref, step)
    dmixed = pair_columns(dmixed_ref, step)
    lanes = lax.broadcasted_iota(jnp.int32, (SLOT, PAIR), 1) // HEAD_DIM
    parts = []
    for which in range(2):
        dprob = dot_nt(jnp.where(lanes == which, dmixed, jnp.zeros_like(dmixed)), values)
        probabilities = prob_ref[which]
        share = jnp.sum(probabilities * dprob, axis=-1, keepdims=True)
        dscore = (probabilities * (dprob - share)).astype(BF16)
        parts.append(
            (
                dot(dscore, keys),
                dot_tn(dscore, queries),
                dot_tn(probabilities.astype(BF16), dmixed),
            )
        )
        offset_ref[pl.ds(2 * step + which, 1), :] = diagonals(dscore.astype(F32))
    for out, first, second in zip((dquery_ref, dkey_ref, dvalue_ref), *parts):
        columns = pl.ds(pl.multiple_of(step * PAIR, PAIR), PAIR)
        out[:, columns] = jnp.where(lanes == 0, first, second).astype(BF16)

    @pl.when(step == pl.num_programs(0) - 1)
    def _():
        part_ref[...] = (
            dot_nt(dquery_ref[...], matrix(weight_ref, 0))
            + dot_nt(dkey_ref[...], matrix(weight_ref, ROWS))
            + dot_nt(dvalue_ref[...], matrix(weight_ref, 2 * ROWS))
        ).astype(BF16)


def square_grads_kernel(norm_ref, attn_ref, mixed_ref, dquery_ref, dkey_ref, dvalue_ref, out_ref):
    normed = norm_ref[...]
    shape = (ROWS,) + out_ref.shape[1:]
    for i, ref in enumerate((dquery_ref, dkey_ref, dvalue_ref)):
        out_ref[i * ROWS : (i + 1) * ROWS] = dot_tn(normed, ref[...]).astype(BF16).reshape(shape)
    out_ref[3 * ROWS :] = dot_tn(attn_ref[...], mixed_ref[...]).astype(BF16).reshape(shape)


def token_grad_kernel(tokens_ref, grad_ref, mine_ref, other_ref, gain_ref, out_ref, gain_grad):
    inputs = tokens_ref[...].astype(F32)
    first = mine_ref[...].astype(F32) + other_ref[...].astype(F32)
    back, gain = norm_back(inputs, inverse_rms(inputs), gain_ref[0:1, :], first)
    out_ref[...] = grad_ref[...] + back
    gain_grad[...] = gain


def order_small_kernel(devices, where_ref, strays_ref, out_ref):
    line = devices // 4
    me = where_ref[0]
    for rz in range(line):
        z = ring_device((ring_place(me // 4, line) - rz + line) % line, line)
        for near in range(4):
            other = z * 4 + jnp.bitwise_xor(me % 4, near)
            out_ref[other] = strays_ref[rz, near].astype(F32)


def stray_update_kernel(own, devices, where_ref, weight, first, second, stray, extra, *refs):
    outs = refs[-4:]
    slot = pl.program_id(0)
    index = where_ref[1] + slot
    grad = jnp.where(index < devices, stray[0].astype(F32), extra[0].astype(F32))
    grad = jnp.where(slot < where_ref[2], grad, 0.0)
    update_slot(weight, first, second, grad, outs)


def update_slot(weight, first, second, grad, outs):
    new_weight, new_first, new_second = adamw_step(
        weight[0], first[0], second[0], grad, RATE_MATRIX
    )
    outs[0][0] = new_weight
    outs[1][0] = new_first
    outs[2][0] = new_second
    outs[3][0] = new_weight.astype(BF16)


def own_update_kernel(where_ref, weight, first, second, grad_ref, *refs):
    outs = refs[-4:]
    grad = jnp.where(pl.program_id(0) < where_ref[4], grad_ref[0], 0.0)
    update_slot(weight, first, second, grad, outs)


def shards(
    tokens,
    out_grad,
    doc_lengths,
    owner_list,
    bucket_table,
    unit_weight,
    unit_first,
    unit_second,
    gain_weight,
    gain_first,
    gain_second,
    bias_weight,
    bias_first,
    bias_second,
    proj_weight,
    proj_first,
    proj_second,
):
    most, _, width = unit_weight.shape
    heads = bias_weight.shape[1]
    count = tokens.shape[0]
    units = owner_list.shape[0]
    proj_width = proj_weight.shape[1]
    devices = lax.axis_size("dp")
    line = devices // 4
    own = max(1, (units - 1) // devices)
    slots = own + 1
    along_x, along_y, along_z = hops(devices)
    me = lax.axis_index("dp").astype(jnp.int32)

    full, left = divmod(units, most)
    stray_most = full * (most - own) + max(0, left - own)
    extra_count = max(0, stray_most - devices)
    indices = jnp.arange(units, dtype=jnp.int32)
    same = owner_list[:, None] == owner_list[None, :]
    rank = jnp.sum((same & (indices[None, :] < indices[:, None])).astype(jnp.int32), axis=1)
    device_ids = jnp.arange(devices, dtype=jnp.int32)
    owned = jnp.sum((owner_list[None, :] == device_ids[:, None]).astype(jnp.int32), axis=1)
    is_stray = rank >= own
    before = (owner_list[None, :] < owner_list[:, None]) & is_stray[None, :]
    stray_index = jnp.sum(before.astype(jnp.int32), axis=1) + rank - own
    position = jnp.where(
        is_stray,
        jnp.where(stray_index < devices, stray_index * slots + own, devices * slots + stray_index - devices),
        owner_list * slots + rank,
    )
    position_ids = jnp.arange(devices * slots + max(extra_count, 1), dtype=jnp.int32)
    hit = position[None, :] == position_ids[:, None]
    placed = jnp.sum(jnp.where(hit, unit_place(indices)[None, :], 0), axis=1)
    table = jnp.where(jnp.any(hit, axis=1), placed, units).astype(jnp.int32)
    my_count = jnp.sum((owner_list == me).astype(jnp.int32))
    my_first = jnp.sum(((owner_list < me) & is_stray).astype(jnp.int32))
    stray_total = jnp.sum(is_stray.astype(jnp.int32))
    where = jnp.stack(
        [me, my_first, jnp.maximum(my_count - own, 0), jnp.maximum(stray_total - devices, 0), my_count]
    ).astype(jnp.int32)
    many = stray_total > devices

    lower = [unit_weight[:own, :HALF].astype(BF16)]
    upper = [unit_weight[:own, HALF:].astype(BF16)]
    for _ in range(line - 1):
        lower.append(send(lower[-1], along_z))
        upper.append(send(upper[-1], along_z))
    pieces = []
    for low, high in zip(lower, upper):
        low_y, high_x = send(low, along_y), send(high, along_x)
        low_x, high_y = send(low, along_x), send(high, along_y)
        low_xy, high_xy = send(low_y, along_x), send(high_x, along_y)
        pieces += [low, high, low_x, high_x, low_y, high_y, low_xy, high_xy]

    half_shape = jax.ShapeDtypeStruct((2, line, HALF, width), BF16)
    keep_a, send_a, keep_b, send_b = pl.pallas_call(
        functools.partial(strays_kernel, own, most, devices),
        out_shape=[half_shape] * 4,
        in_specs=[SMEM, ANY],
        out_specs=[VMEM] * 4,
        scratch_shapes=[
            pltpu.VMEM((most - own, UROWS, width), F32),
            pltpu.SemaphoreType.DMA,
        ],
        compiler_params=params(40),
    )(where, unit_weight)

    def gather_near(values):
        wide = jnp.stack([values, send(values, along_x)])
        return jnp.concatenate([wide, send(wide, along_y)])

    def gather_strays(values):
        near = [gather_near(values)]
        for _ in range(line - 1):
            near.append(send(near[-1], along_z))
        return jnp.stack(near)

    def sum_strays(keep_low, send_low, keep_high, send_high):
        from_x = send(send_low, along_x)
        from_y = send(send_high, along_y)
        low_y = send((keep_low[1].astype(F32) + from_x[1].astype(F32)).astype(BF16), along_y)
        high_x = send((keep_high[1].astype(F32) + from_y[1].astype(F32)).astype(BF16), along_x)
        low = keep_low[0].astype(F32) + from_x[0].astype(F32) + low_y.astype(F32)
        high = keep_high[0].astype(F32) + from_y[0].astype(F32) + high_x.astype(F32)
        summed = jnp.concatenate([low, high], axis=1)
        moving = summed[line - 1]
        for rz in range(line - 2, -1, -1):
            moving = summed[rz] + send(moving.astype(BF16), along_z).astype(F32)
        return moving.astype(BF16)

    strays = gather_strays(sum_strays(keep_a, send_a, keep_b, send_b))

    extra_shape = (max(extra_count, 1), UROWS, width)
    extra_ids = devices + jnp.arange(extra_shape[0], dtype=jnp.int32)

    def extra_weights():
        slot = extra_ids - my_first + own
        mine = (slot >= own) & (slot < my_count)
        taken = jnp.take(unit_weight, jnp.clip(slot, 0, most - 1), axis=0)
        return lax.psum(jnp.where(mine[:, None, None], taken, 0.0), "dp").astype(BF16)

    def no_extra():
        return jnp.zeros(extra_shape, BF16)

    extra = lax.cond(many, extra_weights, no_extra) if extra_count else no_extra()

    stack = pl.pallas_call(
        functools.partial(assemble_kernel, own, devices, units, extra_count),
        out_shape=jax.ShapeDtypeStruct((units + 1, UROWS, width), BF16),
        in_specs=[SMEM, SMEM] + [ANY] * (len(pieces) + 2),
        out_specs=ANY,
        scratch_shapes=[pltpu.SemaphoreType.DMA, pltpu.SemaphoreType.DMA],
        compiler_params=params(16),
    )(where, table, *pieces, strays, extra)

    bucket_hot = (bucket_table[:, None] == jnp.arange(BUCKETS, dtype=jnp.int32)[None, :]).astype(F32)
    bucket_hot = jnp.pad(bucket_hot, ((0, SPREAD - bucket_hot.shape[0]), (0, 0)))
    bias_rows = jnp.pad(precise_dot(bucket_hot, bias_weight).T, ((0, 8 - heads % 8), (0, 0)))
    proj_low = proj_weight.astype(BF16)
    proj_other = swap(proj_low)
    cot_other = swap(out_grad)

    def whole(shape):
        return pl.BlockSpec(shape, lambda i: (0,) * len(shape))

    wide_shape = (count, D)
    head_shape = (count, width)
    square_spec = whole((SQUARES, UROWS, width))
    prob_spec = pl.BlockSpec((2, SLOT, SLOT), lambda i: (i, 0, 0))
    gain_spec = whole((3, D))
    bias_spec = whole(bias_rows.shape)
    column_spec = pl.BlockSpec((count, width), lambda i: (0, i))

    def unit_spec(which):
        return pl.BlockSpec((ROWS, UROWS, width), lambda i: (SQUARES // ROWS + which * BLOCKS + i, 0, 0))

    wide_specs = [unit_spec(0), unit_spec(1), unit_spec(2)]

    def like(shape, kind=F32):
        return jax.ShapeDtypeStruct(shape, kind)

    first_in, queries, keys, values, probabilities, mixed, attn_part = pl.pallas_call(
        attend_kernel,
        grid=(heads // 2,),
        in_specs=[SMEM, whole(wide_shape), gain_spec, square_spec, bias_spec],
        out_specs=[whole(wide_shape)] + [whole(head_shape)] * 3 + [prob_spec, whole(head_shape), whole(wide_shape)],
        out_shape=[like(wide_shape, BF16)]
        + [like(head_shape, BF16)] * 3
        + [like((heads, SLOT, SLOT)), like(head_shape, BF16), like(wide_shape)],
        compiler_params=params(56),
        cost_estimate=cost(8 * count * D * width, 12e6, heads * SLOT * SLOT),
    )(doc_lengths, tokens, gain_weight, stack, bias_rows)

    residual_one, second_in, gate, up, hidden, feed_part = pl.pallas_call(
        feed_kernel,
        grid=(BLOCKS,),
        in_specs=[whole(wide_shape)] * 3 + [gain_spec] + wide_specs,
        out_specs=[whole(wide_shape)] * 2 + [column_spec] * 3 + [whole(wide_shape)],
        out_shape=[
            like(wide_shape),
            like(wide_shape, BF16),
            like((count, BLOCKS * width)),
            like((count, BLOCKS * width)),
            like((count, BLOCKS * width), BF16),
            like(wide_shape),
        ],
        compiler_params=params(56),
        cost_estimate=cost(6 * count * D * BLOCKS * width, 24e6),
    )(tokens, attn_part, swap(attn_part), gain_weight, stack, stack, stack)

    encoded, proj_grad, gain_three, grad_two, feed_grad, dgate, dup, second_part = pl.pallas_call(
        turn_kernel,
        grid=(BLOCKS,),
        in_specs=[SMEM]
        + [whole(wide_shape)] * 3
        + [gain_spec]
        + [whole((D, proj_width))] * 2
        + [whole((count, proj_width))] * 2
        + [column_spec] * 2
        + wide_specs,
        out_specs=[
            whole((count, proj_width)),
            whole((2, proj_width, D // 2)),
            whole((1, D)),
            whole(wide_shape),
            whole(wide_shape),
            column_spec,
            column_spec,
            whole(wide_shape),
        ],
        out_shape=[
            like((count, proj_width)),
            like((2, proj_width, D // 2)),
            like((1, D)),
            like(wide_shape),
            like(wide_shape, BF16),
            like((count, BLOCKS * width), BF16),
            like((count, BLOCKS * width), BF16),
            like(wide_shape),
        ],
        compiler_params=params(56),
        cost_estimate=cost(6 * count * D * BLOCKS * width, 24e6),
    )(
        doc_lengths, residual_one, feed_part, swap(feed_part), gain_weight, proj_low, proj_other,
        out_grad, cot_other, gate, up, stack, stack, stack,
    )

    wides = pl.pallas_call(
        wide_grads_kernel,
        grid=(BLOCKS,),
        in_specs=[whole(wide_shape)] * 2 + [column_spec] * 3,
        out_specs=pl.BlockSpec((3, 1, ROWS, UROWS, width), lambda i: (0, i, 0, 0, 0)),
        out_shape=like((3, BLOCKS, ROWS, UROWS, width), BF16),
        compiler_params=params(56),
        cost_estimate=cost(6 * count * D * BLOCKS * width, 12e6),
    )(second_in, feed_grad, hidden, dgate, dup)
    wides = wides.reshape(3 * BLOCKS * ROWS, UROWS, width)

    grad_one, gain_two, attn_grad, dquery, dkey, dvalue, first_part, offset_grad = pl.pallas_call(
        attend_back_kernel,
        grid=(heads // 2,),
        in_specs=[whole(wide_shape)] * 4 + [gain_spec, square_spec] + [whole(head_shape)] * 3 + [prob_spec],
        out_specs=[whole(wide_shape), whole((1, D)), whole(wide_shape)]
        + [whole(head_shape)] * 3
        + [whole(wide_shape), bias_spec],
        out_shape=[like(wide_shape), like((1, D)), like(wide_shape, BF16)]
        + [like(head_shape, BF16)] * 3
        + [like(wide_shape, BF16), like(bias_rows.shape)],
        scratch_shapes=[pltpu.VMEM(head_shape, BF16)],
        compiler_params=params(56),
        cost_estimate=cost(10 * count * D * width, 16e6),
    )(
        grad_two, residual_one, second_part, swap(second_part), gain_weight, stack,
        queries, keys, values, probabilities,
    )

    squares = pl.pallas_call(
        square_grads_kernel,
        out_shape=like((SQUARES, UROWS, width), BF16),
        compiler_params=params(56),
        cost_estimate=cost(8 * count * D * width, 6e6),
    )(first_in, attn_grad, mixed, dquery, dkey, dvalue)

    token_grad, gain_one = pl.pallas_call(
        token_grad_kernel,
        out_shape=[like(wide_shape), like((1, D))],
        compiler_params=params(56),
        cost_estimate=cost(20 * count * D, 6e6),
    )(tokens, grad_one, first_part, swap(first_part), gain_weight)

    bias_grad = precise_dot(bucket_hot.T, offset_grad[:heads].T)
    gain_rows = jnp.concatenate([gain_one, gain_two, gain_three]).reshape(-1, width)
    bias_row = jnp.pad(bias_grad.reshape(1, -1), ((0, 0), (0, width - BUCKETS * heads)))
    proj_rows = proj_grad.reshape(-1, width)
    small = jnp.concatenate([proj_rows, gain_rows, bias_row])
    share = -(-small.shape[0] // devices)
    small = jnp.pad(small, ((0, share * devices - small.shape[0]), (0, 0)))
    small = small.reshape(devices, share, width)
    small = jnp.pad(small, ((0, 0), (0, SMALL_TILE - share), (0, 0))).astype(BF16)

    part_shape = like((2, own, HALF, width), BF16)
    stray_low = like((2, line, HALF, width), BF16)
    stray_high = like((2, line, HALF + SMALL_TILE, width), BF16)
    spread = pl.pallas_call(
        functools.partial(spread_kernel, own, devices, units),
        out_shape=[part_shape] * (4 * line) + [stray_low] * 2 + [stray_high] * 2,
        in_specs=[SMEM, SMEM, ANY, ANY, ANY],
        out_specs=[ANY] * (4 * line + 4),
        scratch_shapes=[pltpu.SemaphoreType.DMA, pltpu.SemaphoreType.DMA],
        compiler_params=params(16),
    )(where, table, squares, wides, small)

    stray_grads = gather_strays(sum_strays(*spread[4 * line :]))

    moving = None
    for rz in range(line - 1, -1, -1):
        keep_a, send_a, keep_b, send_b = spread[4 * rz : 4 * rz + 4]
        from_x = send(send_a, along_x)
        from_y = send(send_b, along_y)
        low_y = send((keep_a[1].astype(F32) + from_x[1].astype(F32)).astype(BF16), along_y)
        high_x = send((keep_b[1].astype(F32) + from_y[1].astype(F32)).astype(BF16), along_x)
        low = keep_a[0].astype(F32) + from_x[0].astype(F32) + low_y.astype(F32)
        high = keep_b[0].astype(F32) + from_y[0].astype(F32) + high_x.astype(F32)
        summed = jnp.concatenate([low, high], axis=1)
        if moving is not None:
            summed = summed + send(moving.astype(BF16), along_z).astype(F32)
        moving = summed
    own_grads = moving

    def extra_grads():
        every = jnp.concatenate([squares, wides]).astype(F32)
        taken = jnp.take(every, jnp.minimum(table[devices * slots :], units - 1), axis=0)
        return lax.psum(taken, "dp").astype(BF16)

    extra_grad = lax.cond(many, extra_grads, no_extra) if extra_count else no_extra()

    def near_place(index):
        z = ring_place(index // 4, line)
        rz = (ring_place(me // 4, line) - z + line) % line
        return rz * 4 + jnp.bitwise_xor(index % 4, me % 4)

    stray_ids = jnp.minimum(my_first + jnp.arange(most - own, dtype=jnp.int32), devices - 1)
    extra_picks = jnp.clip(my_first + jnp.arange(most - own, dtype=jnp.int32) - devices, 0, extra_shape[0] - 1)
    picks = jnp.concatenate([where, near_place(stray_ids), extra_picks])
    head = where.shape[0]

    def slot_spec(first):
        return pl.BlockSpec((1, UROWS, width), lambda i, pick: (first + i, 0, 0))

    stack_shape = unit_weight.shape
    update_shapes = [like(stack_shape)] * 3 + [like(stack_shape, BF16)]
    partial_update = pl.pallas_call(
        functools.partial(stray_update_kernel, own, devices),
        grid_spec=pltpu.PrefetchScalarGridSpec(
            num_scalar_prefetch=1,
            grid=(most - own,),
            in_specs=[slot_spec(own)] * 3
            + [
                pl.BlockSpec((1, UROWS, width), lambda i, pick: (pick[head + i], 0, 0)),
                pl.BlockSpec((1, UROWS, width), lambda i, pick: (pick[head + most - own + i], 0, 0)),
            ],
            out_specs=[slot_spec(own)] * 4,
        ),
        out_shape=update_shapes,
        compiler_params=params(32),
        cost_estimate=cost(1e7, 10e6),
    )(picks, unit_weight, unit_first, unit_second, stray_grads.reshape(devices, -1, width), extra_grad)
    unit_weights, unit_firsts, unit_seconds, unit_copies = pl.pallas_call(
        own_update_kernel,
        grid_spec=pltpu.PrefetchScalarGridSpec(
            num_scalar_prefetch=1,
            grid=(own,),
            in_specs=[slot_spec(0)] * 4 + [ANY] * 4,
            out_specs=[slot_spec(0)] * 4,
        ),
        out_shape=update_shapes,
        input_output_aliases={5: 0, 6: 1, 7: 2, 8: 3},
        compiler_params=params(32),
        cost_estimate=cost(1e7, 6e6),
    )(where, unit_weight, unit_first, unit_second, own_grads, *partial_update)

    small_total = pl.pallas_call(
        functools.partial(order_small_kernel, devices),
        out_shape=like((devices, SMALL_TILE, width)),
        in_specs=[SMEM, VMEM],
        compiler_params=params(32),
    )(where, stray_grads[:, :, UROWS:])
    small_total = small_total[:, :share].reshape(devices * share, width)
    proj_count = proj_rows.shape[0]
    proj_total = small_total[:proj_count].reshape(2, proj_width, D // 2)
    proj_total = proj_total.transpose(0, 2, 1).reshape(D, proj_width)
    gain_total = small_total[proj_count : proj_count + gain_rows.shape[0]].reshape(3, D)
    bias_total = small_total[proj_count + gain_rows.shape[0], : BUCKETS * heads].reshape(BUCKETS, heads)
    gain_weights, gain_firsts, gain_seconds = adamw_step(
        gain_weight, gain_first, gain_second, gain_total, RATE_GAIN
    )
    bias_weights, bias_firsts, bias_seconds = adamw_step(
        bias_weight, bias_first, bias_second, bias_total, RATE_SMALL
    )
    proj_weights, proj_firsts, proj_seconds = adamw_step(
        proj_weight, proj_first, proj_second, proj_total, RATE_MATRIX
    )
    return (
        encoded,
        token_grad,
        unit_weights,
        unit_firsts,
        unit_seconds,
        unit_copies,
        gain_weights,
        gain_firsts,
        gain_seconds,
        bias_weights,
        bias_firsts,
        bias_seconds,
        proj_weights,
        proj_firsts,
        proj_seconds,
    )


def solution(mesh):
    in_specs = (
        P("dp", None),
        P("dp", "mp"),
        P("dp"),
        P(),
        P(),
        P("dp", None, "mp"),
        P("dp", None, "mp"),
        P("dp", None, "mp"),
        P(),
        P(),
        P(),
        P(None, "mp"),
        P(None, "mp"),
        P(None, "mp"),
        P(None, "mp"),
        P(None, "mp"),
        P(None, "mp"),
    )
    out_specs = (
        P("dp", "mp"),
        P("dp", None),
        P("dp", None, "mp"),
        P("dp", None, "mp"),
        P("dp", None, "mp"),
        P("dp", None, "mp"),
        P(),
        P(),
        P(),
        P(None, "mp"),
        P(None, "mp"),
        P(None, "mp"),
        P(None, "mp"),
        P(None, "mp"),
        P(None, "mp"),
    )
    return jax.shard_map(shards, mesh=mesh, in_specs=in_specs, out_specs=out_specs, check_vma=False)
```

```python
import functools

import jax
import jax.numpy as jnp
from jax import lax
from jax.experimental import pallas as pl
from jax.experimental.pallas import tpu as pltpu
from jax.sharding import PartitionSpec as P

D = 768
HEAD_DIM = 64
FF = 3072
BUCKETS = 32
SLOT = 512
UROWS = 128
STEP = 5
HALF = UROWS // 2

NORM_EPS = 1e-06
ADAM_EPS = 1e-08
BETA_ONE = 0.5
BETA_TWO = 0.5
DECAY = 0.01
RATE_MATRIX = 0.02
RATE_SMALL = 0.1
RATE_GAIN = 0.6
GELU_C = 0.7978845608
GELU_K = 0.044715
MASKED = -1000000000.0

ROWS = D // UROWS
BLOCKS = FF // D
SQUARES = 4 * ROWS
FRONT = 3 * ROWS
SPREAD = 2 * SLOT
STRAY_TILE = 16
WINDOWS = 2, 2, 3
BACK_WINDOWS = 2, 2, 1
ALONG_X, ALONG_Y, ALONG_Z = 0, 1, 2
F32 = jnp.float32
BF16 = jnp.bfloat16
ANY = pl.BlockSpec(memory_space=pl.ANY)
SMEM = pl.BlockSpec(memory_space=pltpu.SMEM)
VMEM = pl.BlockSpec(memory_space=pltpu.VMEM)
HBM = pl.BlockSpec(memory_space=pltpu.HBM)
PAIR = 2 * HEAD_DIM


def dot(left, right):
    return jnp.dot(left, right, preferred_element_type=F32)


def dot_nt(left, right):
    return lax.dot_general(left, right, (((1,), (1,)), ((), ())), preferred_element_type=F32)


def dot_tn(left, right):
    return lax.dot_general(left, right, (((0,), (0,)), ((), ())), preferred_element_type=F32)


def precise_dot(left, right):
    return jnp.dot(left, right, precision=lax.Precision.HIGHEST, preferred_element_type=F32)


def inverse_rms(values):
    return lax.rsqrt(jnp.mean(values * values, axis=-1, keepdims=True) + NORM_EPS)


def norm_back(values, inv_rms, gain_row, grad_in):
    weighted = grad_in * gain_row
    gain_grad = jnp.sum(grad_in * values * inv_rms, axis=0, keepdims=True)
    slope = jnp.mean(weighted * values, axis=-1, keepdims=True)
    values_grad = inv_rms * weighted - values * (inv_rms * inv_rms * inv_rms) * slope
    return values_grad, gain_grad


def adamw_step(weight_now, first_now, second_now, grad_in, rate):
    first_new = BETA_ONE * first_now + (1.0 - BETA_ONE) * grad_in
    second_new = BETA_TWO * second_now + (1.0 - BETA_TWO) * grad_in * grad_in
    first_hat = first_new / (1.0 - BETA_ONE**STEP)
    second_hat = second_new / (1.0 - BETA_TWO**STEP)
    weight_new = weight_now - rate * (
        first_hat / (jnp.sqrt(second_hat) + ADAM_EPS) + DECAY * weight_now
    )
    return weight_new, first_new, second_new


def params(limit_mib):
    return pltpu.CompilerParams(vmem_limit_bytes=limit_mib * 1024 * 1024)


def timed(micros):
    return pl.CostEstimate(flops=int(micros * 1.15e9), bytes_accessed=int(micros * 1e5), transcendentals=0)


def ring_order(line):
    return list(range(0, line, 2)) + list(range(line - 1 - line % 2, 0, -2))


def ring_place(z, line):
    return jnp.where(z % 2 == 0, z // 2, line - (z + 1) // 2)


def ring_device(place, line):
    return jnp.where(2 * place < line, 2 * place, 2 * (line - place) - 1)


def hops(devices):
    line = devices // 4
    order = ring_order(line)
    after = {order[i]: order[(i + 1) % line] for i in range(line)}
    along_x = [(i, i ^ 1) for i in range(devices)]
    along_y = [(i, i ^ 2) for i in range(devices)]
    along_z = [(i, after[i // 4] * 4 + i % 4) for i in range(devices)]
    return along_x, along_y, along_z


def swap(values):
    return lax.ppermute(values, "mp", [(0, 1), (1, 0)])


def rest_place(unit):
    inner = unit - SQUARES
    matrix = inner // (ROWS * BLOCKS)
    rest = inner % (ROWS * BLOCKS)
    wide = ROWS + matrix * ROWS * BLOCKS + (rest % BLOCKS) * ROWS + rest // BLOCKS
    return jnp.where(unit < SQUARES, unit - FRONT, wide)


def after(values, other):
    return lax.optimization_barrier((values, other))[0]


class Links:
    def __init__(self, devices, *windows):
        self.pairs = hops(devices)
        self.sent = ([], [], [])
        self.windows = windows
        self.gate = None

    def settle(self, values):
        return values if self.gate is None else after(values, self.gate)

    def send(self, values, axis, steps=1):
        queue = self.sent[axis]
        window = self.windows[axis] if self.windows else len(queue) + 1
        if len(queue) >= window:
            values = after(values, queue[-window])
        step = dict(self.pairs[axis])
        reach = dict(step)
        for _ in range(steps - 1):
            reach = {i: step[j] for i, j in reach.items()}
        queue.append(lax.ppermute(values, "dp", sorted(reach.items())))
        return queue[-1]


def strays_kernel(own, most, devices, where_ref, index_ref, weight_ref, *refs):
    line = devices // 4
    *outs, stage, sem = refs
    load = pltpu.make_async_copy(weight_ref.at[own:most], stage, sem)
    load.start()
    for out in outs:
        out[...] = jnp.zeros_like(out)
    load.wait()
    me = where_ref[0]
    for j in range(most - own):
        home = index_ref[j]

        @pl.when(home >= 0)
        def _():
            rel = jnp.bitwise_xor(home, me)
            rx = jnp.bitwise_and(rel, 1)
            ry = jnp.bitwise_and(rel // 2, 1)
            rz = (ring_place(home // 4, line) - ring_place(me // 4, line) + line) % line
            unit = stage[j].astype(BF16)
            for odd, (near, far) in enumerate(((rx, ry), (ry, rx))):
                for sent in range(2):

                    @pl.when(jnp.logical_and(rz % 2 == odd, near == sent))
                    def _():
                        outs[2 * odd + sent][far, rz // 2] = unit


def gather_units(own, devices, layout, where_ref, table_ref, pieces, extra_ref, stack, front_sem, rest_sem):
    line = devices // 4
    me = where_ref[0]
    slots = own + 1

    def fetch(source, place):
        @pl.when(place < FRONT)
        def _():
            pltpu.make_async_copy(source, stack.at[place], front_sem).start()

        @pl.when(place >= FRONT)
        def _():
            pltpu.make_async_copy(source, stack.at[place], rest_sem).start()

    for piece, spots in zip(pieces, layout):
        for i, (rx, ry, rz, slot) in enumerate(spots):
            z = ring_device((ring_place(me // 4, line) - rz + line) % line, line)
            other = z * 4 + jnp.bitwise_xor(me % 4, 2 * ry + rx)
            fetch(piece.at[i], table_ref[other * slots + slot])

    @pl.loop(0, where_ref[1])
    def _(i):
        fetch(extra_ref.at[i], table_ref[devices * slots + i])


def wait_units(stack, total, sem):
    while total > 0:
        step = min(stack.shape[0], total)
        pltpu.make_async_copy(stack.at[0:step], stack.at[0:step], sem).wait()
        total -= step


def put_units(dest_ref, first_unit, stage, own_ref, stray_ref, sem):
    for i, unit in enumerate(first_unit):
        dest = dest_ref[unit]

        @pl.when(dest >= 0)
        def _():
            pltpu.make_async_copy(stage.at[i], own_ref.at[dest], sem).start()

        @pl.when(dest < 0)
        def _():
            pltpu.make_async_copy(stage.at[i], stray_ref.at[-1 - dest, :UROWS], sem).start()


def toeplitz(row):
    width = SPREAD
    tile = jnp.broadcast_to(pltpu.roll(row, width - (SLOT - 1), 1), (8, width))
    places = lax.broadcasted_iota(jnp.int32, (8, width), 0)
    for bit in (1, 2, 4):
        tile = jnp.where(jnp.bitwise_and(places, bit) != 0, pltpu.roll(tile, bit, 1), tile)
    reach = 8
    while reach < SLOT // 2:
        tile = jnp.concatenate([tile, pltpu.roll(tile, reach, 1)], axis=0)
        reach *= 2
    lower = jnp.concatenate([tile[:, width - reach :], tile[:, : SLOT - reach]], axis=1)
    return jnp.concatenate([tile[:, :SLOT], lower], axis=0)


def diagonals(tile):
    rows = SLOT
    while rows > 128:
        rows //= 2
        blank = jnp.zeros((rows, rows), F32)
        tile = jnp.concatenate([tile[rows:], blank], axis=1) + jnp.concatenate(
            [blank, tile[:rows]], axis=1
        )
    tile = jnp.concatenate([tile, jnp.zeros((rows, SPREAD - tile.shape[1]), F32)], axis=1)
    while rows > 8:
        rows //= 2
        tile = tile[rows:] + pltpu.roll(tile[:rows], rows, 1)
    places = lax.broadcasted_iota(jnp.int32, tile.shape, 0)
    for bit in (4, 2, 1):
        tile = jnp.where(jnp.bitwise_and(places, bit) == 0, pltpu.roll(tile, bit, 1), tile)
    return jnp.sum(tile, axis=0, keepdims=True)


def matrix(ref, first):
    return ref[first : first + ROWS].reshape(D, ref.shape[2])


def pair_columns(ref, step):
    return ref[:, pl.ds(pl.multiple_of(step * PAIR, PAIR), PAIR)]


def attend_kernel(own, devices, layout, lengths_ref, where_ref, table_ref, tokens_ref, gain_ref, bias_ref, extra_ref, *refs):
    pieces = refs[: len(layout)]
    norm_ref, query_ref, key_ref, value_ref, prob_ref, mixed_ref, front_ref, rest_ref = refs[len(layout) : -5]
    stack, front_sem, rest_sem, front_out, rest_out = refs[-5:]
    step = pl.program_id(0)
    front_copy = pltpu.make_async_copy(stack.at[:FRONT], front_ref, front_out)
    rest_copy = pltpu.make_async_copy(stack.at[FRONT:], rest_ref, rest_out)

    @pl.when(step == 0)
    def _():
        gather_units(
            own, devices, layout, where_ref, table_ref, pieces, extra_ref, stack, front_sem, rest_sem
        )
        inputs = tokens_ref[...].astype(F32)
        normed = (inputs * inverse_rms(inputs) * gain_ref[0:1, :]).astype(BF16)
        norm_ref[...] = normed
        wait_units(stack, FRONT, front_sem)
        front_copy.start()
        query_ref[...] = dot(normed, matrix(stack, 0)).astype(BF16)
        key_ref[...] = dot(normed, matrix(stack, ROWS)).astype(BF16)
        value_ref[...] = dot(normed, matrix(stack, 2 * ROWS)).astype(BF16)
        wait_units(stack, devices * own - FRONT, rest_sem)

        @pl.loop(0, where_ref[1])
        def _(i):
            wait_units(stack, 1, rest_sem)

        rest_copy.start()

    @pl.when(step == pl.num_programs(0) - 1)
    def _():
        front_copy.wait()
        rest_copy.wait()

    queries = pair_columns(query_ref, step)
    keys = pair_columns(key_ref, step)
    values = pair_columns(value_ref, step)
    lanes = lax.broadcasted_iota(jnp.int32, (SLOT, PAIR), 1) // HEAD_DIM
    seen = lax.broadcasted_iota(jnp.int32, (1, SLOT), 1) < lengths_ref[0]
    mixes = []
    for which in range(2):
        scores = dot_nt(jnp.where(lanes == which, queries, jnp.zeros_like(queries)), keys)
        scores = scores + toeplitz(bias_ref[pl.ds(2 * step + which, 1), :])
        scores = jnp.where(seen, scores, MASKED)
        powers = jnp.exp(scores - jnp.max(scores, axis=-1, keepdims=True))
        probabilities = powers * (1.0 / jnp.sum(powers, axis=-1, keepdims=True))
        prob_ref[which] = probabilities
        mixes.append(dot(probabilities.astype(BF16), values))
    mixed = jnp.where(lanes == 0, mixes[0], mixes[1]).astype(BF16)
    mixed_ref[:, pl.ds(pl.multiple_of(step * PAIR, PAIR), PAIR)] = mixed


def out_kernel(own, devices, where_ref, table_ref, mixed_ref, rest_in, *refs):
    line = devices // 4
    *pieces, part_ref, rest_ref, stage, weight, stage_sem, weight_sem, put_sem = refs
    me = where_ref[0]
    load = pltpu.make_async_copy(rest_in.at[0:ROWS], weight, weight_sem)
    load.start()
    for rz in range(line):
        pltpu.make_async_copy(pieces[rz], stage.at[4 * rz : 4 * rz + 4], stage_sem).start()
    load.wait()
    pltpu.make_async_copy(stage, stage, stage_sem).wait()
    for rz in range(line):
        z = ring_device((ring_place(me // 4, line) - rz + line) % line, line)
        for near in range(4):
            other = z * 4 + jnp.bitwise_xor(me % 4, near)
            place = table_ref[other * (own + 1) + own] - FRONT
            i = 4 * rz + near
            pltpu.make_async_copy(stage.at[i], rest_ref.at[place], put_sem).start()

            @pl.when(place < ROWS)
            def _():
                weight[place] = stage[i]

    part_ref[...] = dot_nt(mixed_ref[...], matrix(weight, 0))
    pltpu.make_async_copy(stage, stage, put_sem).wait()


def gelu_tanh(values):
    return jnp.tanh(GELU_C * (values + GELU_K * values * values * values))


def feed_kernel(
    tokens_ref, mine_ref, other_ref, gain_ref, gate_w, up_w, down_w,
    residual_ref, norm_ref, gate_ref, up_ref, hidden_ref, part_ref,
):
    step = pl.program_id(0)

    @pl.when(step == 0)
    def _():
        residual = tokens_ref[...].astype(F32) + (mine_ref[...] + other_ref[...])
        residual_ref[...] = residual
        norm_ref[...] = (residual * inverse_rms(residual) * gain_ref[1:2, :]).astype(BF16)
        part_ref[...] = jnp.zeros_like(part_ref)

    normed = norm_ref[...]
    gate = dot(normed, matrix(gate_w, 0))
    up = dot(normed, matrix(up_w, 0))
    gate_ref[...] = gate
    up_ref[...] = up
    hidden = (0.5 * gate * (1.0 + gelu_tanh(gate)) * up).astype(BF16)
    hidden_ref[...] = hidden
    part_ref[...] += dot_nt(hidden, matrix(down_w, 0))


def turn_kernel(
    lengths_ref, residual_ref, mine_ref, other_ref, gain_ref, proj_ref, proj_other, cot_ref, cot_other,
    gate_ref, up_ref, gate_w, up_w, down_w,
    encoded_ref, proj_grad, gain_grad, grad_ref, feed_ref, dgate_ref, dup_ref, part_ref,
):
    step = pl.program_id(0)

    @pl.when(step == 0)
    def _():
        residual = residual_ref[...] + (mine_ref[...] + other_ref[...])
        inv_rms = inverse_rms(residual)
        normed = (residual * inv_rms * gain_ref[2:3, :]).astype(BF16)
        encoded_ref[...] = dot(normed, proj_ref[...])
        rows = lax.broadcasted_iota(jnp.int32, (SLOT, 1), 0) < lengths_ref[0]
        mine = jnp.where(rows, cot_ref[...], jnp.zeros_like(cot_ref))
        other = jnp.where(rows, cot_other[...], jnp.zeros_like(cot_other))
        backward = dot_tn(mine, normed)
        proj_grad[0] = backward[:, : D // 2]
        proj_grad[1] = backward[:, D // 2 :]
        third = dot_nt(mine, proj_ref[...]) + dot_nt(other, proj_other[...])
        grad, gain = norm_back(residual, inv_rms, gain_ref[2:3, :], third)
        gain_grad[...] = gain
        grad_ref[...] = grad
        feed_ref[...] = grad.astype(BF16)
        part_ref[...] = jnp.zeros_like(part_ref)

    dhidden = dot(feed_ref[...], matrix(down_w, 0))
    gate = gate_ref[...]
    bend = gelu_tanh(gate)
    slope = 0.5 * (1.0 + bend) + 0.5 * gate * (1.0 - bend * bend) * (
        GELU_C * (1.0 + 3.0 * GELU_K * gate * gate)
    )
    dgate = (dhidden * up_ref[...] * slope).astype(BF16)
    dup = (dhidden * (0.5 * gate * (1.0 + bend))).astype(BF16)
    dgate_ref[...] = dgate
    dup_ref[...] = dup
    part_ref[...] += dot_nt(dgate, matrix(gate_w, 0)) + dot_nt(dup, matrix(up_w, 0))


def wide_grads_kernel(
    units, dest_ref, norm_ref, feed_ref, hidden_ref, dgate_ref, dup_ref, own_ref, stray_ref, stage, sems
):
    step = pl.program_id(0)
    slot = step % 2
    shape = (ROWS,) + stage.shape[2:]

    def settle(which):
        pltpu.make_async_copy(stage.at[which], stage.at[which], sems.at[which]).wait()

    @pl.when(step >= 2)
    def _():
        settle(slot)

    normed = norm_ref[...]
    stage[slot, 0:ROWS] = dot_tn(normed, dgate_ref[...]).astype(BF16).reshape(shape)
    stage[slot, ROWS : 2 * ROWS] = dot_tn(normed, dup_ref[...]).astype(BF16).reshape(shape)
    stage[slot, 2 * ROWS :] = dot_tn(feed_ref[...], hidden_ref[...]).astype(BF16).reshape(shape)
    names = [
        SQUARES + which * ROWS * BLOCKS + row * BLOCKS + step for which in range(3) for row in range(ROWS)
    ]
    put_units(dest_ref, names, stage.at[slot], own_ref, stray_ref, sems.at[slot])

    @pl.when(step == pl.num_programs(0) - 1)
    def _():
        settle(1 - slot)
        settle(slot)


def enter_back_kernel(
    dest_ref, home_ref, grad_ref, residual_ref, mine_ref, other_ref, gain_ref, weight_ref, mixed_ref,
    proj_ref, own_in, stray_in,
    grad_one, gain_grad, dmixed_ref, own_ref, stray_ref, stage, sem, proj_sem,
):
    for home in range(proj_ref.shape[0]):
        pltpu.make_async_copy(
            proj_ref.at[home], stray_ref.at[home_ref[home], UROWS:], proj_sem
        ).start()
    residual = residual_ref[...]
    second = mine_ref[...] + other_ref[...]
    back, gain = norm_back(residual, inverse_rms(residual), gain_ref[1:2, :], second)
    gain_grad[...] = gain
    total = grad_ref[...] + back
    grad_one[...] = total
    lowered = total.astype(BF16)
    stage[...] = dot_tn(lowered, mixed_ref[...]).astype(BF16).reshape(stage.shape)
    put_units(dest_ref, range(FRONT, SQUARES), stage, own_ref, stray_ref, sem)
    dmixed_ref[...] = dot(lowered, matrix(weight_ref, 0)).astype(BF16)
    pltpu.make_async_copy(stage, stage, sem).wait()
    pltpu.make_async_copy(proj_ref, proj_ref, proj_sem).wait()


def attend_back_kernel(
    dmixed_ref, query_ref, key_ref, value_ref, prob_ref, dquery_ref, dkey_ref, dvalue_ref, offset_ref
):
    queries, keys, values, dmixed = query_ref[...], key_ref[...], value_ref[...], dmixed_ref[...]
    lanes = lax.broadcasted_iota(jnp.int32, (SLOT, PAIR), 1) // HEAD_DIM
    parts = []
    for which in range(2):
        dprob = dot_nt(jnp.where(lanes == which, dmixed, jnp.zeros_like(dmixed)), values)
        probabilities = prob_ref[which]
        share = jnp.sum(probabilities * dprob, axis=-1, keepdims=True)
        dscore = (probabilities * (dprob - share)).astype(BF16)
        parts.append(
            (
                dot(dscore, keys),
                dot_tn(dscore, queries),
                dot_tn(probabilities.astype(BF16), dmixed),
            )
        )
        offset_ref[0, which : which + 1, :] = diagonals(dscore.astype(F32))
    for out, first, second in zip((dquery_ref, dkey_ref, dvalue_ref), *parts):
        out[...] = jnp.where(lanes == 0, first, second).astype(BF16)


def joined(refs):
    return jnp.concatenate([ref[...] for ref in refs], axis=1)


def first_grad_kernel(weight_ref, *refs):
    *parts, out_ref = refs
    width = len(parts) // 3
    total = 0.0
    for i in range(3):
        total = total + dot_nt(joined(parts[i * width : (i + 1) * width]), matrix(weight_ref, i * ROWS))
    out_ref[...] = total.astype(BF16)


def front_grads_kernel(dest_ref, norm_ref, *refs):
    *parts, own_in, own_ref, stage, sem = refs
    width = len(parts) // 3
    normed = norm_ref[...]
    shape = (ROWS,) + stage.shape[1:]
    for i in range(3):
        first = i * ROWS
        grads = joined(parts[i * width : (i + 1) * width])
        stage[first : first + ROWS] = dot_tn(normed, grads).astype(BF16).reshape(shape)
        for unit in range(first, first + ROWS):
            pltpu.make_async_copy(stage.at[unit], own_ref.at[dest_ref[unit]], sem).start()
    pltpu.make_async_copy(stage, stage, sem).wait()


def token_grad_kernel(tokens_ref, grad_ref, mine_ref, other_ref, gain_ref, out_ref, gain_grad):
    inputs = tokens_ref[...].astype(F32)
    first = mine_ref[...].astype(F32) + other_ref[...].astype(F32)
    back, gain = norm_back(inputs, inverse_rms(inputs), gain_ref[0:1, :], first)
    out_ref[...] = grad_ref[...] + back
    gain_grad[...] = gain


def order_rows_kernel(devices, where_ref, *refs):
    line = devices // 4
    *found, out_ref = refs
    me = where_ref[0]
    for rz in range(line):
        z = ring_device((ring_place(me // 4, line) - rz + line) % line, line)
        for near in range(4):
            other = z * 4 + jnp.bitwise_xor(me % 4, near)
            out_ref[other] = found[rz][near].astype(F32)


def stray_update_kernel(pick_ref, weight, first, second, stray, extra, *refs):
    kind = pick_ref[pl.program_id(0)]
    grad = jnp.where(kind == 1, stray[0].astype(F32), extra[0].astype(F32))
    grad = jnp.where(kind == 0, 0.0, grad)
    update_slot(weight, first, second, grad, refs[-4:])


def update_slot(weight, first, second, grad, outs):
    new_weight, new_first, new_second = adamw_step(
        weight[0], first[0], second[0], grad, RATE_MATRIX
    )
    outs[0][0] = new_weight
    outs[1][0] = new_first
    outs[2][0] = new_second
    outs[3][0] = new_weight.astype(BF16)


def own_update_kernel(count_ref, weight, first, second, grad_ref, *refs):
    grad = jnp.where(pl.program_id(0) < count_ref[0], grad_ref[0], 0.0)
    update_slot(weight, first, second, grad, refs[-4:])


def shards(
    tokens,
    out_grad,
    doc_lengths,
    owner_list,
    bucket_table,
    unit_weight,
    unit_first,
    unit_second,
    gain_weight,
    gain_first,
    gain_second,
    bias_weight,
    bias_first,
    bias_second,
    proj_weight,
    proj_first,
    proj_second,
):
    most, _, width = unit_weight.shape
    heads = bias_weight.shape[1]
    count = tokens.shape[0]
    units = owner_list.shape[0]
    proj_width = proj_weight.shape[1]
    devices = lax.axis_size("dp")
    line = devices // 4
    own = max(1, (units - 1) // devices)
    slots = own + 1
    spare = most - own
    me = lax.axis_index("dp").astype(jnp.int32)

    def like(shape, kind=F32):
        return jax.ShapeDtypeStruct(shape, kind)

    full, left = divmod(units, most)
    extra_count = max(FRONT, full * spare + max(0, left - own) - devices)
    indices = jnp.arange(units, dtype=jnp.int32)
    before = indices[None, :] < indices[:, None]
    same = owner_list[:, None] == owner_list[None, :]
    rank = jnp.sum((same & before).astype(jnp.int32), axis=1)
    is_over = rank >= own
    may_stray = is_over & (indices >= FRONT)
    stray_index = jnp.sum((before & may_stray[None, :]).astype(jnp.int32), axis=1)
    is_stray = may_stray & (stray_index < devices)
    is_extra = is_over & ~is_stray
    extra_index = jnp.sum((before & is_extra[None, :]).astype(jnp.int32), axis=1)
    extra_total = jnp.sum(is_extra.astype(jnp.int32))
    many = extra_total > 0
    position = jnp.where(
        is_stray,
        stray_index * slots + own,
        jnp.where(is_extra, devices * slots + extra_index, owner_list * slots + rank),
    )
    position_ids = jnp.arange(devices * slots + extra_count, dtype=jnp.int32)
    hit = position[None, :] == position_ids[:, None]
    placed = jnp.where(indices < FRONT, indices, FRONT + rest_place(indices))
    table = units + jnp.sum(jnp.where(hit, placed[None, :] - units, 0), axis=1).astype(jnp.int32)
    spare_ids = jnp.arange(spare, dtype=jnp.int32)
    my_over = (owner_list[None, :] == me) & (rank[None, :] == own + spare_ids[:, None])
    my_stray = jnp.sum(jnp.where(my_over & is_stray[None, :], stray_index[None, :] + 1, 0), axis=1) - 1
    my_extra = jnp.sum(jnp.where(my_over & is_extra[None, :], extra_index[None, :] + 1, 0), axis=1) - 1
    my_count = jnp.sum((owner_list == me).astype(jnp.int32)).reshape(1)
    where = jnp.stack([me, extra_total]).astype(jnp.int32)

    home = jnp.where(is_stray, stray_index, owner_list)
    rel_x = jnp.bitwise_and(jnp.bitwise_xor(home, me), 1)
    rel_y = jnp.bitwise_and(jnp.bitwise_xor(home, me) // 2, 1)
    rel_z = (ring_place(home // 4, line) - ring_place(me // 4, line) + line) % line
    cut = (own + 1) // 2
    spans = [(0, cut), (cut, own)] if own > cut else [(0, cut)]
    even = rel_z % 2 == 0
    in_first = rank < cut
    near_is_x = even == in_first
    corner = jnp.where(near_is_x, rel_x, rel_y) * 2 + jnp.where(near_is_x, rel_y, rel_x)
    own_dest = rel_z * 4 * own + jnp.where(
        in_first, corner * cut + rank, 4 * cut + corner * (own - cut) + rank - cut
    )

    def stray_dest_of(x, y, z):
        even = z % 2 == 0
        corner = jnp.where(even, x, y) * 2 + jnp.where(even, y, x)
        return (jnp.where(even, 0, 2 * line) + corner * (line // 2) + z // 2).astype(jnp.int32)

    stray_dest = stray_dest_of(rel_x, rel_y, rel_z)
    homes = jnp.arange(devices, dtype=jnp.int32)
    home_dest = stray_dest_of(
        jnp.bitwise_and(jnp.bitwise_xor(homes, me), 1),
        jnp.bitwise_and(jnp.bitwise_xor(homes, me) // 2, 1),
        (ring_place(homes // 4, line) - ring_place(me // 4, line) + line) % line,
    )
    dest = jnp.where(
        is_stray,
        -1 - stray_dest,
        jnp.where(is_extra, 4 * line * own + extra_index, own_dest),
    ).astype(jnp.int32)

    extra_shape = (extra_count, UROWS, width)

    def extra_weights():
        wanted = jnp.arange(extra_count, dtype=jnp.int32)[:, None] == my_extra[None, :]
        taken = jnp.take(unit_weight[own:], jnp.argmax(wanted, axis=1), axis=0)
        return lax.psum(jnp.where(jnp.any(wanted, axis=1)[:, None, None], taken, 0.0), "dp").astype(BF16)

    def no_extra():
        return jnp.zeros(extra_shape, BF16)

    extra = lax.cond(many, extra_weights, no_extra)

    def sum_strays(links, keep_a, send_a, keep_b, send_b):
        from_x = links.send(send_a, ALONG_X)
        from_y = links.send(send_b, ALONG_Y)
        yield
        from_x, from_y = links.settle(from_x), links.settle(from_y)
        low_y = links.send((keep_a[1].astype(F32) + from_x[1].astype(F32)).astype(BF16), ALONG_Y)
        high_x = links.send((keep_b[1].astype(F32) + from_y[1].astype(F32)).astype(BF16), ALONG_X)
        yield
        low_y, high_x = links.settle(low_y), links.settle(high_x)
        low = keep_a[0].astype(F32) + from_x[0].astype(F32) + low_y.astype(F32)
        high = keep_b[0].astype(F32) + from_y[0].astype(F32) + high_x.astype(F32)
        sums = [(high if rz % 2 else low)[rz // 2] for rz in range(line)]
        total = sums[0]
        terms = [links.send(sums[rz].astype(BF16), ALONG_Z, rz) for rz in range(1, line)]
        yield
        for term in terms:
            total = total + links.settle(term).astype(F32)
        return total.astype(BF16)

    def gather_strays(links, unit):
        got = links.send(unit, ALONG_X)
        yield
        near = jnp.stack([unit, links.settle(got)])
        got = links.send(near, ALONG_Y)
        yield
        near = jnp.concatenate([near, links.settle(got)])
        found = [near]
        for _ in range(line - 1):
            found.append(links.send(found[-1], ALONG_Z))
            yield
            found[-1] = links.settle(found[-1])
        return found

    def stray_chain(links, *arrays):
        unit = yield from sum_strays(links, *arrays)
        return (yield from gather_strays(links, unit))

    class Chain:
        def __init__(self, links, steps):
            self.links, self.steps, self.value = links, steps, None

        def step(self, gate=None):
            self.links.gate = gate
            try:
                if self.value is None:
                    next(self.steps)
            except StopIteration as end:
                self.value = end.value

        def finish(self):
            while self.value is None:
                self.step()
            return self.value

    proj_low = proj_weight.astype(BF16)
    proj_other = swap(proj_low)
    cot_other = swap(out_grad)

    links = Links(devices, *WINDOWS)
    rings = [[unit_weight[first:last].astype(BF16)] for first, last in spans]
    pieces, layout, rounds = [], [], {}

    def ring_step():
        for ring in rings:
            ring.append(links.send(ring[-1], ALONG_Z))

    def keep(values, rx, ry, spots):
        pieces.append(values)
        layout.append([(rx, ry, rz, slot) for rz, slot in spots])

    def near_round(pair):
        for i, axis in enumerate((ALONG_X, ALONG_Y)):
            parts, spots = [], []
            for rz in (2 * pair, 2 * pair + 1):
                which = (i + rz) % 2
                if which < len(rings):
                    parts.append(rings[which][rz])
                    spots += [(rz, slot) for slot in range(*spans[which])]
            if parts:
                values = jnp.concatenate(parts) if len(parts) > 1 else parts[0]
                rounds[pair, axis] = values, spots, links.send(values, axis)

    def far_direct(pair):
        for axis in (ALONG_X, ALONG_Y):
            if (pair, axis) in rounds:
                values, spots, got = rounds[pair, axis]
                other = ALONG_X + ALONG_Y - axis
                keep(values, 0, 0, spots)
                keep(got, int(axis == ALONG_X), int(axis == ALONG_Y), spots)
                keep(links.send(values, other), int(axis == ALONG_Y), int(axis == ALONG_X), spots)

    def far_through(pair):
        for axis in (ALONG_X, ALONG_Y):
            if (pair, axis) in rounds:
                values, spots, got = rounds[pair, axis]
                keep(links.send(got, ALONG_X + ALONG_Y - axis), 1, 1, spots)

    ring_step()
    near_shape = like((2, line // 2, UROWS, width), BF16)
    stray_parts = pl.pallas_call(
        functools.partial(strays_kernel, own, most, devices),
        out_shape=[near_shape] * 4,
        in_specs=[SMEM, SMEM, ANY],
        out_specs=[VMEM] * 4,
        scratch_shapes=[pltpu.VMEM((spare, UROWS, width), F32), pltpu.SemaphoreType.DMA],
        compiler_params=params(40),
        cost_estimate=timed(2),
    )(where, my_stray, unit_weight)
    strays = Chain(links, stray_chain(links, *stray_parts))
    strays.step()
    for pair in range(line // 2):
        while len(rings[0]) < 2 * pair + 2:
            ring_step()
        near_round(pair)
        if pair == 0:
            strays.step(rings[0][-1])
            first_near = links.sent[ALONG_Y][1]
            while len(rings[0]) < min(line, 3):
                ring_step()
            far_direct(pair)
            strays.step(first_near)
            if len(rings[0]) < line:
                ring_step()
            strays.step(links.sent[ALONG_X][-1])
            far_through(pair)
            strays.step(links.sent[ALONG_X][-2])
        else:
            strays.step(links.sent[ALONG_Y][-3])
            far_direct(pair)
            strays.step(links.sent[ALONG_Y][-3])
            far_through(pair)
    found = strays.finish()
    tokens, proj_other, cot_other = lax.optimization_barrier((tokens, proj_other, cot_other))

    bucket_hot = (bucket_table[:, None] == jnp.arange(BUCKETS, dtype=jnp.int32)[None, :]).astype(F32)
    bucket_hot = jnp.pad(bucket_hot, ((0, SPREAD - bucket_hot.shape[0]), (0, 0)))
    bias_rows = jnp.pad(precise_dot(bucket_hot, bias_weight).T, ((0, 8 - heads % 8), (0, 0)))
    def whole(shape):
        return pl.BlockSpec(shape, lambda i: (0,) * len(shape))

    wide_shape = (count, D)
    head_shape = (count, width)
    front_spec = whole((FRONT, UROWS, width))
    out_spec = pl.BlockSpec((ROWS, UROWS, width), lambda i: (0, 0, 0))
    prob_spec = pl.BlockSpec((2, SLOT, SLOT), lambda i: (i, 0, 0))
    gain_spec = whole((3, D))
    bias_spec = whole(bias_rows.shape)
    column_spec = pl.BlockSpec((count, width), lambda i: (0, i))

    def unit_spec(which):
        return pl.BlockSpec((ROWS, UROWS, width), lambda i: (1 + which * BLOCKS + i, 0, 0))

    wide_specs = [unit_spec(0), unit_spec(1), unit_spec(2)]

    stack_shape = (units + 1, UROWS, width)
    rest_shape = like((units + 1 - FRONT, UROWS, width), BF16)
    first_in, queries, keys, values, probabilities, mixed, front, rest = pl.pallas_call(
        functools.partial(attend_kernel, own, devices, layout),
        grid=(heads // 2,),
        in_specs=[SMEM] * 3 + [whole(wide_shape), gain_spec, bias_spec] + [ANY] * (1 + len(pieces)),
        out_specs=[whole(wide_shape)] + [whole(head_shape)] * 3 + [prob_spec, whole(head_shape), HBM, HBM],
        out_shape=[like(wide_shape, BF16)]
        + [like(head_shape, BF16)] * 3
        + [like((heads, SLOT, SLOT)), like(head_shape, BF16), like((FRONT, UROWS, width), BF16), rest_shape],
        scratch_shapes=[pltpu.VMEM(stack_shape, BF16)] + [pltpu.SemaphoreType.DMA] * 4,
        compiler_params=params(60),
        cost_estimate=timed(14),
    )(doc_lengths, where, table, tokens, gain_weight, bias_rows, extra, *pieces)
    attn_part, rest = pl.pallas_call(
        functools.partial(out_kernel, own, devices),
        grid=(1,),
        in_specs=[SMEM] * 2 + [whole(head_shape)] + [ANY] * (1 + line),
        out_specs=[whole(wide_shape), HBM],
        out_shape=[like(wide_shape), rest_shape],
        input_output_aliases={3: 1},
        scratch_shapes=[
            pltpu.VMEM((4 * line, UROWS, width), BF16),
            pltpu.VMEM((ROWS, UROWS, width), BF16),
        ]
        + [pltpu.SemaphoreType.DMA] * 3,
        compiler_params=params(56),
        cost_estimate=timed(4),
    )(where, table, mixed, rest, *found)

    residual_one, second_in, gate, up, hidden, feed_part = pl.pallas_call(
        feed_kernel,
        grid=(BLOCKS,),
        in_specs=[whole(wide_shape)] * 3 + [gain_spec] + wide_specs,
        out_specs=[whole(wide_shape)] * 2 + [column_spec] * 3 + [whole(wide_shape)],
        out_shape=[
            like(wide_shape),
            like(wide_shape, BF16),
            like((count, BLOCKS * width)),
            like((count, BLOCKS * width)),
            like((count, BLOCKS * width), BF16),
            like(wide_shape),
        ],
        compiler_params=params(56),
        cost_estimate=timed(11),
    )(tokens, attn_part, swap(attn_part), gain_weight, rest, rest, rest)

    encoded, proj_grad, gain_three, grad_two, feed_grad, dgate, dup, second_part = pl.pallas_call(
        turn_kernel,
        grid=(BLOCKS,),
        in_specs=[SMEM]
        + [whole(wide_shape)] * 3
        + [gain_spec]
        + [whole((D, proj_width))] * 2
        + [whole((count, proj_width))] * 2
        + [column_spec] * 2
        + wide_specs,
        out_specs=[
            whole((count, proj_width)),
            whole((2, proj_width, D // 2)),
            whole((1, D)),
            whole(wide_shape),
            whole(wide_shape),
            column_spec,
            column_spec,
            whole(wide_shape),
        ],
        out_shape=[
            like((count, proj_width)),
            like((2, proj_width, D // 2)),
            like((1, D)),
            like(wide_shape),
            like(wide_shape, BF16),
            like((count, BLOCKS * width), BF16),
            like((count, BLOCKS * width), BF16),
            like(wide_shape),
        ],
        compiler_params=params(56),
        cost_estimate=timed(14),
    )(
        doc_lengths, residual_one, feed_part, swap(feed_part), gain_weight, proj_low, proj_other,
        out_grad, cot_other, gate, up, rest, rest, rest,
    )

    own_shape = like((4 * line * own + extra_count, UROWS, width), BF16)
    stray_shape = like((4 * line, UROWS + STRAY_TILE, width), BF16)
    proj_rows = proj_grad.reshape(-1, width)
    share = -(-proj_rows.shape[0] // devices)
    proj_rows = jnp.pad(proj_rows, ((0, share * devices - proj_rows.shape[0]), (0, 0)))
    proj_rows = proj_rows.reshape(devices, share, width).astype(BF16)
    proj_rows = jnp.pad(proj_rows, ((0, 0), (0, STRAY_TILE - share), (0, 0)))
    own_units, stray_units = pl.pallas_call(
        functools.partial(wide_grads_kernel, units),
        grid=(BLOCKS,),
        in_specs=[SMEM] + [whole(wide_shape)] * 2 + [column_spec] * 3,
        out_specs=[HBM] * 2,
        out_shape=[own_shape, stray_shape],
        scratch_shapes=[
            pltpu.VMEM((2, 3 * ROWS, UROWS, width), BF16),
            pltpu.SemaphoreType.DMA((2,)),
        ],
        compiler_params=params(56),
        cost_estimate=timed(9),
    )(dest, second_in, feed_grad, hidden, dgate, dup)

    grad_one, gain_two, dmixed, own_units, stray_units = pl.pallas_call(
        enter_back_kernel,
        grid=(1,),
        in_specs=[SMEM] * 2
        + [whole(wide_shape)] * 4
        + [gain_spec, out_spec, whole(head_shape), whole(proj_rows.shape)]
        + [ANY] * 2,
        out_specs=[whole(wide_shape), whole((1, D)), whole(head_shape)] + [HBM] * 2,
        out_shape=[like(wide_shape), like((1, D)), like(head_shape, BF16), own_shape, stray_shape],
        input_output_aliases={10: 3, 11: 4},
        scratch_shapes=[pltpu.VMEM((ROWS, UROWS, width), BF16)] + [pltpu.SemaphoreType.DMA] * 2,
        compiler_params=params(56),
        cost_estimate=timed(6),
    )(
        dest, home_dest, grad_two, residual_one, second_part, swap(second_part), gain_weight, rest, mixed,
        proj_rows, own_units, stray_units,
    )

    links = Links(devices, *BACK_WINDOWS)
    by_near = stray_units.reshape(4, 2, line // 2, UROWS + STRAY_TILE, width)
    strays = Chain(links, stray_chain(links, *[by_near[i] for i in range(4)]))

    def attend_back(first, pairs, dmixed):
        pair_spec = pl.BlockSpec((count, PAIR), lambda i: (0, first + i))
        out_spec = pl.BlockSpec((count, PAIR), lambda i: (0, i))
        return pl.pallas_call(
            attend_back_kernel,
            grid=(pairs,),
            in_specs=[pair_spec] * 4 + [pl.BlockSpec((2, SLOT, SLOT), lambda i: (first + i, 0, 0))],
            out_specs=[out_spec] * 3 + [pl.BlockSpec((1, 8, SPREAD), lambda i: (i, 0, 0))],
            out_shape=[like((count, PAIR * pairs), BF16)] * 3 + [like((pairs, 8, SPREAD))],
            compiler_params=params(56),
            cost_estimate=timed(4.3 * pairs),
        )(dmixed, queries, keys, values, probabilities)

    pairs = heads // 2
    strays.step()
    *grads_a, offsets_a = attend_back(0, pairs - 1, dmixed)
    strays.step()
    *grads_b, offsets_b = attend_back(pairs - 1, 1, after(dmixed, links.sent[ALONG_Y][0]))
    head_grads = [part for both in zip(grads_a, grads_b) for part in both]
    offset_grad = jnp.concatenate([offsets_a, offsets_b])[:, :2].reshape(heads, SPREAD)
    part_specs = [whole(part.shape) for part in head_grads]
    first_part = pl.pallas_call(
        first_grad_kernel,
        grid=(1,),
        in_specs=[front_spec] + part_specs,
        out_specs=whole(wide_shape),
        out_shape=like(wide_shape, BF16),
        compiler_params=params(56),
        cost_estimate=timed(2),
    )(front, *head_grads)

    own_units = pl.pallas_call(
        front_grads_kernel,
        grid=(1,),
        in_specs=[SMEM, whole(wide_shape)] + part_specs + [ANY],
        out_specs=HBM,
        out_shape=own_shape,
        input_output_aliases={2 + len(head_grads): 0},
        scratch_shapes=[pltpu.VMEM((FRONT, UROWS, width), BF16), pltpu.SemaphoreType.DMA],
        compiler_params=params(56),
        cost_estimate=timed(4),
    )(dest, first_in, *head_grads, own_units)

    token_grad, gain_one = pl.pallas_call(
        token_grad_kernel,
        out_shape=[like(wide_shape), like((1, D))],
        compiler_params=params(56),
        cost_estimate=timed(4),
    )(tokens, grad_one, first_part, swap(first_part), gain_weight)

    def total_of(links, values):
        got = links.send(values, ALONG_X)
        yield
        values = values + links.settle(got)
        got = links.send(values, ALONG_Y)
        yield
        values = values + links.settle(got)
        terms = [values] + [links.send(values, ALONG_Z, rz) for rz in range(1, line)]
        yield
        terms = [links.settle(term) for term in terms]
        while len(terms) > 1:
            middle = len(terms) // 2
            terms = [terms[i] + terms[middle + i] for i in range(middle)]
        return terms[0]

    halves = {}

    def near_sums(rz):
        first = 4 * rz * own
        for group, span in enumerate(spans):
            size = span[1] - span[0]
            axis = (ALONG_X, ALONG_Y)[(group + rz) % 2]
            shape = (2, size, UROWS, width)
            kept = own_units[first : first + 2 * size].reshape(shape)
            given = own_units[first + 2 * size : first + 4 * size].reshape(shape)
            halves[rz, group] = axis, kept, links.send(given, axis)
            first += 4 * size

    def far_sums(rz):
        sums = []
        for group in range(len(spans)):
            axis, kept, got = halves[rz, group]
            onward = (kept[1].astype(F32) + got[1].astype(F32)).astype(BF16)
            passed = links.send(onward, ALONG_X + ALONG_Y - axis)
            sums.append(kept[0].astype(F32) + got[0].astype(F32) + passed.astype(F32))
        return jnp.concatenate(sums)

    def ring_sum(value, moving):
        if moving is None:
            return value
        return value + links.send(moving.astype(BF16), ALONG_Z).astype(F32)

    bias_grad = precise_dot(bucket_hot.T, offset_grad.T)
    gain_rows = jnp.concatenate([gain_one, gain_two, gain_three]).reshape(-1, width)
    bias_row = jnp.pad(bias_grad.reshape(1, -1), ((0, 0), (0, width - BUCKETS * heads)))
    small_links = Links(devices)
    small = Chain(small_links, total_of(small_links, jnp.concatenate([gain_rows, bias_row])))

    moving = None
    events = []

    def event(rz=None):
        events.append(links.sent[ALONG_X][-1])

    near_sums(line - 1)
    event()
    strays.step()
    for rz in range(line - 2, -1, -1):
        near_sums(rz)
        event()
        if rz == line - 2:
            strays.step(events[-2])
        else:
            strays.step(events[-3])
            small.step(events[-3])
        value = far_sums(rz + 1)
        event()
        if rz == line - 2:
            strays.step(events[-2])
        strays.step(events[-2])
        moving = ring_sum(value, moving)
    value = far_sums(0)
    event()
    small.step(events[-2])
    strays.step(events[-2])
    own_grads = ring_sum(value, moving)
    links.gate = small_links.gate = events[-1]
    while small.value is None:
        small.step(events[-1])
    small_total = small.value
    while strays.value is None:
        strays.step(events[-1])
    stray_found = strays.value

    def extra_grads():
        return lax.psum(own_units[4 * line * own :].astype(F32), "dp").astype(BF16)

    extra_grad = lax.cond(many, extra_grads, no_extra)

    stray_place = (ring_place(me // 4, line) - ring_place(my_stray // 4, line) + line) % line
    stray_place = stray_place * 4 + jnp.bitwise_xor(my_stray % 4, me % 4)
    picks = jnp.concatenate(
        [
            jnp.where(my_stray >= 0, 1, jnp.where(my_extra >= 0, 2, 0)),
            jnp.where(my_stray >= 0, stray_place, 0),
            jnp.maximum(my_extra, 0),
        ]
    ).astype(jnp.int32)

    def slot_spec(first):
        return pl.BlockSpec((1, UROWS, width), lambda i, pick: (first + i, 0, 0))

    stack_shape = unit_weight.shape
    update_shapes = [like(stack_shape)] * 3 + [like(stack_shape, BF16)]
    partial_update = pl.pallas_call(
        stray_update_kernel,
        grid_spec=pltpu.PrefetchScalarGridSpec(
            num_scalar_prefetch=1,
            grid=(spare,),
            in_specs=[slot_spec(own)] * 3
            + [
                pl.BlockSpec((1, UROWS, width), lambda i, pick: (pick[spare + i], 0, 0)),
                pl.BlockSpec((1, UROWS, width), lambda i, pick: (pick[2 * spare + i], 0, 0)),
            ],
            out_specs=[slot_spec(own)] * 4,
        ),
        out_shape=update_shapes,
        compiler_params=params(32),
        cost_estimate=timed(5),
    )(picks, unit_weight, unit_first, unit_second, jnp.concatenate(stray_found), extra_grad)
    unit_weights, unit_firsts, unit_seconds, unit_copies = pl.pallas_call(
        own_update_kernel,
        grid_spec=pltpu.PrefetchScalarGridSpec(
            num_scalar_prefetch=1,
            grid=(own,),
            in_specs=[slot_spec(0)] * 4 + [ANY] * 4,
            out_specs=[slot_spec(0)] * 4,
        ),
        out_shape=update_shapes,
        input_output_aliases={5: 0, 6: 1, 7: 2, 8: 3},
        compiler_params=params(32),
        cost_estimate=timed(4),
    )(my_count, unit_weight, unit_first, unit_second, own_grads, *partial_update)

    proj_total = pl.pallas_call(
        functools.partial(order_rows_kernel, devices),
        out_shape=like((devices, STRAY_TILE, width)),
        in_specs=[SMEM] + [VMEM] * line,
        compiler_params=params(32),
        cost_estimate=timed(1),
    )(where, *[found[:, UROWS:] for found in stray_found])
    proj_total = proj_total[:, :share].reshape(devices * share, width)[: proj_width * D // width]
    proj_total = proj_total.reshape(2, proj_width, D // 2).transpose(0, 2, 1).reshape(D, proj_width)
    gain_total = small_total[: gain_rows.shape[0]].reshape(3, D)
    bias_total = small_total[gain_rows.shape[0], : BUCKETS * heads].reshape(BUCKETS, heads)
    gain_weights, gain_firsts, gain_seconds = adamw_step(
        gain_weight, gain_first, gain_second, gain_total, RATE_GAIN
    )
    bias_weights, bias_firsts, bias_seconds = adamw_step(
        bias_weight, bias_first, bias_second, bias_total, RATE_SMALL
    )
    proj_weights, proj_firsts, proj_seconds = adamw_step(
        proj_weight, proj_first, proj_second, proj_total, RATE_MATRIX
    )
    return (
        encoded,
        token_grad,
        unit_weights,
        unit_firsts,
        unit_seconds,
        unit_copies,
        gain_weights,
        gain_firsts,
        gain_seconds,
        bias_weights,
        bias_firsts,
        bias_seconds,
        proj_weights,
        proj_firsts,
        proj_seconds,
    )


def solution(mesh):
    in_specs = (
        P("dp", None),
        P("dp", "mp"),
        P("dp"),
        P(),
        P(),
        P("dp", None, "mp"),
        P("dp", None, "mp"),
        P("dp", None, "mp"),
        P(),
        P(),
        P(),
        P(None, "mp"),
        P(None, "mp"),
        P(None, "mp"),
        P(None, "mp"),
        P(None, "mp"),
        P(None, "mp"),
    )
    out_specs = (
        P("dp", "mp"),
        P("dp", None),
        P("dp", None, "mp"),
        P("dp", None, "mp"),
        P("dp", None, "mp"),
        P("dp", None, "mp"),
        P(),
        P(),
        P(),
        P(None, "mp"),
        P(None, "mp"),
        P(None, "mp"),
        P(None, "mp"),
        P(None, "mp"),
        P(None, "mp"),
    )
    return jax.shard_map(shards, mesh=mesh, in_specs=in_specs, out_specs=out_specs, check_vma=False)
```

```python
import functools

import jax
import jax.numpy as jnp
from jax import lax
from jax.experimental import pallas as pl
from jax.experimental.pallas import tpu as pltpu
from jax.sharding import PartitionSpec as P

D = 768
HEAD_DIM = 64
FF = 3072
BUCKETS = 32
SLOT = 512
UROWS = 128
STEP = 5
HALF = UROWS // 2

NORM_EPS = 1e-06
ADAM_EPS = 1e-08
BETA_ONE = 0.5
BETA_TWO = 0.5
DECAY = 0.01
RATE_MATRIX = 0.02
RATE_SMALL = 0.1
RATE_GAIN = 0.6
GELU_C = 0.7978845608
GELU_K = 0.044715
MASKED = -1000000000.0

ROWS = D // UROWS
BLOCKS = FF // D
SQUARES = 4 * ROWS
FRONT = 3 * ROWS
SPREAD = 2 * SLOT
STRAY_TILE = 16
WINDOWS = 2, 2, 3
BACK_WINDOWS = 3, 3, 4
ALONG_X, ALONG_Y, ALONG_Z = 0, 1, 2
F32 = jnp.float32
BF16 = jnp.bfloat16
ANY = pl.BlockSpec(memory_space=pl.ANY)
SMEM = pl.BlockSpec(memory_space=pltpu.SMEM)
VMEM = pl.BlockSpec(memory_space=pltpu.VMEM)
HBM = pl.BlockSpec(memory_space=pltpu.HBM)
PAIR = 2 * HEAD_DIM


def dot(left, right):
    return jnp.dot(left, right, preferred_element_type=F32)


def dot_nt(left, right):
    return lax.dot_general(left, right, (((1,), (1,)), ((), ())), preferred_element_type=F32)


def dot_tn(left, right):
    return lax.dot_general(left, right, (((0,), (0,)), ((), ())), preferred_element_type=F32)


def precise_dot(left, right):
    return jnp.dot(left, right, precision=lax.Precision.HIGHEST, preferred_element_type=F32)


def inverse_rms(values):
    return lax.rsqrt(jnp.mean(values * values, axis=-1, keepdims=True) + NORM_EPS)


def norm_back(values, inv_rms, gain_row, grad_in):
    weighted = grad_in * gain_row
    gain_grad = jnp.sum(grad_in * values * inv_rms, axis=0, keepdims=True)
    slope = jnp.mean(weighted * values, axis=-1, keepdims=True)
    values_grad = inv_rms * weighted - values * (inv_rms * inv_rms * inv_rms) * slope
    return values_grad, gain_grad


def adamw_step(weight_now, first_now, second_now, grad_in, rate):
    first_new = BETA_ONE * first_now + (1.0 - BETA_ONE) * grad_in
    second_new = BETA_TWO * second_now + (1.0 - BETA_TWO) * grad_in * grad_in
    first_hat = first_new / (1.0 - BETA_ONE**STEP)
    second_hat = second_new / (1.0 - BETA_TWO**STEP)
    weight_new = weight_now - rate * (
        first_hat / (jnp.sqrt(second_hat) + ADAM_EPS) + DECAY * weight_now
    )
    return weight_new, first_new, second_new


def params(limit_mib):
    return pltpu.CompilerParams(vmem_limit_bytes=limit_mib * 1024 * 1024)


def timed(micros):
    return pl.CostEstimate(flops=int(micros * 1.15e9), bytes_accessed=int(micros * 1e5), transcendentals=0)


def ring_order(line):
    return list(range(0, line, 2)) + list(range(line - 1 - line % 2, 0, -2))


def ring_place(z, line):
    return jnp.where(z % 2 == 0, z // 2, line - (z + 1) // 2)


def ring_device(place, line):
    return jnp.where(2 * place < line, 2 * place, 2 * (line - place) - 1)


def hops(devices):
    line = devices // 4
    order = ring_order(line)
    after = {order[i]: order[(i + 1) % line] for i in range(line)}
    along_x = [(i, i ^ 1) for i in range(devices)]
    along_y = [(i, i ^ 2) for i in range(devices)]
    along_z = [(i, after[i // 4] * 4 + i % 4) for i in range(devices)]
    return along_x, along_y, along_z


def swap(values):
    return lax.ppermute(values, "mp", [(0, 1), (1, 0)])


def rest_place(unit):
    inner = unit - SQUARES
    matrix = inner // (ROWS * BLOCKS)
    rest = inner % (ROWS * BLOCKS)
    wide = ROWS + matrix * ROWS * BLOCKS + (rest % BLOCKS) * ROWS + rest // BLOCKS
    return jnp.where(unit < SQUARES, unit - FRONT, wide)


def after(values, other):
    return lax.optimization_barrier((values, other))[0]


class Links:
    def __init__(self, devices, *windows):
        self.pairs = hops(devices)
        self.sent = ([], [], [])
        self.windows = windows
        self.gate = None

    def settle(self, values):
        return values if self.gate is None else after(values, self.gate)

    def send(self, values, axis, steps=1):
        queue = self.sent[axis]
        window = self.windows[axis] if self.windows else len(queue) + 1
        if len(queue) >= window:
            values = after(values, queue[-window])
        step = dict(self.pairs[axis])
        reach = dict(step)
        for _ in range(steps - 1):
            reach = {i: step[j] for i, j in reach.items()}
        queue.append(lax.ppermute(values, "dp", sorted(reach.items())))
        return queue[-1]


def strays_kernel(own, most, devices, where_ref, index_ref, weight_ref, *refs):
    line = devices // 4
    *outs, stage, sem = refs
    load = pltpu.make_async_copy(weight_ref.at[own:most], stage, sem)
    load.start()
    for out in outs:
        out[...] = jnp.zeros_like(out)
    load.wait()
    me = where_ref[0]
    for j in range(most - own):
        home = index_ref[j]

        @pl.when(home >= 0)
        def _():
            rel = jnp.bitwise_xor(home, me)
            rx = jnp.bitwise_and(rel, 1)
            ry = jnp.bitwise_and(rel // 2, 1)
            rz = (ring_place(home // 4, line) - ring_place(me // 4, line) + line) % line
            unit = stage[j].astype(BF16)
            for odd, (near, far) in enumerate(((rx, ry), (ry, rx))):
                for sent in range(2):

                    @pl.when(jnp.logical_and(rz % 2 == odd, near == sent))
                    def _():
                        outs[2 * odd + sent][far, rz // 2] = unit


def gather_units(own, devices, layout, where_ref, table_ref, pieces, extra_ref, stack, front_sem, rest_sem):
    line = devices // 4
    me = where_ref[0]
    slots = own + 1

    def fetch(source, place):
        @pl.when(place < FRONT)
        def _():
            pltpu.make_async_copy(source, stack.at[place], front_sem).start()

        @pl.when(place >= FRONT)
        def _():
            pltpu.make_async_copy(source, stack.at[place], rest_sem).start()

    for piece, spots in zip(pieces, layout):
        for i, (rx, ry, rz, slot) in enumerate(spots):
            z = ring_device((ring_place(me // 4, line) - rz + line) % line, line)
            other = z * 4 + jnp.bitwise_xor(me % 4, 2 * ry + rx)
            fetch(piece.at[i], table_ref[other * slots + slot])

    @pl.loop(0, where_ref[1])
    def _(i):
        fetch(extra_ref.at[i], table_ref[devices * slots + i])


def wait_units(stack, total, sem):
    while total > 0:
        step = min(stack.shape[0], total)
        pltpu.make_async_copy(stack.at[0:step], stack.at[0:step], sem).wait()
        total -= step


def put_units(dest_ref, first_unit, stage, own_ref, stray_ref, sem):
    for i, unit in enumerate(first_unit):
        dest = dest_ref[unit]

        @pl.when(dest >= 0)
        def _():
            pltpu.make_async_copy(stage.at[i], own_ref.at[dest], sem).start()

        @pl.when(dest < 0)
        def _():
            pltpu.make_async_copy(stage.at[i], stray_ref.at[-1 - dest, :UROWS], sem).start()


def toeplitz(row):
    width = SPREAD
    tile = jnp.broadcast_to(pltpu.roll(row, width - (SLOT - 1), 1), (8, width))
    places = lax.broadcasted_iota(jnp.int32, (8, width), 0)
    for bit in (1, 2, 4):
        tile = jnp.where(jnp.bitwise_and(places, bit) != 0, pltpu.roll(tile, bit, 1), tile)
    reach = 8
    while reach < SLOT // 2:
        tile = jnp.concatenate([tile, pltpu.roll(tile, reach, 1)], axis=0)
        reach *= 2
    lower = jnp.concatenate([tile[:, width - reach :], tile[:, : SLOT - reach]], axis=1)
    return jnp.concatenate([tile[:, :SLOT], lower], axis=0)


def diagonals(tile):
    rows = SLOT
    while rows > 128:
        rows //= 2
        blank = jnp.zeros((rows, rows), F32)
        tile = jnp.concatenate([tile[rows:], blank], axis=1) + jnp.concatenate(
            [blank, tile[:rows]], axis=1
        )
    tile = jnp.concatenate([tile, jnp.zeros((rows, SPREAD - tile.shape[1]), F32)], axis=1)
    while rows > 8:
        rows //= 2
        tile = tile[rows:] + pltpu.roll(tile[:rows], rows, 1)
    places = lax.broadcasted_iota(jnp.int32, tile.shape, 0)
    for bit in (4, 2, 1):
        tile = jnp.where(jnp.bitwise_and(places, bit) == 0, pltpu.roll(tile, bit, 1), tile)
    return jnp.sum(tile, axis=0, keepdims=True)


def matrix(ref, first):
    return ref[first : first + ROWS].reshape(D, ref.shape[2])


def pair_columns(ref, step):
    return ref[:, pl.ds(pl.multiple_of(step * PAIR, PAIR), PAIR)]


def attend_kernel(own, devices, layout, lengths_ref, where_ref, table_ref, tokens_ref, gain_ref, bias_ref, extra_ref, *refs):
    pieces = refs[: len(layout)]
    norm_ref, query_ref, key_ref, value_ref, prob_ref, mixed_ref, front_ref, rest_ref = refs[len(layout) : -5]
    stack, front_sem, rest_sem, front_out, rest_out = refs[-5:]
    step = pl.program_id(0)
    front_copy = pltpu.make_async_copy(stack.at[:FRONT], front_ref, front_out)
    rest_copy = pltpu.make_async_copy(stack.at[FRONT:], rest_ref, rest_out)

    @pl.when(step == 0)
    def _():
        gather_units(
            own, devices, layout, where_ref, table_ref, pieces, extra_ref, stack, front_sem, rest_sem
        )
        inputs = tokens_ref[...].astype(F32)
        normed = (inputs * inverse_rms(inputs) * gain_ref[0:1, :]).astype(BF16)
        norm_ref[...] = normed
        wait_units(stack, FRONT, front_sem)
        front_copy.start()
        query_ref[...] = dot(normed, matrix(stack, 0)).astype(BF16)
        key_ref[...] = dot(normed, matrix(stack, ROWS)).astype(BF16)
        value_ref[...] = dot(normed, matrix(stack, 2 * ROWS)).astype(BF16)
        wait_units(stack, devices * own - FRONT, rest_sem)

        @pl.loop(0, where_ref[1])
        def _(i):
            wait_units(stack, 1, rest_sem)

        rest_copy.start()

    @pl.when(step == pl.num_programs(0) - 1)
    def _():
        front_copy.wait()
        rest_copy.wait()

    queries = pair_columns(query_ref, step)
    keys = pair_columns(key_ref, step)
    values = pair_columns(value_ref, step)
    lanes = lax.broadcasted_iota(jnp.int32, (SLOT, PAIR), 1) // HEAD_DIM
    seen = lax.broadcasted_iota(jnp.int32, (1, SLOT), 1) < lengths_ref[0]
    mixes = []
    for which in range(2):
        scores = dot_nt(jnp.where(lanes == which, queries, jnp.zeros_like(queries)), keys)
        scores = scores + toeplitz(bias_ref[pl.ds(2 * step + which, 1), :])
        scores = jnp.where(seen, scores, MASKED)
        powers = jnp.exp(scores - jnp.max(scores, axis=-1, keepdims=True))
        probabilities = powers * (1.0 / jnp.sum(powers, axis=-1, keepdims=True))
        prob_ref[which] = probabilities
        mixes.append(dot(probabilities.astype(BF16), values))
    mixed = jnp.where(lanes == 0, mixes[0], mixes[1]).astype(BF16)
    mixed_ref[:, pl.ds(pl.multiple_of(step * PAIR, PAIR), PAIR)] = mixed


def out_kernel(own, devices, where_ref, table_ref, mixed_ref, rest_in, *refs):
    line = devices // 4
    *pieces, part_ref, rest_ref, stage, weight, stage_sem, weight_sem, put_sem = refs
    me = where_ref[0]
    load = pltpu.make_async_copy(rest_in.at[0:ROWS], weight, weight_sem)
    load.start()
    for rz in range(line):
        pltpu.make_async_copy(pieces[rz], stage.at[4 * rz : 4 * rz + 4], stage_sem).start()
    load.wait()
    pltpu.make_async_copy(stage, stage, stage_sem).wait()
    for rz in range(line):
        z = ring_device((ring_place(me // 4, line) - rz + line) % line, line)
        for near in range(4):
            other = z * 4 + jnp.bitwise_xor(me % 4, near)
            place = table_ref[other * (own + 1) + own] - FRONT
            i = 4 * rz + near
            pltpu.make_async_copy(stage.at[i], rest_ref.at[place], put_sem).start()

            @pl.when(place < ROWS)
            def _():
                weight[place] = stage[i]

    part_ref[...] = dot_nt(mixed_ref[...], matrix(weight, 0))
    pltpu.make_async_copy(stage, stage, put_sem).wait()


def gelu_tanh(values):
    return jnp.tanh(GELU_C * (values + GELU_K * values * values * values))


def feed_kernel(
    tokens_ref, mine_ref, other_ref, gain_ref, gate_w, up_w, down_w,
    residual_ref, norm_ref, gate_ref, up_ref, hidden_ref, part_ref,
):
    step = pl.program_id(0)

    @pl.when(step == 0)
    def _():
        residual = tokens_ref[...].astype(F32) + (mine_ref[...] + other_ref[...])
        residual_ref[...] = residual
        norm_ref[...] = (residual * inverse_rms(residual) * gain_ref[1:2, :]).astype(BF16)
        part_ref[...] = jnp.zeros_like(part_ref)

    normed = norm_ref[...]
    gate = dot(normed, matrix(gate_w, 0))
    up = dot(normed, matrix(up_w, 0))
    gate_ref[...] = gate
    up_ref[...] = up
    hidden = (0.5 * gate * (1.0 + gelu_tanh(gate)) * up).astype(BF16)
    hidden_ref[...] = hidden
    part_ref[...] += dot_nt(hidden, matrix(down_w, 0))


def turn_kernel(
    lengths_ref, residual_ref, mine_ref, other_ref, gain_ref, proj_ref, proj_other, cot_ref, cot_other,
    gate_ref, up_ref, gate_w, up_w, down_w,
    encoded_ref, proj_grad, gain_grad, grad_ref, feed_ref, dgate_ref, dup_ref, part_ref,
):
    step = pl.program_id(0)

    @pl.when(step == 0)
    def _():
        residual = residual_ref[...] + (mine_ref[...] + other_ref[...])
        inv_rms = inverse_rms(residual)
        normed = (residual * inv_rms * gain_ref[2:3, :]).astype(BF16)
        encoded_ref[...] = dot(normed, proj_ref[...])
        rows = lax.broadcasted_iota(jnp.int32, (SLOT, 1), 0) < lengths_ref[0]
        mine = jnp.where(rows, cot_ref[...], jnp.zeros_like(cot_ref))
        other = jnp.where(rows, cot_other[...], jnp.zeros_like(cot_other))
        backward = dot_tn(mine, normed)
        proj_grad[0] = backward[:, : D // 2]
        proj_grad[1] = backward[:, D // 2 :]
        third = dot_nt(mine, proj_ref[...]) + dot_nt(other, proj_other[...])
        grad, gain = norm_back(residual, inv_rms, gain_ref[2:3, :], third)
        gain_grad[...] = gain
        grad_ref[...] = grad
        feed_ref[...] = grad.astype(BF16)
        part_ref[...] = jnp.zeros_like(part_ref)

    dhidden = dot(feed_ref[...], matrix(down_w, 0))
    gate = gate_ref[...]
    bend = gelu_tanh(gate)
    slope = 0.5 * (1.0 + bend) + 0.5 * gate * (1.0 - bend * bend) * (
        GELU_C * (1.0 + 3.0 * GELU_K * gate * gate)
    )
    dgate = (dhidden * up_ref[...] * slope).astype(BF16)
    dup = (dhidden * (0.5 * gate * (1.0 + bend))).astype(BF16)
    dgate_ref[...] = dgate
    dup_ref[...] = dup
    part_ref[...] += dot_nt(dgate, matrix(gate_w, 0)) + dot_nt(dup, matrix(up_w, 0))


def wide_grads_kernel(
    units, dest_ref, norm_ref, feed_ref, hidden_ref, dgate_ref, dup_ref, own_ref, stray_ref, stage, sems
):
    step = pl.program_id(0)
    slot = step % 2
    shape = (ROWS,) + stage.shape[2:]

    def settle(which):
        pltpu.make_async_copy(stage.at[which], stage.at[which], sems.at[which]).wait()

    @pl.when(step >= 2)
    def _():
        settle(slot)

    normed = norm_ref[...]
    stage[slot, 0:ROWS] = dot_tn(normed, dgate_ref[...]).astype(BF16).reshape(shape)
    stage[slot, ROWS : 2 * ROWS] = dot_tn(normed, dup_ref[...]).astype(BF16).reshape(shape)
    stage[slot, 2 * ROWS :] = dot_tn(feed_ref[...], hidden_ref[...]).astype(BF16).reshape(shape)
    names = [
        SQUARES + which * ROWS * BLOCKS + row * BLOCKS + step for which in range(3) for row in range(ROWS)
    ]
    put_units(dest_ref, names, stage.at[slot], own_ref, stray_ref, sems.at[slot])

    @pl.when(step == pl.num_programs(0) - 1)
    def _():
        settle(1 - slot)
        settle(slot)


def enter_back_kernel(
    dest_ref, home_ref, grad_ref, residual_ref, mine_ref, other_ref, gain_ref, weight_ref, mixed_ref,
    proj_ref, own_in, stray_in,
    grad_one, gain_grad, dmixed_ref, own_ref, stray_ref, stage, sem, proj_sem,
):
    for home in range(proj_ref.shape[0]):
        pltpu.make_async_copy(
            proj_ref.at[home], stray_ref.at[home_ref[home], UROWS:], proj_sem
        ).start()
    residual = residual_ref[...]
    second = mine_ref[...] + other_ref[...]
    back, gain = norm_back(residual, inverse_rms(residual), gain_ref[1:2, :], second)
    gain_grad[...] = gain
    total = grad_ref[...] + back
    grad_one[...] = total
    lowered = total.astype(BF16)
    stage[...] = dot_tn(lowered, mixed_ref[...]).astype(BF16).reshape(stage.shape)
    put_units(dest_ref, range(FRONT, SQUARES), stage, own_ref, stray_ref, sem)
    dmixed_ref[...] = dot(lowered, matrix(weight_ref, 0)).astype(BF16)
    pltpu.make_async_copy(stage, stage, sem).wait()
    pltpu.make_async_copy(proj_ref, proj_ref, proj_sem).wait()


def attend_back_kernel(
    dmixed_ref, query_ref, key_ref, value_ref, prob_ref, dquery_ref, dkey_ref, dvalue_ref, offset_ref
):
    queries, keys, values, dmixed = query_ref[...], key_ref[...], value_ref[...], dmixed_ref[...]
    lanes = lax.broadcasted_iota(jnp.int32, (SLOT, PAIR), 1) // HEAD_DIM
    parts = []
    for which in range(2):
        dprob = dot_nt(jnp.where(lanes == which, dmixed, jnp.zeros_like(dmixed)), values)
        probabilities = prob_ref[which]
        share = jnp.sum(probabilities * dprob, axis=-1, keepdims=True)
        dscore = (probabilities * (dprob - share)).astype(BF16)
        parts.append(
            (
                dot(dscore, keys),
                dot_tn(dscore, queries),
                dot_tn(probabilities.astype(BF16), dmixed),
            )
        )
        offset_ref[0, which : which + 1, :] = diagonals(dscore.astype(F32))
    for out, first, second in zip((dquery_ref, dkey_ref, dvalue_ref), *parts):
        out[...] = jnp.where(lanes == 0, first, second).astype(BF16)


def joined(refs):
    return jnp.concatenate([ref[...] for ref in refs], axis=1)


def first_grad_kernel(weight_ref, *refs):
    *parts, out_ref = refs
    width = len(parts) // 3
    total = 0.0
    for i in range(3):
        total = total + dot_nt(joined(parts[i * width : (i + 1) * width]), matrix(weight_ref, i * ROWS))
    out_ref[...] = total.astype(BF16)


def front_grads_kernel(dest_ref, norm_ref, *refs):
    *parts, own_in, own_ref, stage, sem = refs
    width = len(parts) // 3
    normed = norm_ref[...]
    shape = (ROWS,) + stage.shape[1:]
    for i in range(3):
        first = i * ROWS
        grads = joined(parts[i * width : (i + 1) * width])
        stage[first : first + ROWS] = dot_tn(normed, grads).astype(BF16).reshape(shape)
        for unit in range(first, first + ROWS):
            pltpu.make_async_copy(stage.at[unit], own_ref.at[dest_ref[unit]], sem).start()
    pltpu.make_async_copy(stage, stage, sem).wait()


def token_grad_kernel(tokens_ref, grad_ref, mine_ref, other_ref, gain_ref, out_ref, gain_grad):
    inputs = tokens_ref[...].astype(F32)
    first = mine_ref[...].astype(F32) + other_ref[...].astype(F32)
    back, gain = norm_back(inputs, inverse_rms(inputs), gain_ref[0:1, :], first)
    out_ref[...] = grad_ref[...] + back
    gain_grad[...] = gain


def order_rows_kernel(devices, where_ref, found_ref, out_ref):
    line = devices // 4
    me = where_ref[0]
    for rz in range(line):
        z = ring_device((ring_place(me // 4, line) - rz + line) % line, line)
        for far in range(2):
            for near in range(2):
                rx, ry = (far, near) if rz % 2 else (near, far)
                other = z * 4 + jnp.bitwise_xor(me % 4, 2 * ry + rx)
                place = ((rz % 2 * 2 + far) * 2 + near) * (line // 2) + rz // 2
                out_ref[other] = found_ref[place].astype(F32)


def stray_update_kernel(pick_ref, weight, first, second, stray, extra, *refs):
    kind = pick_ref[pl.program_id(0)]
    grad = jnp.where(kind == 1, stray[0].astype(F32), extra[0].astype(F32))
    grad = jnp.where(kind == 0, 0.0, grad)
    update_slot(weight, first, second, grad, refs[-4:])


def update_slot(weight, first, second, grad, outs):
    new_weight, new_first, new_second = adamw_step(
        weight[0], first[0], second[0], grad, RATE_MATRIX
    )
    outs[0][0] = new_weight
    outs[1][0] = new_first
    outs[2][0] = new_second
    outs[3][0] = new_weight.astype(BF16)


def own_update_kernel(count_ref, weight, first, second, grad_ref, *refs):
    grad = jnp.where(pl.program_id(0) < count_ref[0], grad_ref[0], 0.0)
    update_slot(weight, first, second, grad, refs[-4:])


def shards(
    tokens,
    out_grad,
    doc_lengths,
    owner_list,
    bucket_table,
    unit_weight,
    unit_first,
    unit_second,
    gain_weight,
    gain_first,
    gain_second,
    bias_weight,
    bias_first,
    bias_second,
    proj_weight,
    proj_first,
    proj_second,
):
    most, _, width = unit_weight.shape
    heads = bias_weight.shape[1]
    count = tokens.shape[0]
    units = owner_list.shape[0]
    proj_width = proj_weight.shape[1]
    devices = lax.axis_size("dp")
    line = devices // 4
    own = max(1, (units - 1) // devices)
    slots = own + 1
    spare = most - own
    me = lax.axis_index("dp").astype(jnp.int32)

    def like(shape, kind=F32):
        return jax.ShapeDtypeStruct(shape, kind)

    full, left = divmod(units, most)
    extra_count = max(FRONT, full * spare + max(0, left - own) - devices)
    indices = jnp.arange(units, dtype=jnp.int32)
    before = indices[None, :] < indices[:, None]
    same = owner_list[:, None] == owner_list[None, :]
    rank = jnp.sum((same & before).astype(jnp.int32), axis=1)
    is_over = rank >= own
    may_stray = is_over & (indices >= FRONT)
    stray_index = jnp.sum((before & may_stray[None, :]).astype(jnp.int32), axis=1)
    is_stray = may_stray & (stray_index < devices)
    is_extra = is_over & ~is_stray
    extra_index = jnp.sum((before & is_extra[None, :]).astype(jnp.int32), axis=1)
    extra_total = jnp.sum(is_extra.astype(jnp.int32))
    many = extra_total > 0
    position = jnp.where(
        is_stray,
        stray_index * slots + own,
        jnp.where(is_extra, devices * slots + extra_index, owner_list * slots + rank),
    )
    position_ids = jnp.arange(devices * slots + extra_count, dtype=jnp.int32)
    hit = position[None, :] == position_ids[:, None]
    placed = jnp.where(indices < FRONT, indices, FRONT + rest_place(indices))
    table = units + jnp.sum(jnp.where(hit, placed[None, :] - units, 0), axis=1).astype(jnp.int32)
    spare_ids = jnp.arange(spare, dtype=jnp.int32)
    my_over = (owner_list[None, :] == me) & (rank[None, :] == own + spare_ids[:, None])
    my_stray = jnp.sum(jnp.where(my_over & is_stray[None, :], stray_index[None, :] + 1, 0), axis=1) - 1
    my_extra = jnp.sum(jnp.where(my_over & is_extra[None, :], extra_index[None, :] + 1, 0), axis=1) - 1
    my_count = jnp.sum((owner_list == me).astype(jnp.int32)).reshape(1)
    where = jnp.stack([me, extra_total]).astype(jnp.int32)

    home = jnp.where(is_stray, stray_index, owner_list)
    rel_x = jnp.bitwise_and(jnp.bitwise_xor(home, me), 1)
    rel_y = jnp.bitwise_and(jnp.bitwise_xor(home, me) // 2, 1)
    rel_z = (ring_place(home // 4, line) - ring_place(me // 4, line) + line) % line
    cut = (own + 1) // 2
    spans = [(0, cut), (cut, own)] if own > cut else [(0, cut)]
    even = rel_z % 2 == 0
    in_first = rank < cut
    near_is_x = even == in_first
    corner = jnp.where(near_is_x, rel_x, rel_y) * 2 + jnp.where(near_is_x, rel_y, rel_x)
    own_dest = rel_z * 4 * own + jnp.where(
        in_first, corner * cut + rank, 4 * cut + corner * (own - cut) + rank - cut
    )

    def stray_dest_of(x, y, z):
        even = z % 2 == 0
        corner = jnp.where(even, x, y) * 2 + jnp.where(even, y, x)
        return (jnp.where(even, 0, 2 * line) + corner * (line // 2) + z // 2).astype(jnp.int32)

    stray_dest = stray_dest_of(rel_x, rel_y, rel_z)
    homes = jnp.arange(devices, dtype=jnp.int32)
    home_dest = stray_dest_of(
        jnp.bitwise_and(jnp.bitwise_xor(homes, me), 1),
        jnp.bitwise_and(jnp.bitwise_xor(homes, me) // 2, 1),
        (ring_place(homes // 4, line) - ring_place(me // 4, line) + line) % line,
    )
    dest = jnp.where(
        is_stray,
        -1 - stray_dest,
        jnp.where(is_extra, 4 * line * own + extra_index, own_dest),
    ).astype(jnp.int32)

    extra_shape = (extra_count, UROWS, width)

    def extra_weights():
        wanted = jnp.arange(extra_count, dtype=jnp.int32)[:, None] == my_extra[None, :]
        taken = jnp.take(unit_weight[own:], jnp.argmax(wanted, axis=1), axis=0)
        return lax.psum(jnp.where(jnp.any(wanted, axis=1)[:, None, None], taken, 0.0), "dp").astype(BF16)

    def no_extra():
        return jnp.zeros(extra_shape, BF16)

    extra = lax.cond(many, extra_weights, no_extra)

    def sum_strays(links, keep_a, send_a, keep_b, send_b):
        from_x = links.send(send_a, ALONG_X)
        from_y = links.send(send_b, ALONG_Y)
        yield
        from_x, from_y = links.settle(from_x), links.settle(from_y)
        low_y = links.send((keep_a[1].astype(F32) + from_x[1].astype(F32)).astype(BF16), ALONG_Y)
        high_x = links.send((keep_b[1].astype(F32) + from_y[1].astype(F32)).astype(BF16), ALONG_X)
        yield
        low_y, high_x = links.settle(low_y), links.settle(high_x)
        low = keep_a[0].astype(F32) + from_x[0].astype(F32) + low_y.astype(F32)
        high = keep_b[0].astype(F32) + from_y[0].astype(F32) + high_x.astype(F32)
        sums = [(high if rz % 2 else low)[rz // 2] for rz in range(line)]
        total = sums[0]
        terms = [links.send(sums[rz].astype(BF16), ALONG_Z, rz) for rz in range(1, line)]
        yield
        for term in terms:
            total = total + links.settle(term).astype(F32)
        return total.astype(BF16)

    def gather_strays(links, unit):
        got = links.send(unit, ALONG_X)
        yield
        near = jnp.stack([unit, links.settle(got)])
        got = links.send(near, ALONG_Y)
        yield
        near = jnp.concatenate([near, links.settle(got)])
        found = [near]
        for _ in range(line - 1):
            found.append(links.send(found[-1], ALONG_Z))
            yield
            found[-1] = links.settle(found[-1])
        return found

    def gather_lines(links, unit):
        got = [links.send(unit, ALONG_Z, rz) for rz in range(1, line)]
        yield
        every = [unit] + [links.settle(term) for term in got]
        halves = [jnp.stack(every[0::2]), jnp.stack(every[1::2])]
        yield
        got = [links.send(half, axis) for half, axis in zip(halves, (ALONG_X, ALONG_Y))]
        yield
        both = [jnp.stack([half, links.settle(term)]) for half, term in zip(halves, got)]
        got = [links.send(half, axis) for half, axis in zip(both, (ALONG_Y, ALONG_X))]
        yield
        return [(half, links.settle(term)) for half, term in zip(both, got)]

    def stray_chain(links, *arrays):
        unit = yield from sum_strays(links, *arrays)
        return (yield from gather_strays(links, unit))

    def stray_grad_chain(links, *arrays):
        unit = yield from sum_strays(links, *arrays)
        return (yield from gather_lines(links, unit))

    class Chain:
        def __init__(self, links, steps):
            self.links, self.steps, self.value = links, steps, None

        def step(self, gate=None):
            self.links.gate = gate
            try:
                if self.value is None:
                    next(self.steps)
            except StopIteration as end:
                self.value = end.value

        def finish(self):
            while self.value is None:
                self.step()
            return self.value

    proj_low = proj_weight.astype(BF16)
    proj_other = swap(proj_low)
    cot_other = swap(out_grad)

    links = Links(devices, *WINDOWS)
    rings = [[unit_weight[first:last].astype(BF16)] for first, last in spans]
    pieces, layout, rounds = [], [], {}

    def ring_step():
        for ring in rings:
            ring.append(links.send(ring[-1], ALONG_Z))

    def keep(values, rx, ry, spots):
        pieces.append(values)
        layout.append([(rx, ry, rz, slot) for rz, slot in spots])

    def near_round(pair):
        for i, axis in enumerate((ALONG_X, ALONG_Y)):
            parts, spots = [], []
            for rz in (2 * pair, 2 * pair + 1):
                which = (i + rz) % 2
                if which < len(rings):
                    parts.append(rings[which][rz])
                    spots += [(rz, slot) for slot in range(*spans[which])]
            if parts:
                values = jnp.concatenate(parts) if len(parts) > 1 else parts[0]
                rounds[pair, axis] = values, spots, links.send(values, axis)

    def far_direct(pair):
        for axis in (ALONG_X, ALONG_Y):
            if (pair, axis) in rounds:
                values, spots, got = rounds[pair, axis]
                other = ALONG_X + ALONG_Y - axis
                keep(values, 0, 0, spots)
                keep(got, int(axis == ALONG_X), int(axis == ALONG_Y), spots)
                keep(links.send(values, other), int(axis == ALONG_Y), int(axis == ALONG_X), spots)

    def far_through(pair):
        for axis in (ALONG_X, ALONG_Y):
            if (pair, axis) in rounds:
                values, spots, got = rounds[pair, axis]
                keep(links.send(got, ALONG_X + ALONG_Y - axis), 1, 1, spots)

    ring_step()
    near_shape = like((2, line // 2, UROWS, width), BF16)
    stray_parts = pl.pallas_call(
        functools.partial(strays_kernel, own, most, devices),
        out_shape=[near_shape] * 4,
        in_specs=[SMEM, SMEM, ANY],
        out_specs=[VMEM] * 4,
        scratch_shapes=[pltpu.VMEM((spare, UROWS, width), F32), pltpu.SemaphoreType.DMA],
        compiler_params=params(40),
        cost_estimate=timed(2),
    )(where, my_stray, unit_weight)
    strays = Chain(links, stray_chain(links, *stray_parts))
    strays.step()
    for pair in range(line // 2):
        while len(rings[0]) < 2 * pair + 2:
            ring_step()
        near_round(pair)
        if pair == 0:
            strays.step(rings[0][-1])
            first_near = links.sent[ALONG_Y][1]
            while len(rings[0]) < min(line, 3):
                ring_step()
            far_direct(pair)
            strays.step(first_near)
            if len(rings[0]) < line:
                ring_step()
            strays.step(links.sent[ALONG_X][-1])
            far_through(pair)
            strays.step(links.sent[ALONG_X][-2])
        else:
            strays.step(links.sent[ALONG_Y][-3])
            far_direct(pair)
            strays.step(links.sent[ALONG_Y][-3])
            far_through(pair)
    found = strays.finish()
    tokens, proj_other, cot_other = lax.optimization_barrier((tokens, proj_other, cot_other))

    bucket_hot = (bucket_table[:, None] == jnp.arange(BUCKETS, dtype=jnp.int32)[None, :]).astype(F32)
    bucket_hot = jnp.pad(bucket_hot, ((0, SPREAD - bucket_hot.shape[0]), (0, 0)))
    bias_rows = jnp.pad(precise_dot(bucket_hot, bias_weight).T, ((0, 8 - heads % 8), (0, 0)))
    def whole(shape):
        return pl.BlockSpec(shape, lambda i: (0,) * len(shape))

    wide_shape = (count, D)
    head_shape = (count, width)
    front_spec = whole((FRONT, UROWS, width))
    out_spec = pl.BlockSpec((ROWS, UROWS, width), lambda i: (0, 0, 0))
    prob_spec = pl.BlockSpec((2, SLOT, SLOT), lambda i: (i, 0, 0))
    gain_spec = whole((3, D))
    bias_spec = whole(bias_rows.shape)
    column_spec = pl.BlockSpec((count, width), lambda i: (0, i))

    def unit_spec(which):
        return pl.BlockSpec((ROWS, UROWS, width), lambda i: (1 + which * BLOCKS + i, 0, 0))

    wide_specs = [unit_spec(0), unit_spec(1), unit_spec(2)]

    stack_shape = (units + 1, UROWS, width)
    rest_shape = like((units + 1 - FRONT, UROWS, width), BF16)
    first_in, queries, keys, values, probabilities, mixed, front, rest = pl.pallas_call(
        functools.partial(attend_kernel, own, devices, layout),
        grid=(heads // 2,),
        in_specs=[SMEM] * 3 + [whole(wide_shape), gain_spec, bias_spec] + [ANY] * (1 + len(pieces)),
        out_specs=[whole(wide_shape)] + [whole(head_shape)] * 3 + [prob_spec, whole(head_shape), HBM, HBM],
        out_shape=[like(wide_shape, BF16)]
        + [like(head_shape, BF16)] * 3
        + [like((heads, SLOT, SLOT)), like(head_shape, BF16), like((FRONT, UROWS, width), BF16), rest_shape],
        scratch_shapes=[pltpu.VMEM(stack_shape, BF16)] + [pltpu.SemaphoreType.DMA] * 4,
        compiler_params=params(60),
        cost_estimate=timed(14),
    )(doc_lengths, where, table, tokens, gain_weight, bias_rows, extra, *pieces)
    attn_part, rest = pl.pallas_call(
        functools.partial(out_kernel, own, devices),
        grid=(1,),
        in_specs=[SMEM] * 2 + [whole(head_shape)] + [ANY] * (1 + line),
        out_specs=[whole(wide_shape), HBM],
        out_shape=[like(wide_shape), rest_shape],
        input_output_aliases={3: 1},
        scratch_shapes=[
            pltpu.VMEM((4 * line, UROWS, width), BF16),
            pltpu.VMEM((ROWS, UROWS, width), BF16),
        ]
        + [pltpu.SemaphoreType.DMA] * 3,
        compiler_params=params(56),
        cost_estimate=timed(4),
    )(where, table, mixed, rest, *found)

    residual_one, second_in, gate, up, hidden, feed_part = pl.pallas_call(
        feed_kernel,
        grid=(BLOCKS,),
        in_specs=[whole(wide_shape)] * 3 + [gain_spec] + wide_specs,
        out_specs=[whole(wide_shape)] * 2 + [column_spec] * 3 + [whole(wide_shape)],
        out_shape=[
            like(wide_shape),
            like(wide_shape, BF16),
            like((count, BLOCKS * width)),
            like((count, BLOCKS * width)),
            like((count, BLOCKS * width), BF16),
            like(wide_shape),
        ],
        compiler_params=params(56),
        cost_estimate=timed(11),
    )(tokens, attn_part, swap(attn_part), gain_weight, rest, rest, rest)

    encoded, proj_grad, gain_three, grad_two, feed_grad, dgate, dup, second_part = pl.pallas_call(
        turn_kernel,
        grid=(BLOCKS,),
        in_specs=[SMEM]
        + [whole(wide_shape)] * 3
        + [gain_spec]
        + [whole((D, proj_width))] * 2
        + [whole((count, proj_width))] * 2
        + [column_spec] * 2
        + wide_specs,
        out_specs=[
            whole((count, proj_width)),
            whole((2, proj_width, D // 2)),
            whole((1, D)),
            whole(wide_shape),
            whole(wide_shape),
            column_spec,
            column_spec,
            whole(wide_shape),
        ],
        out_shape=[
            like((count, proj_width)),
            like((2, proj_width, D // 2)),
            like((1, D)),
            like(wide_shape),
            like(wide_shape, BF16),
            like((count, BLOCKS * width), BF16),
            like((count, BLOCKS * width), BF16),
            like(wide_shape),
        ],
        compiler_params=params(56),
        cost_estimate=timed(14),
    )(
        doc_lengths, residual_one, feed_part, swap(feed_part), gain_weight, proj_low, proj_other,
        out_grad, cot_other, gate, up, rest, rest, rest,
    )

    own_shape = like((4 * line * own + extra_count, UROWS, width), BF16)
    stray_shape = like((4 * line, UROWS + STRAY_TILE, width), BF16)
    proj_rows = proj_grad.reshape(-1, width)
    share = -(-proj_rows.shape[0] // devices)
    proj_rows = jnp.pad(proj_rows, ((0, share * devices - proj_rows.shape[0]), (0, 0)))
    proj_rows = proj_rows.reshape(devices, share, width).astype(BF16)
    proj_rows = jnp.pad(proj_rows, ((0, 0), (0, STRAY_TILE - share), (0, 0)))
    own_units, stray_units = pl.pallas_call(
        functools.partial(wide_grads_kernel, units),
        grid=(BLOCKS,),
        in_specs=[SMEM] + [whole(wide_shape)] * 2 + [column_spec] * 3,
        out_specs=[HBM] * 2,
        out_shape=[own_shape, stray_shape],
        scratch_shapes=[
            pltpu.VMEM((2, 3 * ROWS, UROWS, width), BF16),
            pltpu.SemaphoreType.DMA((2,)),
        ],
        compiler_params=params(56),
        cost_estimate=timed(9),
    )(dest, second_in, feed_grad, hidden, dgate, dup)

    grad_one, gain_two, dmixed, own_units, stray_units = pl.pallas_call(
        enter_back_kernel,
        grid=(1,),
        in_specs=[SMEM] * 2
        + [whole(wide_shape)] * 4
        + [gain_spec, out_spec, whole(head_shape), whole(proj_rows.shape)]
        + [ANY] * 2,
        out_specs=[whole(wide_shape), whole((1, D)), whole(head_shape)] + [HBM] * 2,
        out_shape=[like(wide_shape), like((1, D)), like(head_shape, BF16), own_shape, stray_shape],
        input_output_aliases={10: 3, 11: 4},
        scratch_shapes=[pltpu.VMEM((ROWS, UROWS, width), BF16)] + [pltpu.SemaphoreType.DMA] * 2,
        compiler_params=params(56),
        cost_estimate=timed(6),
    )(
        dest, home_dest, grad_two, residual_one, second_part, swap(second_part), gain_weight, rest, mixed,
        proj_rows, own_units, stray_units,
    )

    links = Links(devices, *BACK_WINDOWS)
    by_near = stray_units.reshape(4, 2, line // 2, UROWS + STRAY_TILE, width)
    strays = Chain(links, stray_grad_chain(links, *[by_near[i] for i in range(4)]))

    def attend_back(first, pairs, dmixed):
        pair_spec = pl.BlockSpec((count, PAIR), lambda i: (0, first + i))
        out_spec = pl.BlockSpec((count, PAIR), lambda i: (0, i))
        return pl.pallas_call(
            attend_back_kernel,
            grid=(pairs,),
            in_specs=[pair_spec] * 4 + [pl.BlockSpec((2, SLOT, SLOT), lambda i: (first + i, 0, 0))],
            out_specs=[out_spec] * 3 + [pl.BlockSpec((1, 8, SPREAD), lambda i: (i, 0, 0))],
            out_shape=[like((count, PAIR * pairs), BF16)] * 3 + [like((pairs, 8, SPREAD))],
            compiler_params=params(56),
            cost_estimate=timed(4.3 * pairs),
        )(dmixed, queries, keys, values, probabilities)

    pairs = heads // 2
    strays.step()
    *grads_a, offsets_a = attend_back(0, pairs - 1, dmixed)
    strays.step()
    *grads_b, offsets_b = attend_back(pairs - 1, 1, after(dmixed, links.sent[ALONG_Y][0]))
    head_grads = [part for both in zip(grads_a, grads_b) for part in both]
    offset_grad = jnp.concatenate([offsets_a, offsets_b])[:, :2].reshape(heads, SPREAD)
    part_specs = [whole(part.shape) for part in head_grads]
    first_part = pl.pallas_call(
        first_grad_kernel,
        grid=(1,),
        in_specs=[front_spec] + part_specs,
        out_specs=whole(wide_shape),
        out_shape=like(wide_shape, BF16),
        compiler_params=params(56),
        cost_estimate=timed(2),
    )(front, *head_grads)

    own_units = pl.pallas_call(
        front_grads_kernel,
        grid=(1,),
        in_specs=[SMEM, whole(wide_shape)] + part_specs + [ANY],
        out_specs=HBM,
        out_shape=own_shape,
        input_output_aliases={2 + len(head_grads): 0},
        scratch_shapes=[pltpu.VMEM((FRONT, UROWS, width), BF16), pltpu.SemaphoreType.DMA],
        compiler_params=params(56),
        cost_estimate=timed(4),
    )(dest, first_in, *head_grads, own_units)

    token_grad, gain_one = pl.pallas_call(
        token_grad_kernel,
        out_shape=[like(wide_shape), like((1, D))],
        compiler_params=params(56),
        cost_estimate=timed(4),
    )(tokens, grad_one, first_part, swap(first_part), gain_weight)

    def total_of(links, values):
        got = links.send(values, ALONG_X)
        yield
        values = values + links.settle(got)
        got = links.send(values, ALONG_Y)
        yield
        values = values + links.settle(got)
        terms = [values] + [links.send(values, ALONG_Z, rz) for rz in range(1, line)]
        yield
        terms = [links.settle(term) for term in terms]
        while len(terms) > 1:
            middle = len(terms) // 2
            terms = [terms[i] + terms[middle + i] for i in range(middle)]
        return terms[0]

    halves = {}

    def near_sums(own_units, rz):
        first = 4 * rz * own
        for group, span in enumerate(spans):
            size = span[1] - span[0]
            axis = (ALONG_X, ALONG_Y)[(group + rz) % 2]
            shape = (2, size, UROWS, width)
            kept = own_units[first : first + 2 * size].reshape(shape)
            given = own_units[first + 2 * size : first + 4 * size].reshape(shape)
            halves[rz, group] = axis, kept, links.send(given, axis)
            first += 4 * size
        return given

    def far_sums(rz):
        sums = []
        for group in range(len(spans)):
            axis, kept, got = halves[rz, group]
            onward = (kept[1].astype(F32) + got[1].astype(F32)).astype(BF16)
            passed = links.send(onward, ALONG_X + ALONG_Y - axis)
            sums.append(kept[0].astype(F32) + got[0].astype(F32) + passed.astype(F32))
        return jnp.concatenate(sums)

    def ring_sum(value, moving):
        if moving is None:
            return value
        return value + links.send(moving.astype(BF16), ALONG_Z).astype(F32)

    bias_grad = precise_dot(bucket_hot.T, offset_grad.T)
    gain_rows = jnp.concatenate([gain_one, gain_two, gain_three]).reshape(-1, width)
    bias_row = jnp.pad(bias_grad.reshape(1, -1), ((0, 0), (0, width - BUCKETS * heads)))
    small_links = Links(devices)
    small = Chain(small_links, total_of(small_links, jnp.concatenate([gain_rows, bias_row])))

    moving = None
    events = []

    def event(rz=None):
        events.append(links.sent[ALONG_X][-1])

    later_units = after(own_units, near_sums(own_units, line - 1))
    event()
    strays.step()
    for rz in range(line - 2, -1, -1):
        near_sums(later_units, rz)
        event()
        if rz == line - 2:
            strays.step(events[-2])
        value = far_sums(rz + 1)
        event()
        if rz == line - 2:
            strays.step(events[-2])
        moving = ring_sum(value, moving)
    value = far_sums(0)
    event()
    links.windows = None
    strays.step(events[-1])
    strays.step(events[-1])
    small.step(events[-1])
    own_grads = ring_sum(value, moving)
    stray_found = [part for half in strays.finish() for part in half]
    small_total = small.finish()

    def extra_grads():
        return lax.psum(own_units[4 * line * own :].astype(F32), "dp").astype(BF16)

    extra_grad = lax.cond(many, extra_grads, no_extra)

    stray_found = jnp.concatenate([part.reshape(-1, UROWS + STRAY_TILE, width) for part in stray_found])
    shift = jnp.bitwise_xor(my_stray, me)
    stray_rz = (ring_place(me // 4, line) - ring_place(my_stray // 4, line) + line) % line
    stray_x, stray_y = jnp.bitwise_and(shift, 1), jnp.bitwise_and(shift // 2, 1)
    is_even = stray_rz % 2 == 0
    far_bit, near_bit = jnp.where(is_even, stray_y, stray_x), jnp.where(is_even, stray_x, stray_y)
    stray_place = (((stray_rz % 2) * 2 + far_bit) * 2 + near_bit) * (line // 2) + stray_rz // 2
    picks = jnp.concatenate(
        [
            jnp.where(my_stray >= 0, 1, jnp.where(my_extra >= 0, 2, 0)),
            jnp.where(my_stray >= 0, stray_place, 0),
            jnp.maximum(my_extra, 0),
        ]
    ).astype(jnp.int32)

    def slot_spec(first):
        return pl.BlockSpec((1, UROWS, width), lambda i, pick: (first + i, 0, 0))

    stack_shape = unit_weight.shape
    update_shapes = [like(stack_shape)] * 3 + [like(stack_shape, BF16)]
    partial_update = pl.pallas_call(
        stray_update_kernel,
        grid_spec=pltpu.PrefetchScalarGridSpec(
            num_scalar_prefetch=1,
            grid=(spare,),
            in_specs=[slot_spec(own)] * 3
            + [
                pl.BlockSpec((1, UROWS, width), lambda i, pick: (pick[spare + i], 0, 0)),
                pl.BlockSpec((1, UROWS, width), lambda i, pick: (pick[2 * spare + i], 0, 0)),
            ],
            out_specs=[slot_spec(own)] * 4,
        ),
        out_shape=update_shapes,
        compiler_params=params(32),
        cost_estimate=timed(5),
    )(picks, unit_weight, unit_first, unit_second, stray_found, extra_grad)
    unit_weights, unit_firsts, unit_seconds, unit_copies = pl.pallas_call(
        own_update_kernel,
        grid_spec=pltpu.PrefetchScalarGridSpec(
            num_scalar_prefetch=1,
            grid=(own,),
            in_specs=[slot_spec(0)] * 4 + [ANY] * 4,
            out_specs=[slot_spec(0)] * 4,
        ),
        out_shape=update_shapes,
        input_output_aliases={5: 0, 6: 1, 7: 2, 8: 3},
        compiler_params=params(32),
        cost_estimate=timed(4),
    )(my_count, unit_weight, unit_first, unit_second, own_grads, *partial_update)

    proj_total = pl.pallas_call(
        functools.partial(order_rows_kernel, devices),
        out_shape=like((devices, STRAY_TILE, width)),
        in_specs=[SMEM, VMEM],
        compiler_params=params(32),
        cost_estimate=timed(1),
    )(where, stray_found[:, UROWS:])
    proj_total = proj_total[:, :share].reshape(devices * share, width)[: proj_width * D // width]
    proj_total = proj_total.reshape(2, proj_width, D // 2).transpose(0, 2, 1).reshape(D, proj_width)
    gain_total = small_total[: gain_rows.shape[0]].reshape(3, D)
    bias_total = small_total[gain_rows.shape[0], : BUCKETS * heads].reshape(BUCKETS, heads)
    gain_weights, gain_firsts, gain_seconds = adamw_step(
        gain_weight, gain_first, gain_second, gain_total, RATE_GAIN
    )
    bias_weights, bias_firsts, bias_seconds = adamw_step(
        bias_weight, bias_first, bias_second, bias_total, RATE_SMALL
    )
    proj_weights, proj_firsts, proj_seconds = adamw_step(
        proj_weight, proj_first, proj_second, proj_total, RATE_MATRIX
    )
    return (
        encoded,
        token_grad,
        unit_weights,
        unit_firsts,
        unit_seconds,
        unit_copies,
        gain_weights,
        gain_firsts,
        gain_seconds,
        bias_weights,
        bias_firsts,
        bias_seconds,
        proj_weights,
        proj_firsts,
        proj_seconds,
    )


def solution(mesh):
    in_specs = (
        P("dp", None),
        P("dp", "mp"),
        P("dp"),
        P(),
        P(),
        P("dp", None, "mp"),
        P("dp", None, "mp"),
        P("dp", None, "mp"),
        P(),
        P(),
        P(),
        P(None, "mp"),
        P(None, "mp"),
        P(None, "mp"),
        P(None, "mp"),
        P(None, "mp"),
        P(None, "mp"),
    )
    out_specs = (
        P("dp", "mp"),
        P("dp", None),
        P("dp", None, "mp"),
        P("dp", None, "mp"),
        P("dp", None, "mp"),
        P("dp", None, "mp"),
        P(),
        P(),
        P(),
        P(None, "mp"),
        P(None, "mp"),
        P(None, "mp"),
        P(None, "mp"),
        P(None, "mp"),
        P(None, "mp"),
    )
    return jax.shard_map(shards, mesh=mesh, in_specs=in_specs, out_specs=out_specs, check_vma=False)
```

```python
import functools

import jax
import jax.numpy as jnp
from jax import lax
from jax.experimental import pallas as pl
from jax.experimental.pallas import tpu as pltpu
from jax.sharding import PartitionSpec as P

D = 768
HEAD_DIM = 64
FF = 3072
BUCKETS = 32
SLOT = 512
UROWS = 128
STEP = 5
HALF = UROWS // 2

NORM_EPS = 1e-06
ADAM_EPS = 1e-08
BETA_ONE = 0.5
BETA_TWO = 0.5
DECAY = 0.01
RATE_MATRIX = 0.02
RATE_SMALL = 0.1
RATE_GAIN = 0.6
GELU_C = 0.7978845608
GELU_K = 0.044715
MASKED = -1000000000.0

ROWS = D // UROWS
BLOCKS = FF // D
SQUARES = 4 * ROWS
FRONT = 3 * ROWS
SPREAD = 2 * SLOT
STRAY_TILE = 16
WINDOWS = 2, 2, 3
BACK_WINDOWS = 3, 3, 4
ALONG_X, ALONG_Y, ALONG_Z = 0, 1, 2
F32 = jnp.float32
BF16 = jnp.bfloat16
ANY = pl.BlockSpec(memory_space=pl.ANY)
SMEM = pl.BlockSpec(memory_space=pltpu.SMEM)
VMEM = pl.BlockSpec(memory_space=pltpu.VMEM)
HBM = pl.BlockSpec(memory_space=pltpu.HBM)
PAIR = 2 * HEAD_DIM


def dot(left, right):
    return jnp.dot(left, right, preferred_element_type=F32)


def dot_nt(left, right):
    return lax.dot_general(left, right, (((1,), (1,)), ((), ())), preferred_element_type=F32)


def dot_tn(left, right):
    return lax.dot_general(left, right, (((0,), (0,)), ((), ())), preferred_element_type=F32)


def precise_dot(left, right):
    return jnp.dot(left, right, precision=lax.Precision.HIGHEST, preferred_element_type=F32)


def inverse_rms(values):
    return lax.rsqrt(jnp.mean(values * values, axis=-1, keepdims=True) + NORM_EPS)


def norm_back(values, inv_rms, gain_row, grad_in):
    weighted = grad_in * gain_row
    gain_grad = jnp.sum(grad_in * values * inv_rms, axis=0, keepdims=True)
    slope = jnp.mean(weighted * values, axis=-1, keepdims=True)
    values_grad = inv_rms * weighted - values * (inv_rms * inv_rms * inv_rms) * slope
    return values_grad, gain_grad


def adamw_step(weight_now, first_now, second_now, grad_in, rate):
    first_new = BETA_ONE * first_now + (1.0 - BETA_ONE) * grad_in
    second_new = BETA_TWO * second_now + (1.0 - BETA_TWO) * grad_in * grad_in
    first_hat = first_new / (1.0 - BETA_ONE**STEP)
    second_hat = second_new / (1.0 - BETA_TWO**STEP)
    weight_new = weight_now - rate * (
        first_hat / (jnp.sqrt(second_hat) + ADAM_EPS) + DECAY * weight_now
    )
    return weight_new, first_new, second_new


def params(limit_mib):
    return pltpu.CompilerParams(vmem_limit_bytes=limit_mib * 1024 * 1024)


def timed(micros):
    return pl.CostEstimate(flops=int(micros * 1.15e9), bytes_accessed=int(micros * 1e5), transcendentals=0)


def ring_order(line):
    return list(range(0, line, 2)) + list(range(line - 1 - line % 2, 0, -2))


def ring_place(z, line):
    return jnp.where(z % 2 == 0, z // 2, line - (z + 1) // 2)


def ring_device(place, line):
    return jnp.where(2 * place < line, 2 * place, 2 * (line - place) - 1)


def hops(devices):
    line = devices // 4
    order = ring_order(line)
    after = {order[i]: order[(i + 1) % line] for i in range(line)}
    along_x = [(i, i ^ 1) for i in range(devices)]
    along_y = [(i, i ^ 2) for i in range(devices)]
    along_z = [(i, after[i // 4] * 4 + i % 4) for i in range(devices)]
    return along_x, along_y, along_z


def swap(values):
    return lax.ppermute(values, "mp", [(0, 1), (1, 0)])


def rest_place(unit):
    inner = unit - SQUARES
    matrix = inner // (ROWS * BLOCKS)
    rest = inner % (ROWS * BLOCKS)
    wide = ROWS + matrix * ROWS * BLOCKS + (rest % BLOCKS) * ROWS + rest // BLOCKS
    return jnp.where(unit < SQUARES, unit - FRONT, wide)


def after(values, other):
    return lax.optimization_barrier((values, other))[0]


class Links:
    def __init__(self, devices, *windows):
        self.pairs = hops(devices)
        self.sent = ([], [], [])
        self.windows = windows
        self.gate = None

    def settle(self, values):
        return values if self.gate is None else after(values, self.gate)

    def send(self, values, axis, steps=1):
        queue = self.sent[axis]
        window = self.windows[axis] if self.windows else len(queue) + 1
        if len(queue) >= window:
            values = after(values, queue[-window])
        step = dict(self.pairs[axis])
        reach = dict(step)
        for _ in range(steps - 1):
            reach = {i: step[j] for i, j in reach.items()}
        queue.append(lax.ppermute(values, "dp", sorted(reach.items())))
        return queue[-1]


def strays_kernel(own, most, devices, where_ref, index_ref, weight_ref, *refs):
    line = devices // 4
    *outs, stage, sem = refs
    load = pltpu.make_async_copy(weight_ref.at[own:most], stage, sem)
    load.start()
    for out in outs:
        out[...] = jnp.zeros_like(out)
    load.wait()
    me = where_ref[0]
    for j in range(most - own):
        home = index_ref[j]

        @pl.when(home >= 0)
        def _():
            rel = jnp.bitwise_xor(home, me)
            rx = jnp.bitwise_and(rel, 1)
            ry = jnp.bitwise_and(rel // 2, 1)
            rz = (ring_place(home // 4, line) - ring_place(me // 4, line) + line) % line
            unit = stage[j].astype(BF16)
            for odd, (near, far) in enumerate(((rx, ry), (ry, rx))):
                for sent in range(2):

                    @pl.when(jnp.logical_and(rz % 2 == odd, near == sent))
                    def _():
                        outs[2 * odd + sent][far, rz // 2] = unit


def gather_units(own, devices, layout, where_ref, table_ref, pieces, extra_ref, stack, front_sem, rest_sem):
    line = devices // 4
    me = where_ref[0]
    slots = own + 1

    def fetch(source, place):
        @pl.when(place < FRONT)
        def _():
            pltpu.make_async_copy(source, stack.at[place], front_sem).start()

        @pl.when(place >= FRONT)
        def _():
            pltpu.make_async_copy(source, stack.at[place], rest_sem).start()

    for piece, spots in zip(pieces, layout):
        for i, (rx, ry, rz, slot) in enumerate(spots):
            z = ring_device((ring_place(me // 4, line) - rz + line) % line, line)
            other = z * 4 + jnp.bitwise_xor(me % 4, 2 * ry + rx)
            fetch(piece.at[i], table_ref[other * slots + slot])

    @pl.loop(0, where_ref[1])
    def _(i):
        fetch(extra_ref.at[i], table_ref[devices * slots + i])


def wait_units(stack, total, sem):
    while total > 0:
        step = min(stack.shape[0], total)
        pltpu.make_async_copy(stack.at[0:step], stack.at[0:step], sem).wait()
        total -= step


def put_units(dest_ref, first_unit, stage, own_ref, stray_ref, sem):
    for i, unit in enumerate(first_unit):
        dest = dest_ref[unit]

        @pl.when(dest >= 0)
        def _():
            pltpu.make_async_copy(stage.at[i], own_ref.at[dest], sem).start()

        @pl.when(dest < 0)
        def _():
            pltpu.make_async_copy(stage.at[i], stray_ref.at[-1 - dest, :UROWS], sem).start()


def toeplitz(row):
    width = SPREAD
    tile = jnp.broadcast_to(pltpu.roll(row, width - (SLOT - 1), 1), (8, width))
    places = lax.broadcasted_iota(jnp.int32, (8, width), 0)
    for bit in (1, 2, 4):
        tile = jnp.where(jnp.bitwise_and(places, bit) != 0, pltpu.roll(tile, bit, 1), tile)
    reach = 8
    while reach < SLOT // 2:
        tile = jnp.concatenate([tile, pltpu.roll(tile, reach, 1)], axis=0)
        reach *= 2
    lower = jnp.concatenate([tile[:, width - reach :], tile[:, : SLOT - reach]], axis=1)
    return jnp.concatenate([tile[:, :SLOT], lower], axis=0)


def diagonals(tile):
    rows = SLOT
    while rows > 128:
        rows //= 2
        blank = jnp.zeros((rows, rows), F32)
        tile = jnp.concatenate([tile[rows:], blank], axis=1) + jnp.concatenate(
            [blank, tile[:rows]], axis=1
        )
    tile = jnp.concatenate([tile, jnp.zeros((rows, SPREAD - tile.shape[1]), F32)], axis=1)
    while rows > 8:
        rows //= 2
        tile = tile[rows:] + pltpu.roll(tile[:rows], rows, 1)
    places = lax.broadcasted_iota(jnp.int32, tile.shape, 0)
    for bit in (4, 2, 1):
        tile = jnp.where(jnp.bitwise_and(places, bit) == 0, pltpu.roll(tile, bit, 1), tile)
    return jnp.sum(tile, axis=0, keepdims=True)


def matrix(ref, first):
    return ref[first : first + ROWS].reshape(D, ref.shape[2])


def pair_columns(ref, step):
    return ref[:, pl.ds(pl.multiple_of(step * PAIR, PAIR), PAIR)]


def attend_kernel(own, devices, layout, lengths_ref, where_ref, table_ref, tokens_ref, gain_ref, bias_ref, extra_ref, *refs):
    pieces = refs[: len(layout)]
    norm_ref, query_ref, key_ref, value_ref, prob_ref, mixed_ref, front_ref, rest_ref = refs[len(layout) : -5]
    stack, front_sem, rest_sem, front_out, rest_out = refs[-5:]
    step = pl.program_id(0)
    front_copy = pltpu.make_async_copy(stack.at[:FRONT], front_ref, front_out)
    rest_copy = pltpu.make_async_copy(stack.at[FRONT:], rest_ref, rest_out)

    @pl.when(step == 0)
    def _():
        gather_units(
            own, devices, layout, where_ref, table_ref, pieces, extra_ref, stack, front_sem, rest_sem
        )
        inputs = tokens_ref[...].astype(F32)
        normed = (inputs * inverse_rms(inputs) * gain_ref[0:1, :]).astype(BF16)
        norm_ref[...] = normed
        wait_units(stack, FRONT, front_sem)
        front_copy.start()
        query_ref[...] = dot(normed, matrix(stack, 0)).astype(BF16)
        key_ref[...] = dot(normed, matrix(stack, ROWS)).astype(BF16)
        value_ref[...] = dot(normed, matrix(stack, 2 * ROWS)).astype(BF16)
        wait_units(stack, devices * own - FRONT, rest_sem)

        @pl.loop(0, where_ref[1])
        def _(i):
            wait_units(stack, 1, rest_sem)

        rest_copy.start()

    @pl.when(step == pl.num_programs(0) - 1)
    def _():
        front_copy.wait()
        rest_copy.wait()

    queries = pair_columns(query_ref, step)
    keys = pair_columns(key_ref, step)
    values = pair_columns(value_ref, step)
    lanes = lax.broadcasted_iota(jnp.int32, (SLOT, PAIR), 1) // HEAD_DIM
    seen = lax.broadcasted_iota(jnp.int32, (1, SLOT), 1) < lengths_ref[0]
    mixes = []
    for which in range(2):
        scores = dot_nt(jnp.where(lanes == which, queries, jnp.zeros_like(queries)), keys)
        scores = scores + toeplitz(bias_ref[pl.ds(2 * step + which, 1), :])
        scores = jnp.where(seen, scores, MASKED)
        powers = jnp.exp(scores - jnp.max(scores, axis=-1, keepdims=True))
        probabilities = powers * (1.0 / jnp.sum(powers, axis=-1, keepdims=True))
        prob_ref[which] = probabilities
        mixes.append(dot(probabilities.astype(BF16), values))
    mixed = jnp.where(lanes == 0, mixes[0], mixes[1]).astype(BF16)
    mixed_ref[:, pl.ds(pl.multiple_of(step * PAIR, PAIR), PAIR)] = mixed


def out_kernel(own, devices, where_ref, table_ref, mixed_ref, rest_in, *refs):
    line = devices // 4
    *pieces, part_ref, rest_ref, stage, weight, stage_sem, weight_sem, put_sem = refs
    me = where_ref[0]
    load = pltpu.make_async_copy(rest_in.at[0:ROWS], weight, weight_sem)
    load.start()
    for rz in range(line):
        pltpu.make_async_copy(pieces[rz], stage.at[4 * rz : 4 * rz + 4], stage_sem).start()
    load.wait()
    pltpu.make_async_copy(stage, stage, stage_sem).wait()
    for rz in range(line):
        z = ring_device((ring_place(me // 4, line) - rz + line) % line, line)
        for near in range(4):
            other = z * 4 + jnp.bitwise_xor(me % 4, near)
            place = table_ref[other * (own + 1) + own] - FRONT
            i = 4 * rz + near
            pltpu.make_async_copy(stage.at[i], rest_ref.at[place], put_sem).start()

            @pl.when(place < ROWS)
            def _():
                weight[place] = stage[i]

    part_ref[...] = dot_nt(mixed_ref[...], matrix(weight, 0)).astype(BF16)
    pltpu.make_async_copy(stage, stage, put_sem).wait()


def both(mine_ref, other_ref):
    return mine_ref[...].astype(F32) + other_ref[...].astype(F32)


def gelu_tanh(values):
    return jnp.tanh(GELU_C * (values + GELU_K * values * values * values))


def feed_kernel(
    tokens_ref, mine_ref, other_ref, gain_ref, gate_w, up_w, down_w,
    residual_ref, norm_ref, gate_ref, up_ref, hidden_ref, part_ref, sum_ref,
):
    step = pl.program_id(0)

    @pl.when(step == 0)
    def _():
        residual = tokens_ref[...].astype(F32) + both(mine_ref, other_ref)
        residual_ref[...] = residual
        norm_ref[...] = (residual * inverse_rms(residual) * gain_ref[1:2, :]).astype(BF16)
        sum_ref[...] = jnp.zeros_like(sum_ref)

    normed = norm_ref[...]
    gate = dot(normed, matrix(gate_w, 0))
    up = dot(normed, matrix(up_w, 0))
    gate_ref[...] = gate
    up_ref[...] = up
    hidden = (0.5 * gate * (1.0 + gelu_tanh(gate)) * up).astype(BF16)
    hidden_ref[...] = hidden
    sum_ref[...] += dot_nt(hidden, matrix(down_w, 0))

    @pl.when(step == pl.num_programs(0) - 1)
    def _():
        part_ref[...] = sum_ref[...].astype(BF16)


def turn_kernel(
    lengths_ref, residual_ref, mine_ref, other_ref, gain_ref, proj_ref, proj_other, cot_ref, cot_other,
    gate_ref, up_ref, gate_w, up_w, down_w,
    encoded_ref, proj_grad, gain_grad, grad_ref, feed_ref, dgate_ref, dup_ref, part_ref, sum_ref,
):
    step = pl.program_id(0)

    @pl.when(step == 0)
    def _():
        residual = residual_ref[...] + both(mine_ref, other_ref)
        inv_rms = inverse_rms(residual)
        normed = (residual * inv_rms * gain_ref[2:3, :]).astype(BF16)
        encoded_ref[...] = dot(normed, proj_ref[...])
        rows = lax.broadcasted_iota(jnp.int32, (SLOT, 1), 0) < lengths_ref[0]
        mine = jnp.where(rows, cot_ref[...], jnp.zeros_like(cot_ref))
        other = jnp.where(rows, cot_other[...], jnp.zeros_like(cot_other))
        backward = dot_tn(mine, normed)
        proj_grad[0] = backward[:, : D // 2]
        proj_grad[1] = backward[:, D // 2 :]
        third = dot_nt(mine, proj_ref[...]) + dot_nt(other, proj_other[...])
        grad, gain = norm_back(residual, inv_rms, gain_ref[2:3, :], third)
        gain_grad[...] = gain
        grad_ref[...] = grad
        feed_ref[...] = grad.astype(BF16)
        sum_ref[...] = jnp.zeros_like(sum_ref)

    dhidden = dot(feed_ref[...], matrix(down_w, 0))
    gate = gate_ref[...]
    bend = gelu_tanh(gate)
    slope = 0.5 * (1.0 + bend) + 0.5 * gate * (1.0 - bend * bend) * (
        GELU_C * (1.0 + 3.0 * GELU_K * gate * gate)
    )
    dgate = (dhidden * up_ref[...] * slope).astype(BF16)
    dup = (dhidden * (0.5 * gate * (1.0 + bend))).astype(BF16)
    dgate_ref[...] = dgate
    dup_ref[...] = dup
    sum_ref[...] += dot_nt(dgate, matrix(gate_w, 0)) + dot_nt(dup, matrix(up_w, 0))

    @pl.when(step == pl.num_programs(0) - 1)
    def _():
        part_ref[...] = sum_ref[...].astype(BF16)


def wide_grads_kernel(
    units, dest_ref, norm_ref, feed_ref, hidden_ref, dgate_ref, dup_ref, own_ref, stray_ref, stage, sems
):
    step = pl.program_id(0)
    slot = step % 2
    shape = (ROWS,) + stage.shape[2:]

    def settle(which):
        pltpu.make_async_copy(stage.at[which], stage.at[which], sems.at[which]).wait()

    @pl.when(step >= 2)
    def _():
        settle(slot)

    normed = norm_ref[...]
    stage[slot, 0:ROWS] = dot_tn(normed, dgate_ref[...]).astype(BF16).reshape(shape)
    stage[slot, ROWS : 2 * ROWS] = dot_tn(normed, dup_ref[...]).astype(BF16).reshape(shape)
    stage[slot, 2 * ROWS :] = dot_tn(feed_ref[...], hidden_ref[...]).astype(BF16).reshape(shape)
    names = [
        SQUARES + which * ROWS * BLOCKS + row * BLOCKS + step for which in range(3) for row in range(ROWS)
    ]
    put_units(dest_ref, names, stage.at[slot], own_ref, stray_ref, sems.at[slot])

    @pl.when(step == pl.num_programs(0) - 1)
    def _():
        settle(1 - slot)
        settle(slot)


def enter_back_kernel(
    dest_ref, home_ref, grad_ref, residual_ref, mine_ref, other_ref, gain_ref, weight_ref, mixed_ref,
    proj_ref, own_in, stray_in,
    grad_one, gain_grad, dmixed_ref, own_ref, stray_ref, stage, sem, proj_sem,
):
    for home in range(proj_ref.shape[0]):
        pltpu.make_async_copy(
            proj_ref.at[home], stray_ref.at[home_ref[home], UROWS:], proj_sem
        ).start()
    residual = residual_ref[...]
    second = both(mine_ref, other_ref)
    back, gain = norm_back(residual, inverse_rms(residual), gain_ref[1:2, :], second)
    gain_grad[...] = gain
    total = grad_ref[...] + back
    grad_one[...] = total
    lowered = total.astype(BF16)
    stage[...] = dot_tn(lowered, mixed_ref[...]).astype(BF16).reshape(stage.shape)
    put_units(dest_ref, range(FRONT, SQUARES), stage, own_ref, stray_ref, sem)
    dmixed_ref[...] = dot(lowered, matrix(weight_ref, 0)).astype(BF16)
    pltpu.make_async_copy(stage, stage, sem).wait()
    pltpu.make_async_copy(proj_ref, proj_ref, proj_sem).wait()


def attend_back_kernel(
    dmixed_ref, query_ref, key_ref, value_ref, prob_ref, dquery_ref, dkey_ref, dvalue_ref, offset_ref
):
    queries, keys, values, dmixed = query_ref[...], key_ref[...], value_ref[...], dmixed_ref[...]
    lanes = lax.broadcasted_iota(jnp.int32, (SLOT, PAIR), 1) // HEAD_DIM
    parts = []
    for which in range(2):
        dprob = dot_nt(jnp.where(lanes == which, dmixed, jnp.zeros_like(dmixed)), values)
        probabilities = prob_ref[which]
        share = jnp.sum(probabilities * dprob, axis=-1, keepdims=True)
        dscore = (probabilities * (dprob - share)).astype(BF16)
        parts.append(
            (
                dot(dscore, keys),
                dot_tn(dscore, queries),
                dot_tn(probabilities.astype(BF16), dmixed),
            )
        )
        offset_ref[0, which : which + 1, :] = diagonals(dscore.astype(F32))
    for out, first, second in zip((dquery_ref, dkey_ref, dvalue_ref), *parts):
        out[...] = jnp.where(lanes == 0, first, second).astype(BF16)


def joined(refs):
    return jnp.concatenate([ref[...] for ref in refs], axis=1)


def first_grad_kernel(weight_ref, *refs):
    *parts, out_ref = refs
    width = len(parts) // 3
    total = 0.0
    for i in range(3):
        total = total + dot_nt(joined(parts[i * width : (i + 1) * width]), matrix(weight_ref, i * ROWS))
    out_ref[...] = total.astype(BF16)


def front_grads_kernel(dest_ref, norm_ref, *refs):
    *parts, own_in, own_ref, stage, sem = refs
    width = len(parts) // 3
    normed = norm_ref[...]
    shape = (ROWS,) + stage.shape[1:]
    for i in range(3):
        first = i * ROWS
        grads = joined(parts[i * width : (i + 1) * width])
        stage[first : first + ROWS] = dot_tn(normed, grads).astype(BF16).reshape(shape)
        for unit in range(first, first + ROWS):
            pltpu.make_async_copy(stage.at[unit], own_ref.at[dest_ref[unit]], sem).start()
    pltpu.make_async_copy(stage, stage, sem).wait()


def token_grad_kernel(tokens_ref, grad_ref, mine_ref, other_ref, gain_ref, out_ref, gain_grad):
    inputs = tokens_ref[...].astype(F32)
    first = both(mine_ref, other_ref)
    back, gain = norm_back(inputs, inverse_rms(inputs), gain_ref[0:1, :], first)
    out_ref[...] = grad_ref[...] + back
    gain_grad[...] = gain


def order_rows_kernel(devices, where_ref, found_ref, out_ref):
    line = devices // 4
    me = where_ref[0]
    for rz in range(line):
        z = ring_device((ring_place(me // 4, line) - rz + line) % line, line)
        for far in range(2):
            for near in range(2):
                rx, ry = (far, near) if rz % 2 else (near, far)
                other = z * 4 + jnp.bitwise_xor(me % 4, 2 * ry + rx)
                place = ((rz % 2 * 2 + far) * 2 + near) * (line // 2) + rz // 2
                out_ref[other] = found_ref[place].astype(F32)


def stray_update_kernel(pick_ref, weight, first, second, stray, extra, *refs):
    kind = pick_ref[pl.program_id(0)]
    grad = jnp.where(kind == 1, stray[0].astype(F32), extra[0].astype(F32))
    grad = jnp.where(kind == 0, 0.0, grad)
    update_slot(weight, first, second, grad, refs[-4:])


def update_slot(weight, first, second, grad, outs):
    new_weight, new_first, new_second = adamw_step(
        weight[0], first[0], second[0], grad, RATE_MATRIX
    )
    outs[0][0] = new_weight
    outs[1][0] = new_first
    outs[2][0] = new_second
    outs[3][0] = new_weight.astype(BF16)


def own_update_kernel(count_ref, weight, first, second, grad_ref, *refs):
    grad = jnp.where(pl.program_id(0) < count_ref[0], grad_ref[0], 0.0)
    update_slot(weight, first, second, grad, refs[-4:])


def shards(
    tokens,
    out_grad,
    doc_lengths,
    owner_list,
    bucket_table,
    unit_weight,
    unit_first,
    unit_second,
    gain_weight,
    gain_first,
    gain_second,
    bias_weight,
    bias_first,
    bias_second,
    proj_weight,
    proj_first,
    proj_second,
):
    most, _, width = unit_weight.shape
    heads = bias_weight.shape[1]
    count = tokens.shape[0]
    units = owner_list.shape[0]
    proj_width = proj_weight.shape[1]
    devices = lax.axis_size("dp")
    line = devices // 4
    own = max(1, (units - 1) // devices)
    slots = own + 1
    spare = most - own
    me = lax.axis_index("dp").astype(jnp.int32)

    def like(shape, kind=F32):
        return jax.ShapeDtypeStruct(shape, kind)

    full, left = divmod(units, most)
    extra_count = max(FRONT, full * spare + max(0, left - own) - devices)
    indices = jnp.arange(units, dtype=jnp.int32)
    before = indices[None, :] < indices[:, None]
    same = owner_list[:, None] == owner_list[None, :]
    rank = jnp.sum((same & before).astype(jnp.int32), axis=1)
    is_over = rank >= own
    may_stray = is_over & (indices >= FRONT)
    stray_index = jnp.sum((before & may_stray[None, :]).astype(jnp.int32), axis=1)
    is_stray = may_stray & (stray_index < devices)
    is_extra = is_over & ~is_stray
    extra_index = jnp.sum((before & is_extra[None, :]).astype(jnp.int32), axis=1)
    extra_total = jnp.sum(is_extra.astype(jnp.int32))
    many = extra_total > 0
    position = jnp.where(
        is_stray,
        stray_index * slots + own,
        jnp.where(is_extra, devices * slots + extra_index, owner_list * slots + rank),
    )
    position_ids = jnp.arange(devices * slots + extra_count, dtype=jnp.int32)
    hit = position[None, :] == position_ids[:, None]
    placed = jnp.where(indices < FRONT, indices, FRONT + rest_place(indices))
    table = units + jnp.sum(jnp.where(hit, placed[None, :] - units, 0), axis=1).astype(jnp.int32)
    spare_ids = jnp.arange(spare, dtype=jnp.int32)
    my_over = (owner_list[None, :] == me) & (rank[None, :] == own + spare_ids[:, None])
    my_stray = jnp.sum(jnp.where(my_over & is_stray[None, :], stray_index[None, :] + 1, 0), axis=1) - 1
    my_extra = jnp.sum(jnp.where(my_over & is_extra[None, :], extra_index[None, :] + 1, 0), axis=1) - 1
    my_count = jnp.sum((owner_list == me).astype(jnp.int32)).reshape(1)
    where = jnp.stack([me, extra_total]).astype(jnp.int32)

    home = jnp.where(is_stray, stray_index, owner_list)
    rel_x = jnp.bitwise_and(jnp.bitwise_xor(home, me), 1)
    rel_y = jnp.bitwise_and(jnp.bitwise_xor(home, me) // 2, 1)
    rel_z = (ring_place(home // 4, line) - ring_place(me // 4, line) + line) % line
    cut = (own + 1) // 2
    spans = [(0, cut), (cut, own)] if own > cut else [(0, cut)]
    even = rel_z % 2 == 0
    in_first = rank < cut
    near_is_x = even == in_first
    corner = jnp.where(near_is_x, rel_x, rel_y) * 2 + jnp.where(near_is_x, rel_y, rel_x)
    own_dest = rel_z * 4 * own + jnp.where(
        in_first, corner * cut + rank, 4 * cut + corner * (own - cut) + rank - cut
    )

    def stray_dest_of(x, y, z):
        even = z % 2 == 0
        corner = jnp.where(even, x, y) * 2 + jnp.where(even, y, x)
        return (jnp.where(even, 0, 2 * line) + corner * (line // 2) + z // 2).astype(jnp.int32)

    stray_dest = stray_dest_of(rel_x, rel_y, rel_z)
    homes = jnp.arange(devices, dtype=jnp.int32)
    home_dest = stray_dest_of(
        jnp.bitwise_and(jnp.bitwise_xor(homes, me), 1),
        jnp.bitwise_and(jnp.bitwise_xor(homes, me) // 2, 1),
        (ring_place(homes // 4, line) - ring_place(me // 4, line) + line) % line,
    )
    dest = jnp.where(
        is_stray,
        -1 - stray_dest,
        jnp.where(is_extra, 4 * line * own + extra_index, own_dest),
    ).astype(jnp.int32)

    extra_shape = (extra_count, UROWS, width)

    def extra_weights():
        wanted = jnp.arange(extra_count, dtype=jnp.int32)[:, None] == my_extra[None, :]
        taken = jnp.take(unit_weight[own:], jnp.argmax(wanted, axis=1), axis=0)
        return lax.psum(jnp.where(jnp.any(wanted, axis=1)[:, None, None], taken, 0.0), "dp").astype(BF16)

    def no_extra():
        return jnp.zeros(extra_shape, BF16)

    extra = lax.cond(many, extra_weights, no_extra)

    def sum_strays(links, keep_a, send_a, keep_b, send_b):
        from_x = links.send(send_a, ALONG_X)
        from_y = links.send(send_b, ALONG_Y)
        yield
        from_x, from_y = links.settle(from_x), links.settle(from_y)
        low_y = links.send((keep_a[1].astype(F32) + from_x[1].astype(F32)).astype(BF16), ALONG_Y)
        high_x = links.send((keep_b[1].astype(F32) + from_y[1].astype(F32)).astype(BF16), ALONG_X)
        yield
        low_y, high_x = links.settle(low_y), links.settle(high_x)
        low = keep_a[0].astype(F32) + from_x[0].astype(F32) + low_y.astype(F32)
        high = keep_b[0].astype(F32) + from_y[0].astype(F32) + high_x.astype(F32)
        sums = [(high if rz % 2 else low)[rz // 2] for rz in range(line)]
        total = sums[0]
        terms = [links.send(sums[rz].astype(BF16), ALONG_Z, rz) for rz in range(1, line)]
        yield
        for term in terms:
            total = total + links.settle(term).astype(F32)
        return total.astype(BF16)

    def gather_strays(links, unit):
        got = links.send(unit, ALONG_X)
        yield
        near = jnp.stack([unit, links.settle(got)])
        got = links.send(near, ALONG_Y)
        yield
        near = jnp.concatenate([near, links.settle(got)])
        found = [near]
        for _ in range(line - 1):
            found.append(links.send(found[-1], ALONG_Z))
            yield
            found[-1] = links.settle(found[-1])
        return found

    def stray_chain(links, *arrays):
        unit = yield from sum_strays(links, *arrays)
        return (yield from gather_strays(links, unit))

    class Chain:
        def __init__(self, links, steps):
            self.links, self.steps, self.value = links, steps, None

        def step(self, gate=None):
            self.links.gate = gate
            try:
                if self.value is None:
                    next(self.steps)
            except StopIteration as end:
                self.value = end.value

        def finish(self):
            while self.value is None:
                self.step()
            return self.value

    proj_low = proj_weight.astype(BF16)
    proj_other = swap(proj_low)
    cot_other = swap(out_grad)

    links = Links(devices, *WINDOWS)
    rings = [[unit_weight[first:last].astype(BF16)] for first, last in spans]
    pieces, layout, rounds = [], [], {}

    def ring_step():
        for ring in rings:
            ring.append(links.send(ring[-1], ALONG_Z))

    def keep(values, rx, ry, spots):
        pieces.append(values)
        layout.append([(rx, ry, rz, slot) for rz, slot in spots])

    def near_round(pair):
        for i, axis in enumerate((ALONG_X, ALONG_Y)):
            parts, spots = [], []
            for rz in (2 * pair, 2 * pair + 1):
                which = (i + rz) % 2
                if which < len(rings):
                    parts.append(rings[which][rz])
                    spots += [(rz, slot) for slot in range(*spans[which])]
            if parts:
                values = jnp.concatenate(parts) if len(parts) > 1 else parts[0]
                rounds[pair, axis] = values, spots, links.send(values, axis)

    def far_direct(pair):
        for axis in (ALONG_X, ALONG_Y):
            if (pair, axis) in rounds:
                values, spots, got = rounds[pair, axis]
                other = ALONG_X + ALONG_Y - axis
                keep(values, 0, 0, spots)
                keep(got, int(axis == ALONG_X), int(axis == ALONG_Y), spots)
                keep(links.send(values, other), int(axis == ALONG_Y), int(axis == ALONG_X), spots)

    def far_through(pair):
        for axis in (ALONG_X, ALONG_Y):
            if (pair, axis) in rounds:
                values, spots, got = rounds[pair, axis]
                keep(links.send(got, ALONG_X + ALONG_Y - axis), 1, 1, spots)

    ring_step()
    near_shape = like((2, line // 2, UROWS, width), BF16)
    stray_parts = pl.pallas_call(
        functools.partial(strays_kernel, own, most, devices),
        out_shape=[near_shape] * 4,
        in_specs=[SMEM, SMEM, ANY],
        out_specs=[VMEM] * 4,
        scratch_shapes=[pltpu.VMEM((spare, UROWS, width), F32), pltpu.SemaphoreType.DMA],
        compiler_params=params(40),
        cost_estimate=timed(2),
    )(where, my_stray, unit_weight)
    strays = Chain(links, stray_chain(links, *stray_parts))
    strays.step()
    for pair in range(line // 2):
        while len(rings[0]) < 2 * pair + 2:
            ring_step()
        near_round(pair)
        if pair == 0:
            strays.step(rings[0][-1])
            first_near = links.sent[ALONG_Y][1]
            while len(rings[0]) < min(line, 3):
                ring_step()
            far_direct(pair)
            strays.step(first_near)
            if len(rings[0]) < line:
                ring_step()
            strays.step(links.sent[ALONG_X][-1])
            far_through(pair)
            strays.step(links.sent[ALONG_X][-2])
        else:
            strays.step(links.sent[ALONG_Y][-3])
            far_direct(pair)
            strays.step(links.sent[ALONG_Y][-3])
            far_through(pair)
    found = strays.finish()
    tokens, proj_other, cot_other = lax.optimization_barrier((tokens, proj_other, cot_other))

    bucket_hot = (bucket_table[:, None] == jnp.arange(BUCKETS, dtype=jnp.int32)[None, :]).astype(F32)
    bucket_hot = jnp.pad(bucket_hot, ((0, SPREAD - bucket_hot.shape[0]), (0, 0)))
    bias_rows = jnp.pad(precise_dot(bucket_hot, bias_weight).T, ((0, 8 - heads % 8), (0, 0)))
    def whole(shape):
        return pl.BlockSpec(shape, lambda i: (0,) * len(shape))

    wide_shape = (count, D)
    head_shape = (count, width)
    front_spec = whole((FRONT, UROWS, width))
    out_spec = pl.BlockSpec((ROWS, UROWS, width), lambda i: (0, 0, 0))
    prob_spec = pl.BlockSpec((2, SLOT, SLOT), lambda i: (i, 0, 0))
    gain_spec = whole((3, D))
    bias_spec = whole(bias_rows.shape)
    column_spec = pl.BlockSpec((count, width), lambda i: (0, i))

    def unit_spec(which):
        return pl.BlockSpec((ROWS, UROWS, width), lambda i: (1 + which * BLOCKS + i, 0, 0))

    wide_specs = [unit_spec(0), unit_spec(1), unit_spec(2)]

    stack_shape = (units + 1, UROWS, width)
    rest_shape = like((units + 1 - FRONT, UROWS, width), BF16)
    first_in, queries, keys, values, probabilities, mixed, front, rest = pl.pallas_call(
        functools.partial(attend_kernel, own, devices, layout),
        grid=(heads // 2,),
        in_specs=[SMEM] * 3 + [whole(wide_shape), gain_spec, bias_spec] + [ANY] * (1 + len(pieces)),
        out_specs=[whole(wide_shape)] + [whole(head_shape)] * 3 + [prob_spec, whole(head_shape), HBM, HBM],
        out_shape=[like(wide_shape, BF16)]
        + [like(head_shape, BF16)] * 3
        + [like((heads, SLOT, SLOT)), like(head_shape, BF16), like((FRONT, UROWS, width), BF16), rest_shape],
        scratch_shapes=[pltpu.VMEM(stack_shape, BF16)] + [pltpu.SemaphoreType.DMA] * 4,
        compiler_params=params(60),
        cost_estimate=timed(14),
    )(doc_lengths, where, table, tokens, gain_weight, bias_rows, extra, *pieces)
    attn_part, rest = pl.pallas_call(
        functools.partial(out_kernel, own, devices),
        grid=(1,),
        in_specs=[SMEM] * 2 + [whole(head_shape)] + [ANY] * (1 + line),
        out_specs=[whole(wide_shape), HBM],
        out_shape=[like(wide_shape, BF16), rest_shape],
        input_output_aliases={3: 1},
        scratch_shapes=[
            pltpu.VMEM((4 * line, UROWS, width), BF16),
            pltpu.VMEM((ROWS, UROWS, width), BF16),
        ]
        + [pltpu.SemaphoreType.DMA] * 3,
        compiler_params=params(56),
        cost_estimate=timed(4),
    )(where, table, mixed, rest, *found)

    residual_one, second_in, gate, up, hidden, feed_part = pl.pallas_call(
        feed_kernel,
        grid=(BLOCKS,),
        in_specs=[whole(wide_shape)] * 3 + [gain_spec] + wide_specs,
        out_specs=[whole(wide_shape)] * 2 + [column_spec] * 3 + [whole(wide_shape)],
        out_shape=[
            like(wide_shape),
            like(wide_shape, BF16),
            like((count, BLOCKS * width)),
            like((count, BLOCKS * width)),
            like((count, BLOCKS * width), BF16),
            like(wide_shape, BF16),
        ],
        scratch_shapes=[pltpu.VMEM(wide_shape, F32)],
        compiler_params=params(56),
        cost_estimate=timed(11),
    )(tokens, attn_part, swap(attn_part), gain_weight, rest, rest, rest)

    encoded, proj_grad, gain_three, grad_two, feed_grad, dgate, dup, second_part = pl.pallas_call(
        turn_kernel,
        grid=(BLOCKS,),
        in_specs=[SMEM]
        + [whole(wide_shape)] * 3
        + [gain_spec]
        + [whole((D, proj_width))] * 2
        + [whole((count, proj_width))] * 2
        + [column_spec] * 2
        + wide_specs,
        out_specs=[
            whole((count, proj_width)),
            whole((2, proj_width, D // 2)),
            whole((1, D)),
            whole(wide_shape),
            whole(wide_shape),
            column_spec,
            column_spec,
            whole(wide_shape),
        ],
        out_shape=[
            like((count, proj_width)),
            like((2, proj_width, D // 2)),
            like((1, D)),
            like(wide_shape),
            like(wide_shape, BF16),
            like((count, BLOCKS * width), BF16),
            like((count, BLOCKS * width), BF16),
            like(wide_shape, BF16),
        ],
        scratch_shapes=[pltpu.VMEM(wide_shape, F32)],
        compiler_params=params(56),
        cost_estimate=timed(14),
    )(
        doc_lengths, residual_one, feed_part, swap(feed_part), gain_weight, proj_low, proj_other,
        out_grad, cot_other, gate, up, rest, rest, rest,
    )

    own_shape = like((4 * line * own + extra_count, UROWS, width), BF16)
    stray_shape = like((4 * line, UROWS + STRAY_TILE, width), BF16)
    proj_rows = proj_grad.reshape(-1, width)
    share = -(-proj_rows.shape[0] // devices)
    proj_rows = jnp.pad(proj_rows, ((0, share * devices - proj_rows.shape[0]), (0, 0)))
    proj_rows = proj_rows.reshape(devices, share, width).astype(BF16)
    proj_rows = jnp.pad(proj_rows, ((0, 0), (0, STRAY_TILE - share), (0, 0)))
    own_units, stray_units = pl.pallas_call(
        functools.partial(wide_grads_kernel, units),
        grid=(BLOCKS,),
        in_specs=[SMEM] + [whole(wide_shape)] * 2 + [column_spec] * 3,
        out_specs=[HBM] * 2,
        out_shape=[own_shape, stray_shape],
        scratch_shapes=[
            pltpu.VMEM((2, 3 * ROWS, UROWS, width), BF16),
            pltpu.SemaphoreType.DMA((2,)),
        ],
        compiler_params=params(56),
        cost_estimate=timed(9),
    )(dest, second_in, feed_grad, hidden, dgate, dup)

    grad_one, gain_two, dmixed, own_units, stray_units = pl.pallas_call(
        enter_back_kernel,
        grid=(1,),
        in_specs=[SMEM] * 2
        + [whole(wide_shape)] * 4
        + [gain_spec, out_spec, whole(head_shape), whole(proj_rows.shape)]
        + [ANY] * 2,
        out_specs=[whole(wide_shape), whole((1, D)), whole(head_shape)] + [HBM] * 2,
        out_shape=[like(wide_shape), like((1, D)), like(head_shape, BF16), own_shape, stray_shape],
        input_output_aliases={10: 3, 11: 4},
        scratch_shapes=[pltpu.VMEM((ROWS, UROWS, width), BF16)] + [pltpu.SemaphoreType.DMA] * 2,
        compiler_params=params(56),
        cost_estimate=timed(6),
    )(
        dest, home_dest, grad_two, residual_one, second_part, swap(second_part), gain_weight, rest, mixed,
        proj_rows, own_units, stray_units,
    )

    links = Links(devices, *BACK_WINDOWS)
    by_near = stray_units.reshape(4, 2, line // 2, UROWS + STRAY_TILE, width)
    strays = Chain(links, sum_strays(links, *[by_near[i] for i in range(4)]))

    def attend_back(first, pairs, dmixed):
        pair_spec = pl.BlockSpec((count, PAIR), lambda i: (0, first + i))
        out_spec = pl.BlockSpec((count, PAIR), lambda i: (0, i))
        return pl.pallas_call(
            attend_back_kernel,
            grid=(pairs,),
            in_specs=[pair_spec] * 4 + [pl.BlockSpec((2, SLOT, SLOT), lambda i: (first + i, 0, 0))],
            out_specs=[out_spec] * 3 + [pl.BlockSpec((1, 8, SPREAD), lambda i: (i, 0, 0))],
            out_shape=[like((count, PAIR * pairs), BF16)] * 3 + [like((pairs, 8, SPREAD))],
            compiler_params=params(56),
            cost_estimate=timed(4.3 * pairs),
        )(dmixed, queries, keys, values, probabilities)

    pairs = heads // 2
    strays.step()
    singles = [attend_back(i, 1, dmixed) for i in range(pairs - 1)]
    grads_a = [joined_parts for joined_parts in singles[-1][:3]]
    strays.step()
    *grads_b, offsets_b = attend_back(pairs - 1, 1, after(dmixed, links.sent[ALONG_Y][0]))
    singles.append((*grads_b, offsets_b))
    head_grads = [single[i] for i in range(3) for single in singles]
    offset_grad = jnp.concatenate([single[3] for single in singles])[:, :2].reshape(heads, SPREAD)
    part_specs = [whole(part.shape) for part in head_grads]
    first_part = pl.pallas_call(
        first_grad_kernel,
        grid=(1,),
        in_specs=[front_spec] + part_specs,
        out_specs=whole(wide_shape),
        out_shape=like(wide_shape, BF16),
        compiler_params=params(56),
        cost_estimate=timed(2),
    )(front, *head_grads)

    own_units = pl.pallas_call(
        front_grads_kernel,
        grid=(1,),
        in_specs=[SMEM, whole(wide_shape)] + part_specs + [ANY],
        out_specs=HBM,
        out_shape=own_shape,
        input_output_aliases={2 + len(head_grads): 0},
        scratch_shapes=[pltpu.VMEM((FRONT, UROWS, width), BF16), pltpu.SemaphoreType.DMA],
        compiler_params=params(56),
        cost_estimate=timed(4),
    )(dest, first_in, *head_grads, own_units)

    token_grad, gain_one = pl.pallas_call(
        token_grad_kernel,
        out_shape=[like(wide_shape), like((1, D))],
        compiler_params=params(56),
        cost_estimate=timed(4),
    )(tokens, grad_one, first_part, swap(first_part), gain_weight)

    bias_grad = precise_dot(bucket_hot.T, offset_grad.T)
    gain_rows = jnp.concatenate([gain_one, gain_two, gain_three]).reshape(-1, width)
    bias_row = jnp.pad(bias_grad.reshape(1, -1), ((0, 0), (0, width - BUCKETS * heads)))
    small = jnp.concatenate([gain_rows, bias_row])
    small = jnp.pad(small, ((0, STRAY_TILE - small.shape[0]), (0, 0))).astype(BF16)
    tall = UROWS + STRAY_TILE

    halves = {}

    def near_sums(own_units, rz):
        first = 4 * rz * own
        for group, span in enumerate(spans):
            size = span[1] - span[0]
            axis = (ALONG_X, ALONG_Y)[(group + rz) % 2]
            shape = (2, size, UROWS, width)
            kept = own_units[first : first + 2 * size].reshape(shape)
            given = own_units[first + 2 * size : first + 4 * size].reshape(shape)
            halves[rz, group] = axis, kept, links.send(given, axis)
            first += 4 * size
        return given

    def far_sums(rz):
        sums = []
        for group in range(len(spans)):
            axis, kept, got = halves[rz, group]
            onward = (kept[1].astype(F32) + got[1].astype(F32)).astype(BF16)
            passed = links.send(onward, ALONG_X + ALONG_Y - axis)
            sums.append(kept[0].astype(F32) + got[0].astype(F32) + passed.astype(F32))
        return jnp.concatenate(sums).reshape(own * UROWS, width)

    own_units = after(after(own_units, links.sent[ALONG_X][-1]), links.sent[ALONG_Y][-1])
    strays.step()
    top = line - 1
    later_units = after(own_units, near_sums(own_units, top))
    rides = [jnp.concatenate([strays.finish(), small])]
    moving = None
    for rz in range(top, -1, -1):
        if rz:
            near_sums(later_units, rz - 1)
        value = far_sums(rz)
        if moving is not None:
            got = links.send(jnp.concatenate([moving.astype(BF16), rides[-1]]), ALONG_Z)
            rides.append(got[own * UROWS :])
            value = value + got[: own * UROWS].astype(F32)
        moving = value
    own_grads = moving.reshape(own, UROWS, width)

    terms = [ride[tall:].astype(F32) for ride in rides]
    while len(terms) > 1:
        middle = len(terms) // 2
        terms = [terms[i] + terms[middle + i] for i in range(middle)]
    low_rides = jnp.concatenate([ride[:tall] for ride in rides[0::2]] + [terms[0].astype(BF16)])
    high_rides = jnp.concatenate([ride[:tall] for ride in rides[1::2]])
    rows = line // 2 * tall
    low_got, high_got = links.send(low_rides, ALONG_X), links.send(high_rides, ALONG_Y)
    small_sum = (low_rides[rows:].astype(F32) + low_got[rows:].astype(F32)).astype(BF16)
    low_rides = jnp.concatenate([low_rides[:rows], low_got[:rows], small_sum])
    high_rides = jnp.concatenate([high_rides, high_got])
    low_got, high_got = links.send(low_rides, ALONG_Y), links.send(high_rides, ALONG_X)
    small_total = small_sum.astype(F32) + low_got[2 * rows :].astype(F32)
    stray_found = [low_rides[: 2 * rows], low_got[: 2 * rows], high_rides, high_got]

    def extra_grads():
        return lax.psum(own_units[4 * line * own :].astype(F32), "dp").astype(BF16)

    extra_grad = lax.cond(many, extra_grads, no_extra)

    stray_found = jnp.concatenate([part.reshape(-1, UROWS + STRAY_TILE, width) for part in stray_found])
    shift = jnp.bitwise_xor(my_stray, me)
    stray_rz = (ring_place(me // 4, line) - ring_place(my_stray // 4, line) + line) % line
    stray_x, stray_y = jnp.bitwise_and(shift, 1), jnp.bitwise_and(shift // 2, 1)
    is_even = stray_rz % 2 == 0
    far_bit, near_bit = jnp.where(is_even, stray_y, stray_x), jnp.where(is_even, stray_x, stray_y)
    stray_place = (((stray_rz % 2) * 2 + far_bit) * 2 + near_bit) * (line // 2) + stray_rz // 2
    picks = jnp.concatenate(
        [
            jnp.where(my_stray >= 0, 1, jnp.where(my_extra >= 0, 2, 0)),
            jnp.where(my_stray >= 0, stray_place, 0),
            jnp.maximum(my_extra, 0),
        ]
    ).astype(jnp.int32)

    def slot_spec(first):
        return pl.BlockSpec((1, UROWS, width), lambda i, pick: (first + i, 0, 0))

    stack_shape = unit_weight.shape
    update_shapes = [like(stack_shape)] * 3 + [like(stack_shape, BF16)]
    partial_update = pl.pallas_call(
        stray_update_kernel,
        grid_spec=pltpu.PrefetchScalarGridSpec(
            num_scalar_prefetch=1,
            grid=(spare,),
            in_specs=[slot_spec(own)] * 3
            + [
                pl.BlockSpec((1, UROWS, width), lambda i, pick: (pick[spare + i], 0, 0)),
                pl.BlockSpec((1, UROWS, width), lambda i, pick: (pick[2 * spare + i], 0, 0)),
            ],
            out_specs=[slot_spec(own)] * 4,
        ),
        out_shape=update_shapes,
        compiler_params=params(32),
        cost_estimate=timed(5),
    )(picks, unit_weight, unit_first, unit_second, stray_found, extra_grad)
    unit_weights, unit_firsts, unit_seconds, unit_copies = pl.pallas_call(
        own_update_kernel,
        grid_spec=pltpu.PrefetchScalarGridSpec(
            num_scalar_prefetch=1,
            grid=(own,),
            in_specs=[slot_spec(0)] * 4 + [ANY] * 4,
            out_specs=[slot_spec(0)] * 4,
        ),
        out_shape=update_shapes,
        input_output_aliases={5: 0, 6: 1, 7: 2, 8: 3},
        compiler_params=params(32),
        cost_estimate=timed(4),
    )(my_count, unit_weight, unit_first, unit_second, own_grads, *partial_update)

    proj_total = pl.pallas_call(
        functools.partial(order_rows_kernel, devices),
        out_shape=like((devices, STRAY_TILE, width)),
        in_specs=[SMEM, VMEM],
        compiler_params=params(32),
        cost_estimate=timed(1),
    )(where, stray_found[:, UROWS:])
    proj_total = proj_total[:, :share].reshape(devices * share, width)[: proj_width * D // width]
    proj_total = proj_total.reshape(2, proj_width, D // 2).transpose(0, 2, 1).reshape(D, proj_width)
    gain_total = small_total[: gain_rows.shape[0]].reshape(3, D)
    bias_total = small_total[gain_rows.shape[0], : BUCKETS * heads].reshape(BUCKETS, heads)
    gain_weights, gain_firsts, gain_seconds = adamw_step(
        gain_weight, gain_first, gain_second, gain_total, RATE_GAIN
    )
    bias_weights, bias_firsts, bias_seconds = adamw_step(
        bias_weight, bias_first, bias_second, bias_total, RATE_SMALL
    )
    proj_weights, proj_firsts, proj_seconds = adamw_step(
        proj_weight, proj_first, proj_second, proj_total, RATE_MATRIX
    )
    return (
        encoded,
        token_grad,
        unit_weights,
        unit_firsts,
        unit_seconds,
        unit_copies,
        gain_weights,
        gain_firsts,
        gain_seconds,
        bias_weights,
        bias_firsts,
        bias_seconds,
        proj_weights,
        proj_firsts,
        proj_seconds,
    )


def solution(mesh):
    in_specs = (
        P("dp", None),
        P("dp", "mp"),
        P("dp"),
        P(),
        P(),
        P("dp", None, "mp"),
        P("dp", None, "mp"),
        P("dp", None, "mp"),
        P(),
        P(),
        P(),
        P(None, "mp"),
        P(None, "mp"),
        P(None, "mp"),
        P(None, "mp"),
        P(None, "mp"),
        P(None, "mp"),
    )
    out_specs = (
        P("dp", "mp"),
        P("dp", None),
        P("dp", None, "mp"),
        P("dp", None, "mp"),
        P("dp", None, "mp"),
        P("dp", None, "mp"),
        P(),
        P(),
        P(),
        P(None, "mp"),
        P(None, "mp"),
        P(None, "mp"),
        P(None, "mp"),
        P(None, "mp"),
        P(None, "mp"),
    )
    return jax.shard_map(shards, mesh=mesh, in_specs=in_specs, out_specs=out_specs, check_vma=False)
```

```python
import functools

import jax
import jax.numpy as jnp
from jax import lax
from jax.experimental import pallas as pl
from jax.experimental.pallas import tpu as pltpu
from jax.sharding import PartitionSpec as P

D = 768
HEAD_DIM = 64
FF = 3072
BUCKETS = 32
SLOT = 512
UROWS = 128
STEP = 5
HALF = UROWS // 2

NORM_EPS = 1e-06
ADAM_EPS = 1e-08
BETA_ONE = 0.5
BETA_TWO = 0.5
DECAY = 0.01
RATE_MATRIX = 0.02
RATE_SMALL = 0.1
RATE_GAIN = 0.6
GELU_C = 0.7978845608
GELU_K = 0.044715
MASKED = -1000000000.0

ROWS = D // UROWS
BLOCKS = FF // D
SQUARES = 4 * ROWS
FRONT = 3 * ROWS
SPREAD = 2 * SLOT
STRAY_TILE = 16
WINDOWS = 2, 2, 3
BACK_WINDOWS = 3, 3, 4
ALONG_X, ALONG_Y, ALONG_Z = 0, 1, 2
F32 = jnp.float32
BF16 = jnp.bfloat16
ANY = pl.BlockSpec(memory_space=pl.ANY)
SMEM = pl.BlockSpec(memory_space=pltpu.SMEM)
VMEM = pl.BlockSpec(memory_space=pltpu.VMEM)
HBM = pl.BlockSpec(memory_space=pltpu.HBM)
PAIR = 2 * HEAD_DIM


def dot(left, right):
    return jnp.dot(left, right, preferred_element_type=F32)


def dot_nt(left, right):
    return lax.dot_general(left, right, (((1,), (1,)), ((), ())), preferred_element_type=F32)


def dot_tn(left, right):
    return lax.dot_general(left, right, (((0,), (0,)), ((), ())), preferred_element_type=F32)


def precise_dot(left, right):
    return jnp.dot(left, right, precision=lax.Precision.HIGHEST, preferred_element_type=F32)


def inverse_rms(values):
    return lax.rsqrt(jnp.mean(values * values, axis=-1, keepdims=True) + NORM_EPS)


def norm_back(values, inv_rms, gain_row, grad_in):
    weighted = grad_in * gain_row
    gain_grad = jnp.sum(grad_in * values * inv_rms, axis=0, keepdims=True)
    slope = jnp.mean(weighted * values, axis=-1, keepdims=True)
    values_grad = inv_rms * weighted - values * (inv_rms * inv_rms * inv_rms) * slope
    return values_grad, gain_grad


def adamw_step(weight_now, first_now, second_now, grad_in, rate):
    first_new = BETA_ONE * first_now + (1.0 - BETA_ONE) * grad_in
    second_new = BETA_TWO * second_now + (1.0 - BETA_TWO) * grad_in * grad_in
    first_hat = first_new / (1.0 - BETA_ONE**STEP)
    second_hat = second_new / (1.0 - BETA_TWO**STEP)
    weight_new = weight_now - rate * (
        first_hat / (jnp.sqrt(second_hat) + ADAM_EPS) + DECAY * weight_now
    )
    return weight_new, first_new, second_new


def params(limit_mib):
    return pltpu.CompilerParams(vmem_limit_bytes=limit_mib * 1024 * 1024)


def timed(micros):
    return pl.CostEstimate(flops=int(micros * 1.15e9), bytes_accessed=int(micros * 1e5), transcendentals=0)


def ring_order(line):
    return list(range(0, line, 2)) + list(range(line - 1 - line % 2, 0, -2))


def ring_place(z, line):
    return jnp.where(z % 2 == 0, z // 2, line - (z + 1) // 2)


def ring_device(place, line):
    return jnp.where(2 * place < line, 2 * place, 2 * (line - place) - 1)


def hops(devices):
    line = devices // 4
    order = ring_order(line)
    after = {order[i]: order[(i + 1) % line] for i in range(line)}
    along_x = [(i, i ^ 1) for i in range(devices)]
    along_y = [(i, i ^ 2) for i in range(devices)]
    along_z = [(i, after[i // 4] * 4 + i % 4) for i in range(devices)]
    return along_x, along_y, along_z


def swap(values):
    return lax.ppermute(values, "mp", [(0, 1), (1, 0)])


def rest_place(unit):
    inner = unit - SQUARES
    matrix = inner // (ROWS * BLOCKS)
    rest = inner % (ROWS * BLOCKS)
    wide = ROWS + matrix * ROWS * BLOCKS + (rest % BLOCKS) * ROWS + rest // BLOCKS
    return jnp.where(unit < SQUARES, unit - FRONT, wide)


def after(values, other):
    return lax.optimization_barrier((values, other))[0]


class Links:
    def __init__(self, devices, *windows):
        self.pairs = hops(devices)
        self.sent = ([], [], [])
        self.windows = windows
        self.gate = None

    def settle(self, values):
        return values if self.gate is None else after(values, self.gate)

    def send(self, values, axis, steps=1):
        queue = self.sent[axis]
        window = self.windows[axis] if self.windows else len(queue) + 1
        if len(queue) >= window:
            values = after(values, queue[-window])
        step = dict(self.pairs[axis])
        reach = dict(step)
        for _ in range(steps - 1):
            reach = {i: step[j] for i, j in reach.items()}
        queue.append(lax.ppermute(values, "dp", sorted(reach.items())))
        return queue[-1]


def strays_kernel(own, most, devices, where_ref, index_ref, weight_ref, *refs):
    line = devices // 4
    *outs, stage, sem = refs
    load = pltpu.make_async_copy(weight_ref.at[own:most], stage, sem)
    load.start()
    for out in outs:
        out[...] = jnp.zeros_like(out)
    load.wait()
    me = where_ref[0]
    for j in range(most - own):
        home = index_ref[j]

        @pl.when(home >= 0)
        def _():
            rel = jnp.bitwise_xor(home, me)
            rx = jnp.bitwise_and(rel, 1)
            ry = jnp.bitwise_and(rel // 2, 1)
            rz = (ring_place(home // 4, line) - ring_place(me // 4, line) + line) % line
            unit = stage[j].astype(BF16)
            for odd, (near, far) in enumerate(((rx, ry), (ry, rx))):
                for sent in range(2):

                    @pl.when(jnp.logical_and(rz % 2 == odd, near == sent))
                    def _():
                        outs[2 * odd + sent][far, rz // 2] = unit


def gather_units(own, devices, layout, where_ref, table_ref, pieces, extra_ref, stack, front_sem, rest_sem):
    line = devices // 4
    me = where_ref[0]
    slots = own + 1

    def fetch(source, place):
        @pl.when(place < FRONT)
        def _():
            pltpu.make_async_copy(source, stack.at[place], front_sem).start()

        @pl.when(place >= FRONT)
        def _():
            pltpu.make_async_copy(source, stack.at[place], rest_sem).start()

    for piece, spots in zip(pieces, layout):
        for i, (rx, ry, rz, slot) in enumerate(spots):
            z = ring_device((ring_place(me // 4, line) - rz + line) % line, line)
            other = z * 4 + jnp.bitwise_xor(me % 4, 2 * ry + rx)
            fetch(piece.at[i], table_ref[other * slots + slot])

    @pl.loop(0, where_ref[1])
    def _(i):
        fetch(extra_ref.at[i], table_ref[devices * slots + i])


def wait_units(stack, total, sem):
    while total > 0:
        step = min(stack.shape[0], total)
        pltpu.make_async_copy(stack.at[0:step], stack.at[0:step], sem).wait()
        total -= step


def put_units(dest_ref, first_unit, stage, own_ref, stray_ref, sem):
    for i, unit in enumerate(first_unit):
        dest = dest_ref[unit]

        @pl.when(dest >= 0)
        def _():
            pltpu.make_async_copy(stage.at[i], own_ref.at[dest], sem).start()

        @pl.when(dest < 0)
        def _():
            pltpu.make_async_copy(stage.at[i], stray_ref.at[-1 - dest, :UROWS], sem).start()


def toeplitz(row):
    width = SPREAD
    tile = jnp.broadcast_to(pltpu.roll(row, width - (SLOT - 1), 1), (8, width))
    places = lax.broadcasted_iota(jnp.int32, (8, width), 0)
    for bit in (1, 2, 4):
        tile = jnp.where(jnp.bitwise_and(places, bit) != 0, pltpu.roll(tile, bit, 1), tile)
    reach = 8
    while reach < SLOT // 2:
        tile = jnp.concatenate([tile, pltpu.roll(tile, reach, 1)], axis=0)
        reach *= 2
    lower = jnp.concatenate([tile[:, width - reach :], tile[:, : SLOT - reach]], axis=1)
    return jnp.concatenate([tile[:, :SLOT], lower], axis=0)


def diagonals(tile):
    rows = SLOT
    while rows > 128:
        rows //= 2
        blank = jnp.zeros((rows, rows), F32)
        tile = jnp.concatenate([tile[rows:], blank], axis=1) + jnp.concatenate(
            [blank, tile[:rows]], axis=1
        )
    tile = jnp.concatenate([tile, jnp.zeros((rows, SPREAD - tile.shape[1]), F32)], axis=1)
    while rows > 8:
        rows //= 2
        tile = tile[rows:] + pltpu.roll(tile[:rows], rows, 1)
    places = lax.broadcasted_iota(jnp.int32, tile.shape, 0)
    for bit in (4, 2, 1):
        tile = jnp.where(jnp.bitwise_and(places, bit) == 0, pltpu.roll(tile, bit, 1), tile)
    return jnp.sum(tile, axis=0, keepdims=True)


def matrix(ref, first):
    return ref[first : first + ROWS].reshape(D, ref.shape[2])


def pair_columns(ref, step):
    return ref[:, pl.ds(pl.multiple_of(step * PAIR, PAIR), PAIR)]


def attend_kernel(own, devices, layout, lengths_ref, where_ref, table_ref, tokens_ref, gain_ref, bias_ref, extra_ref, *refs):
    pieces = refs[: len(layout)]
    norm_ref, query_ref, key_ref, value_ref, prob_ref, mixed_ref, front_ref, rest_ref = refs[len(layout) : -5]
    stack, front_sem, rest_sem, front_out, rest_out = refs[-5:]
    step = pl.program_id(0)
    front_copy = pltpu.make_async_copy(stack.at[:FRONT], front_ref, front_out)
    rest_copy = pltpu.make_async_copy(stack.at[FRONT:], rest_ref, rest_out)

    @pl.when(step == 0)
    def _():
        gather_units(
            own, devices, layout, where_ref, table_ref, pieces, extra_ref, stack, front_sem, rest_sem
        )
        inputs = tokens_ref[...].astype(F32)
        normed = (inputs * inverse_rms(inputs) * gain_ref[0:1, :]).astype(BF16)
        norm_ref[...] = normed
        wait_units(stack, FRONT, front_sem)
        front_copy.start()
        query_ref[...] = dot(normed, matrix(stack, 0)).astype(BF16)
        key_ref[...] = dot(normed, matrix(stack, ROWS)).astype(BF16)
        value_ref[...] = dot(normed, matrix(stack, 2 * ROWS)).astype(BF16)
        wait_units(stack, devices * own - FRONT, rest_sem)

        @pl.loop(0, where_ref[1])
        def _(i):
            wait_units(stack, 1, rest_sem)

        rest_copy.start()

    @pl.when(step == pl.num_programs(0) - 1)
    def _():
        front_copy.wait()
        rest_copy.wait()

    queries = pair_columns(query_ref, step)
    keys = pair_columns(key_ref, step)
    values = pair_columns(value_ref, step)
    lanes = lax.broadcasted_iota(jnp.int32, (SLOT, PAIR), 1) // HEAD_DIM
    seen = lax.broadcasted_iota(jnp.int32, (1, SLOT), 1) < lengths_ref[0]
    mixes = []
    for which in range(2):
        scores = dot_nt(jnp.where(lanes == which, queries, jnp.zeros_like(queries)), keys)
        scores = scores + toeplitz(bias_ref[pl.ds(2 * step + which, 1), :])
        scores = jnp.where(seen, scores, MASKED)
        powers = jnp.exp(scores - jnp.max(scores, axis=-1, keepdims=True))
        probabilities = powers * (1.0 / jnp.sum(powers, axis=-1, keepdims=True))
        prob_ref[which] = probabilities
        mixes.append(dot(probabilities.astype(BF16), values))
    mixed = jnp.where(lanes == 0, mixes[0], mixes[1]).astype(BF16)
    mixed_ref[:, pl.ds(pl.multiple_of(step * PAIR, PAIR), PAIR)] = mixed


def out_kernel(own, devices, where_ref, table_ref, mixed_ref, rest_in, *refs):
    line = devices // 4
    *pieces, part_ref, rest_ref, stage, weight, stage_sem, weight_sem, put_sem = refs
    me = where_ref[0]
    load = pltpu.make_async_copy(rest_in.at[0:ROWS], weight, weight_sem)
    load.start()
    for rz in range(line):
        pltpu.make_async_copy(pieces[rz], stage.at[4 * rz : 4 * rz + 4], stage_sem).start()
    load.wait()
    pltpu.make_async_copy(stage, stage, stage_sem).wait()
    for rz in range(line):
        z = ring_device((ring_place(me // 4, line) - rz + line) % line, line)
        for near in range(4):
            other = z * 4 + jnp.bitwise_xor(me % 4, near)
            place = table_ref[other * (own + 1) + own] - FRONT
            i = 4 * rz + near
            pltpu.make_async_copy(stage.at[i], rest_ref.at[place], put_sem).start()

            @pl.when(place < ROWS)
            def _():
                weight[place] = stage[i]

    part_ref[...] = dot_nt(mixed_ref[...], matrix(weight, 0)).astype(BF16)
    pltpu.make_async_copy(stage, stage, put_sem).wait()


def both(mine_ref, other_ref):
    return mine_ref[...].astype(F32) + other_ref[...].astype(F32)


def gelu_tanh(values):
    return jnp.tanh(GELU_C * (values + GELU_K * values * values * values))


def feed_kernel(
    tokens_ref, mine_ref, other_ref, gain_ref, gate_w, up_w, down_w,
    residual_ref, norm_ref, gate_ref, up_ref, hidden_ref, part_ref, sum_ref,
):
    step = pl.program_id(0)

    @pl.when(step == 0)
    def _():
        residual = tokens_ref[...].astype(F32) + both(mine_ref, other_ref)
        residual_ref[...] = residual
        norm_ref[...] = (residual * inverse_rms(residual) * gain_ref[1:2, :]).astype(BF16)
        sum_ref[...] = jnp.zeros_like(sum_ref)

    normed = norm_ref[...]
    gate = dot(normed, matrix(gate_w, 0))
    up = dot(normed, matrix(up_w, 0))
    gate_ref[...] = gate
    up_ref[...] = up
    hidden = (0.5 * gate * (1.0 + gelu_tanh(gate)) * up).astype(BF16)
    hidden_ref[...] = hidden
    sum_ref[...] += dot_nt(hidden, matrix(down_w, 0))

    @pl.when(step == pl.num_programs(0) - 1)
    def _():
        part_ref[...] = sum_ref[...].astype(BF16)


def turn_kernel(
    lengths_ref, residual_ref, mine_ref, other_ref, gain_ref, proj_ref, proj_other, cot_ref, cot_other,
    gate_ref, up_ref, gate_w, up_w, down_w,
    encoded_ref, proj_grad, gain_grad, grad_ref, feed_ref, dgate_ref, dup_ref, part_ref, sum_ref,
):
    step = pl.program_id(0)

    @pl.when(step == 0)
    def _():
        residual = residual_ref[...] + both(mine_ref, other_ref)
        inv_rms = inverse_rms(residual)
        normed = (residual * inv_rms * gain_ref[2:3, :]).astype(BF16)
        encoded_ref[...] = dot(normed, proj_ref[...])
        rows = lax.broadcasted_iota(jnp.int32, (SLOT, 1), 0) < lengths_ref[0]
        mine = jnp.where(rows, cot_ref[...], jnp.zeros_like(cot_ref))
        other = jnp.where(rows, cot_other[...], jnp.zeros_like(cot_other))
        backward = dot_tn(mine, normed)
        proj_grad[0] = backward[:, : D // 2]
        proj_grad[1] = backward[:, D // 2 :]
        third = dot_nt(mine, proj_ref[...]) + dot_nt(other, proj_other[...])
        grad, gain = norm_back(residual, inv_rms, gain_ref[2:3, :], third)
        gain_grad[...] = gain
        grad_ref[...] = grad
        feed_ref[...] = grad.astype(BF16)
        sum_ref[...] = jnp.zeros_like(sum_ref)

    dhidden = dot(feed_ref[...], matrix(down_w, 0))
    gate = gate_ref[...]
    bend = gelu_tanh(gate)
    slope = 0.5 * (1.0 + bend) + 0.5 * gate * (1.0 - bend * bend) * (
        GELU_C * (1.0 + 3.0 * GELU_K * gate * gate)
    )
    dgate = (dhidden * up_ref[...] * slope).astype(BF16)
    dup = (dhidden * (0.5 * gate * (1.0 + bend))).astype(BF16)
    dgate_ref[...] = dgate
    dup_ref[...] = dup
    sum_ref[...] += dot_nt(dgate, matrix(gate_w, 0)) + dot_nt(dup, matrix(up_w, 0))

    @pl.when(step == pl.num_programs(0) - 1)
    def _():
        part_ref[...] = sum_ref[...].astype(BF16)


def wide_grads_kernel(
    units, dest_ref, norm_ref, feed_ref, hidden_ref, dgate_ref, dup_ref, own_ref, stray_ref, stage, sems
):
    step = pl.program_id(0)
    slot = step % 2
    shape = (ROWS,) + stage.shape[2:]

    def settle(which):
        pltpu.make_async_copy(stage.at[which], stage.at[which], sems.at[which]).wait()

    @pl.when(step >= 2)
    def _():
        settle(slot)

    normed = norm_ref[...]
    stage[slot, 0:ROWS] = dot_tn(normed, dgate_ref[...]).astype(BF16).reshape(shape)
    stage[slot, ROWS : 2 * ROWS] = dot_tn(normed, dup_ref[...]).astype(BF16).reshape(shape)
    stage[slot, 2 * ROWS :] = dot_tn(feed_ref[...], hidden_ref[...]).astype(BF16).reshape(shape)
    names = [
        SQUARES + which * ROWS * BLOCKS + row * BLOCKS + step for which in range(3) for row in range(ROWS)
    ]
    put_units(dest_ref, names, stage.at[slot], own_ref, stray_ref, sems.at[slot])

    @pl.when(step == pl.num_programs(0) - 1)
    def _():
        settle(1 - slot)
        settle(slot)


def enter_back_kernel(
    dest_ref, home_ref, grad_ref, residual_ref, mine_ref, other_ref, gain_ref, weight_ref, mixed_ref,
    proj_ref, own_in, stray_in,
    grad_one, gain_grad, dmixed_ref, own_ref, stray_ref, stage, sem, proj_sem,
):
    for home in range(proj_ref.shape[0]):
        pltpu.make_async_copy(
            proj_ref.at[home], stray_ref.at[home_ref[home], UROWS:], proj_sem
        ).start()
    residual = residual_ref[...]
    second = both(mine_ref, other_ref)
    back, gain = norm_back(residual, inverse_rms(residual), gain_ref[1:2, :], second)
    gain_grad[...] = gain
    total = grad_ref[...] + back
    grad_one[...] = total
    lowered = total.astype(BF16)
    stage[...] = dot_tn(lowered, mixed_ref[...]).astype(BF16).reshape(stage.shape)
    put_units(dest_ref, range(FRONT, SQUARES), stage, own_ref, stray_ref, sem)
    dmixed_ref[...] = dot(lowered, matrix(weight_ref, 0)).astype(BF16)
    pltpu.make_async_copy(stage, stage, sem).wait()
    pltpu.make_async_copy(proj_ref, proj_ref, proj_sem).wait()


def attend_back_kernel(
    dmixed_ref, query_ref, key_ref, value_ref, prob_ref, dquery_ref, dkey_ref, dvalue_ref, offset_ref
):
    queries, keys, values, dmixed = query_ref[...], key_ref[...], value_ref[...], dmixed_ref[...]
    lanes = lax.broadcasted_iota(jnp.int32, (SLOT, PAIR), 1) // HEAD_DIM
    parts = []
    for which in range(2):
        dprob = dot_nt(jnp.where(lanes == which, dmixed, jnp.zeros_like(dmixed)), values)
        probabilities = prob_ref[which]
        share = jnp.sum(probabilities * dprob, axis=-1, keepdims=True)
        dscore = (probabilities * (dprob - share)).astype(BF16)
        parts.append(
            (
                dot(dscore, keys),
                dot_tn(dscore, queries),
                dot_tn(probabilities.astype(BF16), dmixed),
            )
        )
        offset_ref[0, which : which + 1, :] = diagonals(dscore.astype(F32))
    for out, first, second in zip((dquery_ref, dkey_ref, dvalue_ref), *parts):
        out[...] = jnp.where(lanes == 0, first, second).astype(BF16)


def joined(refs):
    return jnp.concatenate([ref[...] for ref in refs], axis=1)


def first_grad_kernel(weight_ref, *refs):
    *parts, out_ref = refs
    width = len(parts) // 3
    total = 0.0
    for i in range(3):
        total = total + dot_nt(joined(parts[i * width : (i + 1) * width]), matrix(weight_ref, i * ROWS))
    out_ref[...] = total.astype(BF16)


def front_grads_kernel(dest_ref, norm_ref, *refs):
    *parts, own_in, own_ref, stage, sem = refs
    width = len(parts) // 3
    normed = norm_ref[...]
    shape = (ROWS,) + stage.shape[1:]
    for i in range(3):
        first = i * ROWS
        grads = joined(parts[i * width : (i + 1) * width])
        stage[first : first + ROWS] = dot_tn(normed, grads).astype(BF16).reshape(shape)
        for unit in range(first, first + ROWS):
            pltpu.make_async_copy(stage.at[unit], own_ref.at[dest_ref[unit]], sem).start()
    pltpu.make_async_copy(stage, stage, sem).wait()


def token_grad_kernel(tokens_ref, grad_ref, mine_ref, other_ref, gain_ref, out_ref, gain_grad):
    inputs = tokens_ref[...].astype(F32)
    first = both(mine_ref, other_ref)
    back, gain = norm_back(inputs, inverse_rms(inputs), gain_ref[0:1, :], first)
    out_ref[...] = grad_ref[...] + back
    gain_grad[...] = gain


def order_rows_kernel(devices, where_ref, found_ref, out_ref):
    line = devices // 4
    me = where_ref[0]
    for rz in range(line):
        z = ring_device((ring_place(me // 4, line) - rz + line) % line, line)
        for far in range(2):
            for near in range(2):
                rx, ry = (far, near) if rz % 2 else (near, far)
                other = z * 4 + jnp.bitwise_xor(me % 4, 2 * ry + rx)
                place = ((rz % 2 * 2 + far) * 2 + near) * (line // 2) + rz // 2
                out_ref[other] = found_ref[place].astype(F32)


def update_kernel(pick_ref, weight, first, second, own_grad, stray, extra, *outs):
    kind = pick_ref[pl.program_id(0)]
    grad = jnp.where(kind == 1, stray[0].astype(F32), extra[0].astype(F32))
    grad = jnp.where(kind == 3, own_grad[0], grad)
    grad = jnp.where(kind == 0, 0.0, grad)
    update_slot(weight, first, second, grad, outs)


def update_slot(weight, first, second, grad, outs):
    new_weight, new_first, new_second = adamw_step(
        weight[0], first[0], second[0], grad, RATE_MATRIX
    )
    outs[0][0] = new_weight
    outs[1][0] = new_first
    outs[2][0] = new_second
    outs[3][0] = new_weight.astype(BF16)


def shards(
    tokens,
    out_grad,
    doc_lengths,
    owner_list,
    bucket_table,
    unit_weight,
    unit_first,
    unit_second,
    gain_weight,
    gain_first,
    gain_second,
    bias_weight,
    bias_first,
    bias_second,
    proj_weight,
    proj_first,
    proj_second,
):
    most, _, width = unit_weight.shape
    heads = bias_weight.shape[1]
    count = tokens.shape[0]
    units = owner_list.shape[0]
    proj_width = proj_weight.shape[1]
    devices = lax.axis_size("dp")
    line = devices // 4
    own = max(1, (units - 1) // devices)
    slots = own + 1
    spare = most - own
    me = lax.axis_index("dp").astype(jnp.int32)

    def like(shape, kind=F32):
        return jax.ShapeDtypeStruct(shape, kind)

    full, left = divmod(units, most)
    extra_count = max(FRONT, full * spare + max(0, left - own) - devices)
    indices = jnp.arange(units, dtype=jnp.int32)
    before = indices[None, :] < indices[:, None]
    same = owner_list[:, None] == owner_list[None, :]
    rank = jnp.sum((same & before).astype(jnp.int32), axis=1)
    is_over = rank >= own
    may_stray = is_over & (indices >= FRONT)
    stray_index = jnp.sum((before & may_stray[None, :]).astype(jnp.int32), axis=1)
    is_stray = may_stray & (stray_index < devices)
    is_extra = is_over & ~is_stray
    extra_index = jnp.sum((before & is_extra[None, :]).astype(jnp.int32), axis=1)
    extra_total = jnp.sum(is_extra.astype(jnp.int32))
    many = extra_total > 0
    position = jnp.where(
        is_stray,
        stray_index * slots + own,
        jnp.where(is_extra, devices * slots + extra_index, owner_list * slots + rank),
    )
    position_ids = jnp.arange(devices * slots + extra_count, dtype=jnp.int32)
    hit = position[None, :] == position_ids[:, None]
    placed = jnp.where(indices < FRONT, indices, FRONT + rest_place(indices))
    table = units + jnp.sum(jnp.where(hit, placed[None, :] - units, 0), axis=1).astype(jnp.int32)
    spare_ids = jnp.arange(spare, dtype=jnp.int32)
    my_over = (owner_list[None, :] == me) & (rank[None, :] == own + spare_ids[:, None])
    my_stray = jnp.sum(jnp.where(my_over & is_stray[None, :], stray_index[None, :] + 1, 0), axis=1) - 1
    my_extra = jnp.sum(jnp.where(my_over & is_extra[None, :], extra_index[None, :] + 1, 0), axis=1) - 1
    my_count = jnp.sum((owner_list == me).astype(jnp.int32)).reshape(1)
    where = jnp.stack([me, extra_total]).astype(jnp.int32)

    home = jnp.where(is_stray, stray_index, owner_list)
    rel_x = jnp.bitwise_and(jnp.bitwise_xor(home, me), 1)
    rel_y = jnp.bitwise_and(jnp.bitwise_xor(home, me) // 2, 1)
    rel_z = (ring_place(home // 4, line) - ring_place(me // 4, line) + line) % line
    cut = (own + 1) // 2
    spans = [(0, cut), (cut, own)] if own > cut else [(0, cut)]
    even = rel_z % 2 == 0
    in_first = rank < cut
    near_is_x = even == in_first
    corner = jnp.where(near_is_x, rel_x, rel_y) * 2 + jnp.where(near_is_x, rel_y, rel_x)
    own_dest = rel_z * 4 * own + jnp.where(
        in_first, corner * cut + rank, 4 * cut + corner * (own - cut) + rank - cut
    )

    def stray_dest_of(x, y, z):
        even = z % 2 == 0
        corner = jnp.where(even, x, y) * 2 + jnp.where(even, y, x)
        return (jnp.where(even, 0, 2 * line) + corner * (line // 2) + z // 2).astype(jnp.int32)

    stray_dest = stray_dest_of(rel_x, rel_y, rel_z)
    homes = jnp.arange(devices, dtype=jnp.int32)
    home_dest = stray_dest_of(
        jnp.bitwise_and(jnp.bitwise_xor(homes, me), 1),
        jnp.bitwise_and(jnp.bitwise_xor(homes, me) // 2, 1),
        (ring_place(homes // 4, line) - ring_place(me // 4, line) + line) % line,
    )
    dest = jnp.where(
        is_stray,
        -1 - stray_dest,
        jnp.where(is_extra, 4 * line * own + extra_index, own_dest),
    ).astype(jnp.int32)

    extra_shape = (extra_count, UROWS, width)

    def extra_weights():
        wanted = jnp.arange(extra_count, dtype=jnp.int32)[:, None] == my_extra[None, :]
        taken = jnp.take(unit_weight[own:], jnp.argmax(wanted, axis=1), axis=0)
        return lax.psum(jnp.where(jnp.any(wanted, axis=1)[:, None, None], taken, 0.0), "dp").astype(BF16)

    def no_extra():
        return jnp.zeros(extra_shape, BF16)

    extra = lax.cond(many, extra_weights, no_extra)

    def sum_strays(links, keep_a, send_a, keep_b, send_b):
        from_x = links.send(send_a, ALONG_X)
        from_y = links.send(send_b, ALONG_Y)
        yield
        from_x, from_y = links.settle(from_x), links.settle(from_y)
        low_y = links.send((keep_a[1].astype(F32) + from_x[1].astype(F32)).astype(BF16), ALONG_Y)
        high_x = links.send((keep_b[1].astype(F32) + from_y[1].astype(F32)).astype(BF16), ALONG_X)
        yield
        low_y, high_x = links.settle(low_y), links.settle(high_x)
        low = keep_a[0].astype(F32) + from_x[0].astype(F32) + low_y.astype(F32)
        high = keep_b[0].astype(F32) + from_y[0].astype(F32) + high_x.astype(F32)
        sums = [(high if rz % 2 else low)[rz // 2] for rz in range(line)]
        total = sums[0]
        terms = [links.send(sums[rz].astype(BF16), ALONG_Z, rz) for rz in range(1, line)]
        yield
        for term in terms:
            total = total + links.settle(term).astype(F32)
        return total.astype(BF16)

    def gather_strays(links, unit):
        got = links.send(unit, ALONG_X)
        yield
        near = jnp.stack([unit, links.settle(got)])
        got = links.send(near, ALONG_Y)
        yield
        near = jnp.concatenate([near, links.settle(got)])
        found = [near]
        for _ in range(line - 1):
            found.append(links.send(found[-1], ALONG_Z))
            yield
            found[-1] = links.settle(found[-1])
        return found

    def stray_chain(links, *arrays):
        unit = yield from sum_strays(links, *arrays)
        return (yield from gather_strays(links, unit))

    class Chain:
        def __init__(self, links, steps):
            self.links, self.steps, self.value = links, steps, None

        def step(self, gate=None):
            self.links.gate = gate
            try:
                if self.value is None:
                    next(self.steps)
            except StopIteration as end:
                self.value = end.value

        def finish(self):
            while self.value is None:
                self.step()
            return self.value

    proj_low = proj_weight.astype(BF16)
    proj_other = swap(proj_low)
    cot_other = swap(out_grad)

    links = Links(devices, *WINDOWS)
    rings = [[unit_weight[first:last].astype(BF16)] for first, last in spans]
    pieces, layout, rounds = [], [], {}

    def ring_step():
        for ring in rings:
            ring.append(links.send(ring[-1], ALONG_Z))

    def keep(values, rx, ry, spots):
        pieces.append(values)
        layout.append([(rx, ry, rz, slot) for rz, slot in spots])

    def near_round(pair):
        for i, axis in enumerate((ALONG_X, ALONG_Y)):
            parts, spots = [], []
            for rz in (2 * pair, 2 * pair + 1):
                which = (i + rz) % 2
                if which < len(rings):
                    parts.append(rings[which][rz])
                    spots += [(rz, slot) for slot in range(*spans[which])]
            if parts:
                values = jnp.concatenate(parts) if len(parts) > 1 else parts[0]
                rounds[pair, axis] = values, spots, links.send(values, axis)

    def far_direct(pair):
        for axis in (ALONG_X, ALONG_Y):
            if (pair, axis) in rounds:
                values, spots, got = rounds[pair, axis]
                other = ALONG_X + ALONG_Y - axis
                keep(values, 0, 0, spots)
                keep(got, int(axis == ALONG_X), int(axis == ALONG_Y), spots)
                keep(links.send(values, other), int(axis == ALONG_Y), int(axis == ALONG_X), spots)

    def far_through(pair):
        for axis in (ALONG_X, ALONG_Y):
            if (pair, axis) in rounds:
                values, spots, got = rounds[pair, axis]
                keep(links.send(got, ALONG_X + ALONG_Y - axis), 1, 1, spots)

    ring_step()
    near_shape = like((2, line // 2, UROWS, width), BF16)
    stray_parts = pl.pallas_call(
        functools.partial(strays_kernel, own, most, devices),
        out_shape=[near_shape] * 4,
        in_specs=[SMEM, SMEM, ANY],
        out_specs=[VMEM] * 4,
        scratch_shapes=[pltpu.VMEM((spare, UROWS, width), F32), pltpu.SemaphoreType.DMA],
        compiler_params=params(40),
        cost_estimate=timed(2),
    )(where, my_stray, unit_weight)
    strays = Chain(links, stray_chain(links, *stray_parts))
    strays.step()
    for pair in range(line // 2):
        while len(rings[0]) < 2 * pair + 2:
            ring_step()
        near_round(pair)
        if pair == 0:
            strays.step(rings[0][-1])
            first_near = links.sent[ALONG_Y][1]
            while len(rings[0]) < min(line, 3):
                ring_step()
            far_direct(pair)
            strays.step(first_near)
            if len(rings[0]) < line:
                ring_step()
            strays.step(links.sent[ALONG_X][-1])
            far_through(pair)
            strays.step(links.sent[ALONG_X][-2])
        else:
            strays.step(links.sent[ALONG_Y][-3])
            far_direct(pair)
            strays.step(links.sent[ALONG_Y][-3])
            far_through(pair)
    found = strays.finish()
    tokens, proj_other, cot_other = lax.optimization_barrier((tokens, proj_other, cot_other))

    bucket_hot = (bucket_table[:, None] == jnp.arange(BUCKETS, dtype=jnp.int32)[None, :]).astype(F32)
    bucket_hot = jnp.pad(bucket_hot, ((0, SPREAD - bucket_hot.shape[0]), (0, 0)))
    bias_rows = jnp.pad(precise_dot(bucket_hot, bias_weight).T, ((0, 8 - heads % 8), (0, 0)))
    def whole(shape):
        return pl.BlockSpec(shape, lambda i: (0,) * len(shape))

    wide_shape = (count, D)
    head_shape = (count, width)
    front_spec = whole((FRONT, UROWS, width))
    out_spec = pl.BlockSpec((ROWS, UROWS, width), lambda i: (0, 0, 0))
    prob_spec = pl.BlockSpec((2, SLOT, SLOT), lambda i: (i, 0, 0))
    gain_spec = whole((3, D))
    bias_spec = whole(bias_rows.shape)
    column_spec = pl.BlockSpec((count, width), lambda i: (0, i))

    def unit_spec(which):
        return pl.BlockSpec((ROWS, UROWS, width), lambda i: (1 + which * BLOCKS + i, 0, 0))

    wide_specs = [unit_spec(0), unit_spec(1), unit_spec(2)]

    stack_shape = (units + 1, UROWS, width)
    rest_shape = like((units + 1 - FRONT, UROWS, width), BF16)
    first_in, queries, keys, values, probabilities, mixed, front, rest = pl.pallas_call(
        functools.partial(attend_kernel, own, devices, layout),
        grid=(heads // 2,),
        in_specs=[SMEM] * 3 + [whole(wide_shape), gain_spec, bias_spec] + [ANY] * (1 + len(pieces)),
        out_specs=[whole(wide_shape)] + [whole(head_shape)] * 3 + [prob_spec, whole(head_shape), HBM, HBM],
        out_shape=[like(wide_shape, BF16)]
        + [like(head_shape, BF16)] * 3
        + [like((heads, SLOT, SLOT)), like(head_shape, BF16), like((FRONT, UROWS, width), BF16), rest_shape],
        scratch_shapes=[pltpu.VMEM(stack_shape, BF16)] + [pltpu.SemaphoreType.DMA] * 4,
        compiler_params=params(60),
        cost_estimate=timed(14),
    )(doc_lengths, where, table, tokens, gain_weight, bias_rows, extra, *pieces)
    attn_part, rest = pl.pallas_call(
        functools.partial(out_kernel, own, devices),
        grid=(1,),
        in_specs=[SMEM] * 2 + [whole(head_shape)] + [ANY] * (1 + line),
        out_specs=[whole(wide_shape), HBM],
        out_shape=[like(wide_shape, BF16), rest_shape],
        input_output_aliases={3: 1},
        scratch_shapes=[
            pltpu.VMEM((4 * line, UROWS, width), BF16),
            pltpu.VMEM((ROWS, UROWS, width), BF16),
        ]
        + [pltpu.SemaphoreType.DMA] * 3,
        compiler_params=params(56),
        cost_estimate=timed(4),
    )(where, table, mixed, rest, *found)

    residual_one, second_in, gate, up, hidden, feed_part = pl.pallas_call(
        feed_kernel,
        grid=(BLOCKS,),
        in_specs=[whole(wide_shape)] * 3 + [gain_spec] + wide_specs,
        out_specs=[whole(wide_shape)] * 2 + [column_spec] * 3 + [whole(wide_shape)],
        out_shape=[
            like(wide_shape),
            like(wide_shape, BF16),
            like((count, BLOCKS * width)),
            like((count, BLOCKS * width)),
            like((count, BLOCKS * width), BF16),
            like(wide_shape, BF16),
        ],
        scratch_shapes=[pltpu.VMEM(wide_shape, F32)],
        compiler_params=params(56),
        cost_estimate=timed(11),
    )(tokens, attn_part, swap(attn_part), gain_weight, rest, rest, rest)

    encoded, proj_grad, gain_three, grad_two, feed_grad, dgate, dup, second_part = pl.pallas_call(
        turn_kernel,
        grid=(BLOCKS,),
        in_specs=[SMEM]
        + [whole(wide_shape)] * 3
        + [gain_spec]
        + [whole((D, proj_width))] * 2
        + [whole((count, proj_width))] * 2
        + [column_spec] * 2
        + wide_specs,
        out_specs=[
            whole((count, proj_width)),
            whole((2, proj_width, D // 2)),
            whole((1, D)),
            whole(wide_shape),
            whole(wide_shape),
            column_spec,
            column_spec,
            whole(wide_shape),
        ],
        out_shape=[
            like((count, proj_width)),
            like((2, proj_width, D // 2)),
            like((1, D)),
            like(wide_shape),
            like(wide_shape, BF16),
            like((count, BLOCKS * width), BF16),
            like((count, BLOCKS * width), BF16),
            like(wide_shape, BF16),
        ],
        scratch_shapes=[pltpu.VMEM(wide_shape, F32)],
        compiler_params=params(56),
        cost_estimate=timed(14),
    )(
        doc_lengths, residual_one, feed_part, swap(feed_part), gain_weight, proj_low, proj_other,
        out_grad, cot_other, gate, up, rest, rest, rest,
    )

    own_shape = like((4 * line * own + extra_count, UROWS, width), BF16)
    stray_shape = like((4 * line, UROWS + STRAY_TILE, width), BF16)
    proj_rows = proj_grad.reshape(-1, width)
    share = -(-proj_rows.shape[0] // devices)
    proj_rows = jnp.pad(proj_rows, ((0, share * devices - proj_rows.shape[0]), (0, 0)))
    proj_rows = proj_rows.reshape(devices, share, width).astype(BF16)
    proj_rows = jnp.pad(proj_rows, ((0, 0), (0, STRAY_TILE - share), (0, 0)))
    own_units, stray_units = pl.pallas_call(
        functools.partial(wide_grads_kernel, units),
        grid=(BLOCKS,),
        in_specs=[SMEM] + [whole(wide_shape)] * 2 + [column_spec] * 3,
        out_specs=[HBM] * 2,
        out_shape=[own_shape, stray_shape],
        scratch_shapes=[
            pltpu.VMEM((2, 3 * ROWS, UROWS, width), BF16),
            pltpu.SemaphoreType.DMA((2,)),
        ],
        compiler_params=params(56),
        cost_estimate=timed(9),
    )(dest, second_in, feed_grad, hidden, dgate, dup)

    grad_one, gain_two, dmixed, own_units, stray_units = pl.pallas_call(
        enter_back_kernel,
        grid=(1,),
        in_specs=[SMEM] * 2
        + [whole(wide_shape)] * 4
        + [gain_spec, out_spec, whole(head_shape), whole(proj_rows.shape)]
        + [ANY] * 2,
        out_specs=[whole(wide_shape), whole((1, D)), whole(head_shape)] + [HBM] * 2,
        out_shape=[like(wide_shape), like((1, D)), like(head_shape, BF16), own_shape, stray_shape],
        input_output_aliases={10: 3, 11: 4},
        scratch_shapes=[pltpu.VMEM((ROWS, UROWS, width), BF16)] + [pltpu.SemaphoreType.DMA] * 2,
        compiler_params=params(56),
        cost_estimate=timed(0.4 * 6),
    )(
        dest, home_dest, grad_two, residual_one, second_part, swap(second_part), gain_weight, rest, mixed,
        proj_rows, own_units, stray_units,
    )

    links = Links(devices, *BACK_WINDOWS)
    by_near = stray_units.reshape(4, 2, line // 2, UROWS + STRAY_TILE, width)
    strays = Chain(links, sum_strays(links, *[by_near[i] for i in range(4)]))

    def attend_back(first, pairs, dmixed):
        pair_spec = pl.BlockSpec((count, PAIR), lambda i: (0, first + i))
        out_spec = pl.BlockSpec((count, PAIR), lambda i: (0, i))
        return pl.pallas_call(
            attend_back_kernel,
            grid=(pairs,),
            in_specs=[pair_spec] * 4 + [pl.BlockSpec((2, SLOT, SLOT), lambda i: (first + i, 0, 0))],
            out_specs=[out_spec] * 3 + [pl.BlockSpec((1, 8, SPREAD), lambda i: (i, 0, 0))],
            out_shape=[like((count, PAIR * pairs), BF16)] * 3 + [like((pairs, 8, SPREAD))],
            compiler_params=params(56),
            cost_estimate=timed(0.4 * 4.3 * pairs),
        )(dmixed, queries, keys, values, probabilities)

    pairs = heads // 2
    strays.step()
    singles = [attend_back(i, 1, dmixed) for i in range(pairs - 1)]
    grads_a = [joined_parts for joined_parts in singles[-1][:3]]
    strays.step()
    *grads_b, offsets_b = attend_back(pairs - 1, 1, after(dmixed, links.sent[ALONG_Y][0]))
    singles.append((*grads_b, offsets_b))
    head_grads = [single[i] for i in range(3) for single in singles]
    offset_grad = jnp.concatenate([single[3] for single in singles])[:, :2].reshape(heads, SPREAD)
    part_specs = [whole(part.shape) for part in head_grads]
    first_part = pl.pallas_call(
        first_grad_kernel,
        grid=(1,),
        in_specs=[front_spec] + part_specs,
        out_specs=whole(wide_shape),
        out_shape=like(wide_shape, BF16),
        compiler_params=params(56),
        cost_estimate=timed(2),
    )(front, *head_grads)

    own_units = pl.pallas_call(
        front_grads_kernel,
        grid=(1,),
        in_specs=[SMEM, whole(wide_shape)] + part_specs + [ANY],
        out_specs=HBM,
        out_shape=own_shape,
        input_output_aliases={2 + len(head_grads): 0},
        scratch_shapes=[pltpu.VMEM((FRONT, UROWS, width), BF16), pltpu.SemaphoreType.DMA],
        compiler_params=params(56),
        cost_estimate=timed(4),
    )(dest, first_in, *head_grads, own_units)

    token_grad, gain_one = pl.pallas_call(
        token_grad_kernel,
        out_shape=[like(wide_shape), like((1, D))],
        compiler_params=params(56),
        cost_estimate=timed(4),
    )(tokens, grad_one, first_part, swap(first_part), gain_weight)

    bias_grad = precise_dot(bucket_hot.T, offset_grad.T)
    gain_rows = jnp.concatenate([gain_one, gain_two, gain_three]).reshape(-1, width)
    bias_row = jnp.pad(bias_grad.reshape(1, -1), ((0, 0), (0, width - BUCKETS * heads)))
    small = jnp.concatenate([gain_rows, bias_row])
    small = jnp.pad(small, ((0, STRAY_TILE - small.shape[0]), (0, 0))).astype(BF16)
    tall = UROWS + STRAY_TILE

    halves = {}

    def near_sums(own_units, rz):
        first = 4 * rz * own
        for group, span in enumerate(spans):
            size = span[1] - span[0]
            axis = (ALONG_X, ALONG_Y)[(group + rz) % 2]
            shape = (2, size, UROWS, width)
            kept = own_units[first : first + 2 * size].reshape(shape)
            given = own_units[first + 2 * size : first + 4 * size].reshape(shape)
            halves[rz, group] = axis, kept, links.send(given, axis)
            first += 4 * size
        return given

    def far_sums(rz):
        sums = []
        for group in range(len(spans)):
            axis, kept, got = halves[rz, group]
            onward = (kept[1].astype(F32) + got[1].astype(F32)).astype(BF16)
            passed = links.send(onward, ALONG_X + ALONG_Y - axis)
            sums.append(kept[0].astype(F32) + got[0].astype(F32) + passed.astype(F32))
        return jnp.concatenate(sums).reshape(own * UROWS, width)

    own_units = after(after(own_units, links.sent[ALONG_X][-1]), links.sent[ALONG_Y][-1])
    strays.step()
    top = line - 1
    later_units = after(own_units, near_sums(own_units, top))
    rides = [jnp.concatenate([strays.finish(), small])]
    moving = None
    for rz in range(top, -1, -1):
        if rz:
            near_sums(later_units, rz - 1)
        value = far_sums(rz)
        if moving is not None:
            got = links.send(jnp.concatenate([moving.astype(BF16), rides[-1]]), ALONG_Z)
            rides.append(got[own * UROWS :])
            value = value + got[: own * UROWS].astype(F32)
        moving = value
    own_grads = moving.reshape(own, UROWS, width)

    terms = [ride[tall:].astype(F32) for ride in rides]
    while len(terms) > 1:
        middle = len(terms) // 2
        terms = [terms[i] + terms[middle + i] for i in range(middle)]
    low_rides = jnp.concatenate([ride[:tall] for ride in rides[0::2]] + [terms[0].astype(BF16)])
    high_rides = jnp.concatenate([ride[:tall] for ride in rides[1::2]])
    rows = line // 2 * tall
    low_got, high_got = links.send(low_rides, ALONG_X), links.send(high_rides, ALONG_Y)
    small_sum = (low_rides[rows:].astype(F32) + low_got[rows:].astype(F32)).astype(BF16)
    low_rides = jnp.concatenate([low_rides[:rows], low_got[:rows], small_sum])
    high_rides = jnp.concatenate([high_rides, high_got])
    low_got, high_got = links.send(low_rides, ALONG_Y), links.send(high_rides, ALONG_X)
    small_total = small_sum.astype(F32) + low_got[2 * rows :].astype(F32)
    stray_found = [low_rides[: 2 * rows], low_got[: 2 * rows], high_rides, high_got]

    def extra_grads():
        return lax.psum(own_units[4 * line * own :].astype(F32), "dp").astype(BF16)

    extra_grad = lax.cond(many, extra_grads, no_extra)

    stray_found = jnp.concatenate([part.reshape(-1, UROWS + STRAY_TILE, width) for part in stray_found])
    shift = jnp.bitwise_xor(my_stray, me)
    stray_rz = (ring_place(me // 4, line) - ring_place(my_stray // 4, line) + line) % line
    stray_x, stray_y = jnp.bitwise_and(shift, 1), jnp.bitwise_and(shift // 2, 1)
    is_even = stray_rz % 2 == 0
    far_bit, near_bit = jnp.where(is_even, stray_y, stray_x), jnp.where(is_even, stray_x, stray_y)
    stray_place = (((stray_rz % 2) * 2 + far_bit) * 2 + near_bit) * (line // 2) + stray_rz // 2
    own_ids = jnp.arange(own, dtype=jnp.int32)
    picks = jnp.concatenate(
        [
            jnp.where(own_ids < my_count, 3, 0),
            jnp.where(my_stray >= 0, 1, jnp.where(my_extra >= 0, 2, 0)),
            jnp.zeros_like(own_ids),
            jnp.where(my_stray >= 0, stray_place, 0),
            jnp.zeros_like(own_ids),
            jnp.maximum(my_extra, 0),
        ]
    ).astype(jnp.int32)

    slot_spec = pl.BlockSpec((1, UROWS, width), lambda i, pick: (i, 0, 0))
    stack_shape = unit_weight.shape
    unit_weights, unit_firsts, unit_seconds, unit_copies = pl.pallas_call(
        update_kernel,
        grid_spec=pltpu.PrefetchScalarGridSpec(
            num_scalar_prefetch=1,
            grid=(most,),
            in_specs=[slot_spec] * 3
            + [
                pl.BlockSpec((1, UROWS, width), lambda i, pick: (jnp.minimum(i, own - 1), 0, 0)),
                pl.BlockSpec((1, UROWS, width), lambda i, pick: (pick[most + i], 0, 0)),
                pl.BlockSpec((1, UROWS, width), lambda i, pick: (pick[2 * most + i], 0, 0)),
            ],
            out_specs=[slot_spec] * 4,
        ),
        out_shape=[like(stack_shape)] * 3 + [like(stack_shape, BF16)],
        compiler_params=params(32),
        cost_estimate=timed(8),
    )(picks, unit_weight, unit_first, unit_second, own_grads, stray_found, extra_grad)

    proj_total = pl.pallas_call(
        functools.partial(order_rows_kernel, devices),
        out_shape=like((devices, STRAY_TILE, width)),
        in_specs=[SMEM, VMEM],
        compiler_params=params(32),
        cost_estimate=timed(1),
    )(where, stray_found[:, UROWS:])
    proj_total = proj_total[:, :share].reshape(devices * share, width)[: proj_width * D // width]
    proj_total = proj_total.reshape(2, proj_width, D // 2).transpose(0, 2, 1).reshape(D, proj_width)
    gain_total = small_total[: gain_rows.shape[0]].reshape(3, D)
    bias_total = small_total[gain_rows.shape[0], : BUCKETS * heads].reshape(BUCKETS, heads)
    gain_weights, gain_firsts, gain_seconds = adamw_step(
        gain_weight, gain_first, gain_second, gain_total, RATE_GAIN
    )
    bias_weights, bias_firsts, bias_seconds = adamw_step(
        bias_weight, bias_first, bias_second, bias_total, RATE_SMALL
    )
    proj_weights, proj_firsts, proj_seconds = adamw_step(
        proj_weight, proj_first, proj_second, proj_total, RATE_MATRIX
    )
    return (
        encoded,
        token_grad,
        unit_weights,
        unit_firsts,
        unit_seconds,
        unit_copies,
        gain_weights,
        gain_firsts,
        gain_seconds,
        bias_weights,
        bias_firsts,
        bias_seconds,
        proj_weights,
        proj_firsts,
        proj_seconds,
    )


def solution(mesh):
    in_specs = (
        P("dp", None),
        P("dp", "mp"),
        P("dp"),
        P(),
        P(),
        P("dp", None, "mp"),
        P("dp", None, "mp"),
        P("dp", None, "mp"),
        P(),
        P(),
        P(),
        P(None, "mp"),
        P(None, "mp"),
        P(None, "mp"),
        P(None, "mp"),
        P(None, "mp"),
        P(None, "mp"),
    )
    out_specs = (
        P("dp", "mp"),
        P("dp", None),
        P("dp", None, "mp"),
        P("dp", None, "mp"),
        P("dp", None, "mp"),
        P("dp", None, "mp"),
        P(),
        P(),
        P(),
        P(None, "mp"),
        P(None, "mp"),
        P(None, "mp"),
        P(None, "mp"),
        P(None, "mp"),
        P(None, "mp"),
    )
    return jax.shard_map(shards, mesh=mesh, in_specs=in_specs, out_specs=out_specs, check_vma=False)
```
